32 devices in a mesh: dp: 4 (over x, core), wide: 8 (over z, y).
Axes of the slice: x: 2, y: 2, z: 4, core: 2. Of those that a mesh axis runs over, the one named last changes fastest.
Arguments:
- x_in: float32 [4096, 2048], P(('dp', 'wide')), may hold values from -6 to 6
- lengths: int32 [4, 4], P('dp'), may hold values from 1 to 1021, as said below
- modality: int32 [4096], P(('dp', 'wide')), may hold values from 0 to 2, as said below
- norm_gain: float32 [2048], replicated, may hold values from 0.5 to 1.5
- conv_weight: float32 [4, 4096], replicated, may hold values from -3 to 3
- conv_bias: float32 [4096], replicated, may hold values from -3 to 3
- a_log: float32 [16, 4096], replicated, may hold values from -4.6 to 1
- d_skip: float32 [4096], replicated, may hold values from 0.5 to 1.5
- in_master: float32 [2048, 3, 8192], P('dp', None, 'wide'), may hold values from -0.125 to 0.125
- xproj_master: float32 [160, 3, 4096], P('dp', None, 'wide'), may hold values from -0.09375 to 0.09375
- dtproj_master: float32 [128, 3, 4096], P('dp', None, 'wide'), may hold values from -0.5 to 0.5
- dt_bias: float32 [3, 4096], P(None, 'wide'), may hold values from -7 to -2
- out_master: float32 [2048, 3, 4096], P('dp', None, 'wide'), may hold values from -0.375 to 0.375
- cotangent: float32 [4096, 2048], P(('dp', 'wide')), may hold values from -6 to 6
Outputs:
- out: float32 [4096, 2048], P(('dp', 'wide'))
- x_grad: float32 [4096, 2048], P(('dp', 'wide'))
- norm_gain_grad: float32 [2048], replicated
- conv_weight_grad: float32 [4, 4096], replicated
- conv_bias_grad: float32 [4096], replicated
- a_log_grad: float32 [16, 4096], replicated
- d_skip_grad: float32 [4096], replicated
- in_grad: float32 [2048, 3, 8192], P('dp', None, 'wide')
- xproj_grad: float32 [160, 3, 4096], P('dp', None, 'wide')
- dtproj_grad: float32 [128, 3, 4096], P('dp', None, 'wide')
- dt_bias_grad: float32 [3, 4096], P(None, 'wide')
- out_grad: float32 [2048, 3, 4096], P('dp', None, 'wide')
The draws below stay inside these ranges and needn't reach their ends.
Inputs may be any that keep to these rules, and one draw needn't show every extreme that they name: Row r gives, in order, the lengths of the 4 sequences that fill group r of 1024 positions from its start; fewer than 17 positions at the group's end are padding. In each row one sequence, at a slot drawn from the seed, starts within the first 128 positions and ends within the last 128; each other sequence has at most 32 positions. In each block of 128 positions that one device holds, at most 64 live positions have modality 1 and at most 64 have modality 2; padding positions have modality 0. In every draw, for one index along dp, every device along wide has exactly 64 live positions of modality 1.
All inputs are finite; a program needn't handle non-finite values.
Results may differ from the reference program's by a relative error of at most 0.012.
The reference program's roundings to bfloat16 on the way count: a program that leaves them out, or rounds other values in their place, can miss the bound.
Values may be sent and summed in bfloat16 or wider, within the bound.
A program may use at most 384 MiB of HBM per device.

```python
import jax
import jax.numpy as jnp
from jax import lax

D = 2048
INNER = 4096
STATE = 16
CONV_WIDTH = 4
DT_RANK = 128
TOK_DEV = 128
SEQS = 4
XW = 160
TOKENS = 4096
N_DP = 4
N_WIDE = 8
DEVICES = 32


def draw_plan(key):
    keys = jax.random.split(key, 8)
    groups = N_DP
    span = TOK_DEV * N_WIDE
    places = jnp.arange(TOK_DEV, dtype=jnp.int32)
    half = TOK_DEV // 2
    least = TOK_DEV // 8
    long_slot = jax.random.randint(keys[0], (groups,), 0, SEQS)
    shorts = jax.random.randint(keys[1], (groups, SEQS), 1, TOK_DEV // 4 + 1)
    padding = jax.random.randint(keys[2], (groups,), 0, least + 1)
    tight = jax.random.randint(keys[3], (), 0, groups)
    is_tight = jnp.arange(groups) == tight
    shorts = jnp.where(is_tight[:, None], 1, shorts)
    padding = jnp.where(is_tight, 0, padding)
    is_long = jnp.arange(SEQS)[None, :] == long_slot[:, None]
    short_total = jnp.sum(jnp.where(is_long, 0, shorts), axis=1)
    lengths = jnp.where(is_long, (span - short_total - padding)[:, None], shorts).astype(jnp.int32)
    rows = DEVICES
    row_index = jnp.arange(rows)
    group_live = span - padding
    living = jnp.clip(group_live[row_index // N_WIDE] - row_index % N_WIDE * TOK_DEV, 0, TOK_DEV)
    ones_count = jax.random.randint(keys[4], (rows,), least, half + 1)
    full_group = jax.random.randint(keys[5], (), 0, groups)
    ones_count = jnp.where(row_index // N_WIDE == full_group, half, ones_count)
    remain = jnp.minimum(living - ones_count, half)
    twos_count = jax.random.randint(keys[6], (rows,), jnp.minimum(least, remain), remain + 1)
    scores = jax.random.randint(keys[7], (rows, TOK_DEV), 0, 1 << 19) * TOK_DEV + places[None, :]
    scores = jnp.where(places[None, :] < living[:, None], scores, (1 << 30) + places[None, :])
    ordering = jnp.argsort(scores, axis=1)
    ranking = jnp.argsort(ordering, axis=1)
    kinds = jnp.where(ranking < ones_count[:, None], 1, jnp.where(ranking < (ones_count + twos_count)[:, None], 2, 0))
    return (lengths, kinds.reshape(-1).astype(jnp.int32))


def draw_lengths(key, part):
    return draw_plan(key)[0]


def draw_modality(key, part):
    return draw_plan(key)[1]


def block_scale(key, dims, cuts, low, high):
    def one(axis_at, shards_of):
        steps = jax.random.uniform(jax.random.fold_in(jax.random.fold_in(key, 6), axis_at), (shards_of,), jnp.float32, low / len(cuts), high / len(cuts))
        return jnp.repeat(jnp.exp(steps), dims[axis_at] // shards_of).reshape((-1,) + (1,) * (len(dims) - axis_at - 1))

    level = one(*cuts[0])
    for cut in cuts[1:]:
        level = level * one(*cut)
    return level


def centred(stream_key, shape, width, bound, cuts=(), held_as=jnp.bfloat16):
    level = block_scale(stream_key, shape, cuts, -0.22, 0.18) if cuts else 1.0
    entries = jax.random.normal(stream_key, shape, jnp.float32) * width * level
    return jnp.minimum(jnp.maximum(entries, -bound), bound).astype(held_as)


def setup_inputs(seed: int = 0) -> dict:
    arg_keys = jax.random.split(jax.random.key(seed), 15)
    x_in = centred(arg_keys[0], (TOKENS, D), 1.0, 6.0, ((0, 32),), jnp.float32)
    lengths = draw_lengths(jax.random.fold_in(arg_keys[14], 71), 0)
    modality = draw_modality(jax.random.fold_in(arg_keys[14], 71), 0)
    norm_gain = jnp.clip(1.0 + 0.1 * jax.random.normal(arg_keys[3], (D,), jnp.float32), 0.5, 1.5)
    conv_weight = centred(arg_keys[4], (CONV_WIDTH, INNER), CONV_WIDTH ** -0.5, 3.0, (), jnp.float32)
    conv_bias = centred(arg_keys[5], (INNER,), 0.5, 3.0, (), jnp.float32)
    a_log = jnp.clip(jax.random.uniform(arg_keys[6], (STATE, INNER), jnp.float32, -4.6, 1.0), -4.6, 1.0)
    d_skip = jnp.clip(jax.random.uniform(arg_keys[7], (INNER,), jnp.float32, 0.5, 1.5), 0.5, 1.5)
    in_master = centred(arg_keys[8], (D, 3, 2 * INNER), D ** -0.5, 0.125, ((0, 4), (2, 8)), jnp.float32)
    xproj_master = centred(arg_keys[9], (XW, 3, INNER), INNER ** -0.5, 0.09375, ((0, 4), (2, 8)), jnp.float32)
    dtproj_master = centred(arg_keys[10], (DT_RANK, 3, INNER), DT_RANK ** -0.5, 0.5, ((0, 4), (2, 8)), jnp.float32)
    dt_bias = jnp.clip(-7.0 + 5.0 * jax.random.uniform(arg_keys[11], (3, INNER), jnp.float32) ** block_scale(arg_keys[11], (3, INNER), ((1, 8),), -0.2, 0.2), -7.0, -2.0)
    out_master = centred(arg_keys[12], (D, 3, INNER), (INNER // 16) ** -0.5, 0.375, ((0, 4), (2, 8)), jnp.float32)
    cotangent = centred(arg_keys[13], (TOKENS, D), 1.0, 6.0, ((0, 32),), jnp.float32)
    return dict(x_in=x_in, lengths=lengths, modality=modality, norm_gain=norm_gain, conv_weight=conv_weight, conv_bias=conv_bias, a_log=a_log, d_skip=d_skip, in_master=in_master, xproj_master=xproj_master, dtproj_master=dtproj_master, dt_bias=dt_bias, out_master=out_master, cotangent=cotangent)


@jax.custom_vjp
def low(v):
    return lax.optimization_barrier(v.astype(jnp.bfloat16)).astype(jnp.float32)

@jax.custom_vjp
def low_back(v):
    return v

def low_keep(v):
    return (low(v), None)

def low_pass(kept, grad):
    return (grad,)

def back_keep(v):
    return (v, None)

def back_low(kept, grad):
    return (low(grad),)
low.defvjp(low_keep, low_pass)
low_back.defvjp(back_keep, back_low)
EPSILON = 1e-05

def product(left, right):
    return jnp.dot(left, right, precision=lax.Precision.HIGHEST)

def product_across(left, right):
    return lax.dot_general(left, right, (((1,), (1,)), ((), ())), precision=lax.Precision.HIGHEST)

def shifted(values, offset):
    if offset == 0:
        return values
    filler = jnp.zeros((offset,) + values.shape[1:], values.dtype)
    return jnp.concatenate([filler, values[:-offset]], axis=0)

def select(picks, make):
    total = picks[0] * make(0)
    total = total + picks[1] * make(1)
    return total + picks[2] * make(2)

def selective_scan(delta, inputs, b_rows, c_rows, keep, a_neg):

    def advance(state, pieces):
        step_size, value, b_row, c_row, kept = pieces
        state = jnp.exp(step_size[None, :] * a_neg) * kept * state + b_row[:, None] * (step_size * value)[None, :]
        return (state, lax.optimization_barrier(jnp.sum(c_row[:, None] * state, axis=0)))
    start = jnp.zeros(a_neg.shape, delta.dtype)
    _, outputs = lax.scan(advance, start, (delta, inputs, b_rows, c_rows, keep))
    return outputs

def group_block(tokens, lengths, modality, weights):
    gain, conv_weight, conv_bias, a_log, d_skip, w_in, w_x, w_dt, b_dt, w_out = weights
    count = tokens.shape[0]
    places = jnp.arange(count, dtype=jnp.int32)
    bounds = jnp.cumsum(lengths).astype(jnp.int32)
    segment = lax.optimization_barrier(jnp.sum((places[:, None] >= bounds[None, :]).astype(jnp.int32), axis=1)).astype(jnp.int32)
    live = (places < bounds[-1]).astype(tokens.dtype)[:, None]
    picks = [(modality == kind).astype(tokens.dtype)[:, None] for kind in range(3)]
    masks = [((places >= offset) & (shifted(segment, offset) == segment)).astype(tokens.dtype)[:, None] for offset in range(CONV_WIDTH)]
    scale = lax.rsqrt(lax.optimization_barrier(jnp.mean(tokens * tokens, axis=1, keepdims=True)) + EPSILON)
    normed = low_back(low(tokens * scale * gain[None, :]))
    mixed = live * low_back(low(select(picks, lambda kind: product(normed, w_in[:, kind, :]))))
    xs_part = mixed[:, :INNER]
    z_part = mixed[:, INNER:]
    pre = conv_bias[None, :]
    for offset in range(CONV_WIDTH):
        pre = pre + conv_weight[CONV_WIDTH - 1 - offset][None, :] * shifted(xs_part, offset) * masks[offset]
    inner = low(jax.nn.silu(pre))
    inner_send = low_back(inner)
    proj = low_back(select(picks, lambda kind: product_across(inner_send, w_x[:, kind, :])))
    rates = low(proj[:, :DT_RANK])
    maps = live * low_back(low(proj[:, DT_RANK:]))
    steps = live * low_back(low(select(picks, lambda kind: product(rates, w_dt[:, kind, :]) + b_dt[kind][None, :])))
    delta = jax.nn.softplus(steps)
    a_neg = -jnp.exp(a_log)
    scanned = selective_scan(delta, inner, maps[:, :STATE], maps[:, STATE:], masks[1][:, 0], a_neg)
    y_value = scanned + d_skip[None, :] * inner
    gated = low_back(low(y_value * jax.nn.silu(z_part)))
    branch = live * low_back(low(select(picks, lambda kind: product_across(gated, w_out[:, kind, :]))))
    return tokens + branch

def reference(x_in, lengths, modality, norm_gain, conv_weight, conv_bias, a_log, d_skip, in_master, xproj_master, dtproj_master, dt_bias, out_master, cotangent):
    groups = lengths.shape[0]
    span = x_in.shape[0] // groups
    token_kinds = modality.reshape(groups, span)

    def forward(tokens, gain, conv_w, conv_b, decay_log, skip, w_in, w_x, w_dt, b_dt, w_out):
        weights = (gain, conv_w, conv_b, decay_log, skip, low(w_in), low(w_x), low(w_dt), low(b_dt), low(w_out))

        def one_group(pieces):
            return group_block(pieces[0], pieces[1], pieces[2], weights)
        outputs = lax.map(jax.checkpoint(one_group), (tokens.reshape(groups, span, D), lengths, token_kinds))
        return outputs.reshape(groups * span, D)
    result, pull = jax.vjp(forward, x_in, norm_gain, conv_weight, conv_bias, a_log, d_skip, in_master, xproj_master, dtproj_master, dt_bias, out_master)
    grads = pull(cotangent)
    return (result, grads[0], grads[1], grads[2], grads[3], grads[4], grads[5], grads[6], grads[7], grads[8], grads[9], grads[10])
```

```python
import jax
import jax.numpy as jnp
from jax import lax
from jax.experimental import pallas as pl
from jax.experimental.pallas import tpu as pltpu
from jax.sharding import PartitionSpec as P

F32 = jnp.float32
BF = jnp.bfloat16
INNER = 4096
STATE = 16
DT_RANK = 128
EPSILON = 1e-05


STEPS=16
HUGE=1e30

def scan_forward_kernel(dtp_ref,u_ref,b_ref,c_ref,keep_ref,alog_ref,skip_ref,z_ref, gated_ref,y_ref,heads_ref, st, dec, inj, ys, a2):
    T,C=u_ref.shape
    @pl.when(pl.program_id(0)==0)
    def _():
        st[...]=jnp.zeros_like(st)
        a2[...]=-jnp.exp(alog_ref[...])*1.4426950408889634
    delta=jax.nn.softplus(dtp_ref[...].astype(F32))
    u=u_ref[...].astype(F32)
    dec[...]=jnp.where(keep_ref[...]>0,delta,HUGE)
    inj[...]=delta*u
    def chunk(k,state):
        heads_ref[k]=state
        b=b_ref[k]; c=c_ref[k]
        an=a2[...]
        base=pl.multiple_of(k*STEPS,STEPS)
        for j in range(STEPS):
            d=dec[pl.ds(base+j,1),:]
            v=inj[pl.ds(base+j,1),:]
            state=jnp.exp2(d*an)*state+b[:,j:j+1]*v
            ys[pl.ds(base+j,1),:]=jnp.sum(c[:,j:j+1]*state,axis=0,keepdims=True)
        return state
    st[...]=lax.fori_loop(0,T//STEPS,chunk,st[...])
    y=ys[...]+skip_ref[...]*u
    y_ref[...]=y
    z=z_ref[...].astype(F32)
    gated_ref[...]=(y*(z*jax.nn.sigmoid(z))).astype(BF)

def scan_forward(dtp,u,b,c,keep,alog,skip,z,T=128):
    N,C=u.shape
    S=alog.shape[0]
    nk=N//STEPS; tk=T//STEPS
    row=pl.BlockSpec((T,C),lambda i:(i,0))
    col=pl.BlockSpec((tk,S,STEPS),lambda i:(i,0,0))
    whole=lambda s: pl.BlockSpec(s,lambda i:(0,0))
    return pl.pallas_call(scan_forward_kernel,grid=(N//T,),
      in_specs=[row,row,col,col,pl.BlockSpec((T,1),lambda i:(i,0)),whole((S,C)),whole((1,C)),row],
      out_specs=[row,row,pl.BlockSpec((tk,S,C),lambda i:(i,0,0))],
      out_shape=[jax.ShapeDtypeStruct((N,C),BF),jax.ShapeDtypeStruct((N,C),F32),jax.ShapeDtypeStruct((nk,S,C),F32)],
      scratch_shapes=[pltpu.VMEM((S,C),F32),pltpu.VMEM((T,C),F32),pltpu.VMEM((T,C),F32),pltpu.VMEM((T,C),F32),pltpu.VMEM((S,C),F32)],
      compiler_params=pltpu.CompilerParams(vmem_limit_bytes=48<<20),
      name="scan_forward")(dtp,u,b,c,keep,alog,skip,z)

def scan_backward_kernel(dtp_ref,u_ref,b_ref,c_ref,keep_ref,alog_ref,skip_ref,z_ref,y_ref,dg_ref,heads_ref,
        ddtp_ref,dus_ref,dz_ref,dm_ref,dalog_ref,dskip_ref, run, dec, inj, dly, dys, sq, wa, sts, dcs, an2, an1, acc):
    T,C=u_ref.shape
    S=alog_ref.shape[0]
    first=pl.program_id(0)==0
    last=pl.program_id(0)==pl.num_programs(0)-1
    @pl.when(first)
    def _():
        run[...]=jnp.zeros_like(run)
        acc[...]=jnp.zeros_like(acc)
        dskip_ref[...]=jnp.zeros_like(dskip_ref)
        an1[...]=-jnp.exp(alog_ref[...])
        an2[...]=an1[...]*1.4426950408889634
    dtp=dtp_ref[...].astype(F32)
    delta=jax.nn.softplus(dtp)
    u=u_ref[...].astype(F32)
    dec[...]=jnp.where(keep_ref[...]>0,delta,HUGE)
    dly[...]=delta
    inj[...]=delta*u
    z=z_ref[...].astype(F32)
    sg=jax.nn.sigmoid(z)
    dg=dg_ref[...].astype(F32)
    dy=dg*(z*sg)
    dys[...]=dy
    dz_ref[...]=(dg*y_ref[...]*(sg*(1.0+z*(1.0-sg)))).astype(BF)
    dskip_ref[...]+=jnp.sum(dy*u,axis=0,keepdims=True)
    def chunk(i,running):
        k=T//STEPS-1-i
        b=b_ref[k]; c=c_ref[k]
        base=pl.multiple_of(k*STEPS,STEPS)
        state=heads_ref[k]
        an=an2[...]
        for j in range(STEPS):
            d=dec[pl.ds(base+j,1),:]
            v=inj[pl.ds(base+j,1),:]
            dc=jnp.exp2(d*an)
            sd=dc*state
            state=sd+b[:,j:j+1]*v
            dcs[j]=dc
            sts[j]=sd
        lane=lax.broadcasted_iota(jnp.int32,(S,STEPS),1)
        db=jnp.zeros((S,STEPS),F32); dcc=jnp.zeros((S,STEPS),F32)
        for j in range(STEPS-1,-1,-1):
            g=dys[pl.ds(base+j,1),:]
            v=inj[pl.ds(base+j,1),:]
            bj=b[:,j:j+1]
            ds=c[:,j:j+1]*g+running
            sd=sts[j]
            w=ds*sd
            sq[pl.ds(base+j,1),:]=jnp.sum(ds*bj,axis=0,keepdims=True)
            wa[pl.ds(base+j,1),:]=jnp.sum(w*an1[...],axis=0,keepdims=True)
            acc[...]+=w*dly[pl.ds(base+j,1),:]
            db=jnp.where(lane==j,jnp.sum(ds*v,axis=1,keepdims=True),db)
            dcc=jnp.where(lane==j,jnp.sum(g*(sd+bj*v),axis=1,keepdims=True),dcc)
            running=dcs[j]*ds
        dm_ref[k,:S]=db
        dm_ref[k,S:]=dcc
        return running
    run[...]=lax.fori_loop(0,T//STEPS,chunk,run[...])
    dd=wa[...]+u*sq[...]
    ddtp_ref[...]=(dd*jax.nn.sigmoid(dtp)).astype(BF)
    dus_ref[...]=delta*sq[...]+dy*skip_ref[...]
    @pl.when(last)
    def _():
        dalog_ref[...]=acc[...]*an1[...]

def scan_backward(dtp,u,b,c,keep,alog,skip,z,y,dg,heads,T=128):
    N,C=u.shape
    S=alog.shape[0]
    nk=N//STEPS; tk=T//STEPS; nb=N//T
    row=pl.BlockSpec((T,C),lambda i:(nb-1-i,0))
    col=pl.BlockSpec((tk,S,STEPS),lambda i:(nb-1-i,0,0))
    whole=lambda s: pl.BlockSpec(s,lambda i:(0,0))
    sc=lambda *s: pltpu.VMEM(s,F32)
    return pl.pallas_call(scan_backward_kernel,grid=(nb,),
      in_specs=[row,row,col,col,pl.BlockSpec((T,1),lambda i:(nb-1-i,0)),whole((S,C)),whole((1,C)),row,row,row,pl.BlockSpec((tk,S,C),lambda i:(nb-1-i,0,0))],
      out_specs=[row,row,row,pl.BlockSpec((tk,2*S,STEPS),lambda i:(nb-1-i,0,0)),whole((S,C)),whole((1,C))],
      out_shape=[jax.ShapeDtypeStruct((N,C),BF),jax.ShapeDtypeStruct((N,C),F32),jax.ShapeDtypeStruct((N,C),BF),jax.ShapeDtypeStruct((nk,2*S,STEPS),F32),jax.ShapeDtypeStruct((S,C),F32),jax.ShapeDtypeStruct((1,C),F32)],
      scratch_shapes=[sc(S,C),sc(T,C),sc(T,C),sc(T,C),sc(T,C),sc(T,C),sc(T,C),sc(STEPS,S,C),sc(STEPS,S,C),sc(S,C),sc(S,C),sc(S,C)],
      compiler_params=pltpu.CompilerParams(vmem_limit_bytes=48<<20),
      name="scan_backward")(dtp,u,b,c,keep,alog,skip,z,y,dg,heads)


def contract(left, right, left_dim, right_dim):
    return lax.dot_general(
        left, right, (((left_dim,), (right_dim,)), ((), ())), preferred_element_type=F32
    )


def segment_of(places, bounds):
    return jnp.sum((places[:, None] >= bounds[None, :]).astype(jnp.int32), axis=1)


def conv_masks(places, bounds, width):
    segment = segment_of(places, bounds)
    return [
        ((places >= offset) & (segment_of(places - offset, bounds) == segment)).astype(F32)
        for offset in range(width)
    ]


def silu_slope(values):
    sigma = jax.nn.sigmoid(values)
    return sigma * (1.0 + values * (1.0 - sigma))


def split_kinds(rows, kinds, parts):
    count, depth = rows.shape
    pieces = rows.reshape(count, parts, 1, depth // parts)
    picked = kinds[:, None, :, None]
    return jnp.where(picked, pieces, jnp.zeros((), rows.dtype)).reshape(count, 3 * depth)


def gather_master(master):
    rows = lax.all_gather(jnp.transpose(master.astype(BF), (1, 0, 2)), "dp", axis=0)
    return rows.reshape(-1, master.shape[2])


def scatter_master(grad, rows):
    parts = lax.axis_size("dp")
    kept = lax.psum_scatter(
        grad.reshape(parts, 3, rows, grad.shape[1]), "dp", scatter_dimension=0, tiled=False
    )
    return jnp.transpose(kept, (1, 0, 2))


def halves_out(block, wide):
    half = wide // 2
    columns = block.shape[1] // 2
    low = lax.axis_index("wide") < half
    first, second = block[:, :columns], block[:, columns:]
    even = [(v, 2 * v) if v < half else (v, 2 * (v - half) + 1) for v in range(wide)]
    odd = [(v, 2 * v + 1) if v < half else (v, 2 * (v - half)) for v in range(wide)]
    got_a = lax.ppermute(jnp.where(low, first, second), "wide", even)
    got_b = lax.ppermute(jnp.where(low, second, first), "wide", odd)
    is_even = lax.axis_index("wide") % 2 == 0
    return jnp.where(is_even, got_a, got_b), jnp.where(is_even, got_b, got_a)


def halves_back(xs, z, wide):
    half = wide // 2
    low = lax.axis_index("wide") < half
    even = [(2 * v, v) if v < half else (2 * (v - half) + 1, v) for v in range(wide)]
    odd = [(2 * v + 1, v) if v < half else (2 * (v - half), v) for v in range(wide)]
    is_even = lax.axis_index("wide") % 2 == 0
    got_a = lax.ppermute(jnp.where(is_even, xs, z), "wide", even)
    got_b = lax.ppermute(jnp.where(is_even, z, xs), "wide", odd)
    return jnp.concatenate([jnp.where(low, got_a, got_b), jnp.where(low, got_b, got_a)], axis=1)


def body(
    x_in,
    lengths,
    modality,
    norm_gain,
    conv_weight,
    conv_bias,
    a_log,
    d_skip,
    in_master,
    xproj_master,
    dtproj_master,
    dt_bias,
    out_master,
    cotangent,
):
    wide, dp = lax.axis_size("wide"), lax.axis_size("dp")
    place = lax.axis_index("wide")
    count = x_in.shape[0]
    span = count * wide
    channels = INNER // wide
    width = conv_weight.shape[0]
    own = lambda table: lax.dynamic_slice_in_dim(table, place * channels, channels, table.ndim - 1)

    bounds = jnp.cumsum(lengths.reshape(-1))
    places = jnp.arange(span, dtype=jnp.int32)
    living = places < bounds[-1]
    masks = conv_masks(places, bounds, width)
    later = conv_masks(jnp.arange(span + width - 1, dtype=jnp.int32), bounds, width)
    alive_here = (place * count + jnp.arange(count, dtype=jnp.int32)) < bounds[-1]

    scale = lax.rsqrt(jnp.mean(x_in * x_in, axis=1, keepdims=True) + EPSILON)
    normed = (x_in * scale * norm_gain[None, :]).astype(BF)
    d_branch = jnp.where(alive_here[:, None], cotangent, 0.0).astype(BF)
    w_in = gather_master(in_master)
    normed_all = lax.all_gather(normed, "wide", axis=0, tiled=True)
    kinds_all = lax.all_gather(modality, "wide", axis=0, tiled=True)
    w_x = gather_master(xproj_master)
    w_dt = gather_master(dtproj_master)
    w_out = gather_master(out_master)
    d_branch_all = lax.all_gather(d_branch, "wide", axis=0, tiled=True)
    kinds = (kinds_all[:, None] == jnp.arange(3, dtype=jnp.int32)[None, :]) & living[:, None]

    normed_kinds = split_kinds(normed_all, kinds, dp)
    mixed = contract(normed_kinds, w_in, 1, 0).astype(BF)
    xs, z = halves_out(mixed, wide)

    taps = own(conv_weight)
    xs_value = xs.astype(F32)
    extended = jnp.concatenate([jnp.zeros((width - 1, channels), F32), xs_value], axis=0)
    pre = own(conv_bias)[None, :]
    for offset in range(width):
        begin = width - 1 - offset
        pre = (
            pre + taps[begin][None, :] * extended[begin : begin + span] * masks[offset][:, None]
        )
    inner = jax.nn.silu(pre).astype(BF)

    rank = xproj_master.shape[0] * dp
    w_x_kinds = w_x.reshape(dp, 3, rank // dp, channels).transpose(1, 0, 2, 3).reshape(3, rank, channels)
    by_kind = contract(inner, w_x_kinds.reshape(3 * rank, channels), 1, 1).reshape(span, 3, rank)
    proj = lax.psum(jnp.sum(jnp.where(kinds[:, :, None], by_kind, 0.0), axis=1), "wide")
    rates = proj[:, :DT_RANK].astype(BF)
    maps = proj[:, DT_RANK:].astype(BF).astype(F32)
    rates_kinds = split_kinds(rates, kinds, dp)
    bias = jnp.where(kinds[:, :, None], dt_bias.astype(BF).astype(F32)[None], 0.0).sum(axis=1)
    dtp = (contract(rates_kinds, w_dt, 1, 0) + bias).astype(BF)

    blocks = span // STEPS
    to_columns = lambda rows: rows.reshape(blocks, STEPS, -1).transpose(0, 2, 1)
    b_columns = to_columns(maps[:, :STATE])
    c_columns = to_columns(maps[:, STATE:])
    keep = masks[1][:, None]
    a_own = own(a_log)
    skip_own = own(d_skip)[None, :]
    gated, y_value, heads = scan_forward(dtp, inner, b_columns, c_columns, keep, a_own, skip_own, z)

    d_branch_kinds = split_kinds(d_branch_all, kinds, dp)
    d_gated = contract(d_branch_kinds, w_out, 1, 0).astype(BF)
    w_out_kinds = w_out.reshape(dp, 3, -1, channels)
    branch = jnp.zeros((span, x_in.shape[1]), F32)
    for kind in range(3):
        picked = jnp.where(kinds[:, kind : kind + 1], gated, jnp.zeros((), BF))
        branch = branch + contract(picked, w_out_kinds[:, kind].reshape(-1, channels), 1, 1)
    branch = lax.psum_scatter(branch.astype(BF), "wide", scatter_dimension=0, tiled=True)
    result = x_in + branch.astype(F32)
    grad_out = contract(d_branch_kinds, gated, 0, 0)
    out_grad = scatter_master(grad_out.astype(BF), out_master.shape[0]).astype(F32)

    d_dtp, d_scan, d_z, d_columns, alog_part, skip_part = scan_backward(
        dtp, inner, b_columns, c_columns, keep, a_own, skip_own, z, y_value, d_gated, heads
    )
    d_dtp = jnp.where(living[:, None], d_dtp, jnp.zeros((), BF))
    d_maps = d_columns.transpose(0, 2, 1).reshape(span, 2 * STATE)
    d_rates = jnp.zeros((span, DT_RANK), F32)
    w_dt_kinds = w_dt.reshape(dp, 3, -1, channels)
    d_dtp_kinds = split_kinds(d_dtp, kinds, 1)
    for kind in range(3):
        picked = jnp.where(kinds[:, kind : kind + 1], d_dtp, jnp.zeros((), BF))
        d_rates = d_rates + contract(picked, w_dt_kinds[:, kind].reshape(-1, channels), 1, 1)
    d_proj = lax.psum(jnp.concatenate([d_rates, d_maps], axis=1), "wide")
    d_proj = jnp.where(living[:, None], d_proj, 0.0).astype(BF)
    grad_dt = contract(rates_kinds, d_dtp, 0, 0)
    bias_part = jnp.stack(
        [jnp.sum(jnp.where(kinds[:, k : k + 1], d_dtp.astype(F32), 0.0), axis=0) for k in range(3)]
    )
    d_proj_kinds = split_kinds(d_proj, kinds, 1)
    d_inner = contract(d_proj_kinds, w_x_kinds.reshape(3 * rank, channels), 1, 0).astype(BF)
    grad_x = contract(d_proj_kinds, inner, 0, 0)
    grad_x = grad_x.reshape(3, dp, rank // dp, channels).transpose(1, 0, 2, 3).reshape(-1, channels)
    xproj_grad = scatter_master(grad_x, rank // dp)
    dtproj_grad = scatter_master(grad_dt, dtproj_master.shape[0])

    d_pre = (d_inner.astype(F32) + d_scan) * silu_slope(pre)
    further = jnp.concatenate([d_pre, jnp.zeros((width - 1, channels), F32)], axis=0)
    conv_rows = []
    d_xs = jnp.zeros_like(xs_value)
    for offset in range(width):
        begin = width - 1 - offset
        conv_rows.append(
            jnp.sum(d_pre * masks[offset][:, None] * extended[begin : begin + span], axis=0)
        )
        masked = further * later[offset][:, None]
        d_xs = d_xs + taps[begin][None, :] * masked[offset : offset + span]
    conv_part = jnp.stack(conv_rows[::-1], axis=0)
    conv_bias_part = jnp.sum(d_pre, axis=0)
    d_xs = jnp.where(living[:, None], d_xs, 0.0).astype(BF)
    d_z = jnp.where(living[:, None], d_z, jnp.zeros((), BF))
    d_mixed = halves_back(d_xs, d_z, wide)
    grad_in = contract(normed_kinds, d_mixed, 0, 0)
    in_grad = scatter_master(grad_in.astype(BF), in_master.shape[0]).astype(F32)

    d_normed = jnp.zeros((span, x_in.shape[1]), F32)
    w_in_kinds = w_in.reshape(dp, 3, -1, w_in.shape[1])
    for kind in range(3):
        picked = jnp.where(kinds[:, kind : kind + 1], d_mixed, jnp.zeros((), BF))
        d_normed = d_normed + contract(
            picked, w_in_kinds[:, kind].reshape(-1, w_in.shape[1]), 1, 1
        )
    d_normed = lax.psum_scatter(d_normed.astype(BF), "wide", scatter_dimension=0, tiled=True)
    d_normed = d_normed.astype(F32)
    gain_part = jnp.sum(d_normed * x_in * scale, axis=0)
    scaled_back = d_normed * norm_gain[None, :]
    x_grad = cotangent + scale * (
        scaled_back - x_in * scale * scale * jnp.mean(scaled_back * x_in, axis=1, keepdims=True)
    )

    shared = jnp.concatenate([conv_part, conv_bias_part[None], alog_part, skip_part, bias_part], axis=0)
    shared = lax.psum(shared, "dp")
    table = lax.all_gather(shared[: width + STATE + 2], "wide", axis=1, tiled=True)
    gain_grad = lax.psum(gain_part, ("dp", "wide"))
    return (
        result,
        x_grad,
        gain_grad,
        table[:width],
        table[width],
        table[width + 1 : width + 1 + STATE],
        table[width + 1 + STATE],
        in_grad,
        xproj_grad,
        dtproj_grad,
        shared[width + STATE + 2 :],
        out_grad,
    )


def solution(mesh):
    in_specs = (
        P(("dp", "wide"), None),
        P("dp", None),
        P(("dp", "wide")),
        P(),
        P(),
        P(),
        P(),
        P(),
        P("dp", None, "wide"),
        P("dp", None, "wide"),
        P("dp", None, "wide"),
        P(None, "wide"),
        P("dp", None, "wide"),
        P(("dp", "wide"), None),
    )
    out_specs = (
        P(("dp", "wide"), None),
        P(("dp", "wide"), None),
        P(),
        P(),
        P(),
        P(),
        P(),
        P("dp", None, "wide"),
        P("dp", None, "wide"),
        P("dp", None, "wide"),
        P(None, "wide"),
        P("dp", None, "wide"),
    )
    return jax.shard_map(body, mesh=mesh, in_specs=in_specs, out_specs=out_specs, check_vma=False)
```

```python
import functools

import jax
import jax.numpy as jnp
from jax import lax
from jax.experimental import pallas as pl
from jax.experimental.pallas import tpu as pltpu
from jax.sharding import PartitionSpec as P

F32 = jnp.float32
BF = jnp.bfloat16
INNER = 4096
STATE = 16
DT_RANK = 128
EPSILON = 1e-05


STEPS=16
HUGE=1e30

def scan_forward_kernel(dtp_ref,u_ref,b_ref,c_ref,keep_ref,alog_ref,skip_ref,z_ref, gated_ref,y_ref,heads_ref, st, dec, inj, ys, a2):
    T,C=u_ref.shape
    @pl.when(pl.program_id(0)==0)
    def _():
        st[...]=jnp.zeros_like(st)
        a2[...]=-jnp.exp(alog_ref[...])*1.4426950408889634
    delta=jax.nn.softplus(dtp_ref[...].astype(F32))
    u=u_ref[...].astype(F32)
    dec[...]=jnp.where(keep_ref[...]>0,delta,HUGE)
    inj[...]=delta*u
    def chunk(k,state):
        heads_ref[k]=state
        b=b_ref[k]; c=c_ref[k]
        an=a2[...]
        base=pl.multiple_of(k*STEPS,STEPS)
        for j in range(STEPS):
            d=dec[pl.ds(base+j,1),:]
            v=inj[pl.ds(base+j,1),:]
            state=jnp.exp2(d*an)*state+b[:,j:j+1]*v
            ys[pl.ds(base+j,1),:]=jnp.sum(c[:,j:j+1]*state,axis=0,keepdims=True)
        return state
    st[...]=lax.fori_loop(0,T//STEPS,chunk,st[...])
    y=ys[...]+skip_ref[...]*u
    y_ref[...]=y
    z=z_ref[...].astype(F32)
    gated_ref[...]=(y*(z*jax.nn.sigmoid(z))).astype(BF)

def scan_forward(dtp,u,b,c,keep,alog,skip,z,T=128):
    N,C=u.shape
    S=alog.shape[0]
    nk=N//STEPS; tk=T//STEPS
    row=pl.BlockSpec((T,C),lambda i:(i,0))
    col=pl.BlockSpec((tk,S,STEPS),lambda i:(i,0,0))
    whole=lambda s: pl.BlockSpec(s,lambda i:(0,0))
    return pl.pallas_call(scan_forward_kernel,grid=(N//T,),
      in_specs=[row,row,col,col,pl.BlockSpec((T,1),lambda i:(i,0)),whole((S,C)),whole((1,C)),row],
      out_specs=[row,row,pl.BlockSpec((tk,S,C),lambda i:(i,0,0))],
      out_shape=[jax.ShapeDtypeStruct((N,C),BF),jax.ShapeDtypeStruct((N,C),F32),jax.ShapeDtypeStruct((nk,S,C),F32)],
      scratch_shapes=[pltpu.VMEM((S,C),F32),pltpu.VMEM((T,C),F32),pltpu.VMEM((T,C),F32),pltpu.VMEM((T,C),F32),pltpu.VMEM((S,C),F32)],
      compiler_params=pltpu.CompilerParams(vmem_limit_bytes=48<<20),
      name="scan_forward")(dtp,u,b,c,keep,alog,skip,z)

def scan_backward_kernel(dtp_ref,u_ref,b_ref,c_ref,keep_ref,alog_ref,skip_ref,z_ref,y_ref,dg_ref,heads_ref,
        ddtp_ref,dus_ref,dz_ref,dm_ref,dalog_ref,dskip_ref, run, dec, inj, dly, dys, sq, wa, sts, dcs, an2, an1, acc):
    T,C=u_ref.shape
    S=alog_ref.shape[0]
    first=pl.program_id(0)==0
    last=pl.program_id(0)==pl.num_programs(0)-1
    @pl.when(first)
    def _():
        run[...]=jnp.zeros_like(run)
        acc[...]=jnp.zeros_like(acc)
        dskip_ref[...]=jnp.zeros_like(dskip_ref)
        an1[...]=-jnp.exp(alog_ref[...])
        an2[...]=an1[...]*1.4426950408889634
    dtp=dtp_ref[...].astype(F32)
    delta=jax.nn.softplus(dtp)
    u=u_ref[...].astype(F32)
    dec[...]=jnp.where(keep_ref[...]>0,delta,HUGE)
    dly[...]=delta
    inj[...]=delta*u
    z=z_ref[...].astype(F32)
    sg=jax.nn.sigmoid(z)
    dg=dg_ref[...].astype(F32)
    dy=dg*(z*sg)
    dys[...]=dy
    dz_ref[...]=(dg*y_ref[...]*(sg*(1.0+z*(1.0-sg)))).astype(BF)
    dskip_ref[...]+=jnp.sum(dy*u,axis=0,keepdims=True)
    def chunk(i,running):
        k=T//STEPS-1-i
        b=b_ref[k]; c=c_ref[k]
        base=pl.multiple_of(k*STEPS,STEPS)
        state=heads_ref[k]
        an=an2[...]
        for j in range(STEPS):
            d=dec[pl.ds(base+j,1),:]
            v=inj[pl.ds(base+j,1),:]
            dc=jnp.exp2(d*an)
            sd=dc*state
            state=sd+b[:,j:j+1]*v
            dcs[j]=dc
            sts[j]=sd
        lane=lax.broadcasted_iota(jnp.int32,(S,STEPS),1)
        db=jnp.zeros((S,STEPS),F32); dcc=jnp.zeros((S,STEPS),F32)
        for j in range(STEPS-1,-1,-1):
            g=dys[pl.ds(base+j,1),:]
            v=inj[pl.ds(base+j,1),:]
            bj=b[:,j:j+1]
            ds=c[:,j:j+1]*g+running
            sd=sts[j]
            w=ds*sd
            sq[pl.ds(base+j,1),:]=jnp.sum(ds*bj,axis=0,keepdims=True)
            wa[pl.ds(base+j,1),:]=jnp.sum(w*an1[...],axis=0,keepdims=True)
            acc[...]+=w*dly[pl.ds(base+j,1),:]
            db=jnp.where(lane==j,jnp.sum(ds*v,axis=1,keepdims=True),db)
            dcc=jnp.where(lane==j,jnp.sum(g*(sd+bj*v),axis=1,keepdims=True),dcc)
            running=dcs[j]*ds
        dm_ref[k,:S]=db
        dm_ref[k,S:]=dcc
        return running
    run[...]=lax.fori_loop(0,T//STEPS,chunk,run[...])
    dd=wa[...]+u*sq[...]
    ddtp_ref[...]=(dd*jax.nn.sigmoid(dtp)).astype(BF)
    dus_ref[...]=delta*sq[...]+dy*skip_ref[...]
    @pl.when(last)
    def _():
        dalog_ref[...]=acc[...]*an1[...]

def scan_backward(dtp,u,b,c,keep,alog,skip,z,y,dg,heads,T=128):
    N,C=u.shape
    S=alog.shape[0]
    nk=N//STEPS; tk=T//STEPS; nb=N//T
    row=pl.BlockSpec((T,C),lambda i:(nb-1-i,0))
    col=pl.BlockSpec((tk,S,STEPS),lambda i:(nb-1-i,0,0))
    whole=lambda s: pl.BlockSpec(s,lambda i:(0,0))
    sc=lambda *s: pltpu.VMEM(s,F32)
    return pl.pallas_call(scan_backward_kernel,grid=(nb,),
      in_specs=[row,row,col,col,pl.BlockSpec((T,1),lambda i:(nb-1-i,0)),whole((S,C)),whole((1,C)),row,row,row,pl.BlockSpec((tk,S,C),lambda i:(nb-1-i,0,0))],
      out_specs=[row,row,row,pl.BlockSpec((tk,2*S,STEPS),lambda i:(nb-1-i,0,0)),whole((S,C)),whole((1,C))],
      out_shape=[jax.ShapeDtypeStruct((N,C),BF),jax.ShapeDtypeStruct((N,C),F32),jax.ShapeDtypeStruct((N,C),BF),jax.ShapeDtypeStruct((nk,2*S,STEPS),F32),jax.ShapeDtypeStruct((S,C),F32),jax.ShapeDtypeStruct((1,C),F32)],
      scratch_shapes=[sc(S,C),sc(T,C),sc(T,C),sc(T,C),sc(T,C),sc(T,C),sc(T,C),sc(STEPS,S,C),sc(STEPS,S,C),sc(S,C),sc(S,C),sc(S,C)],
      compiler_params=pltpu.CompilerParams(vmem_limit_bytes=48<<20),
      name="scan_backward")(dtp,u,b,c,keep,alog,skip,z,y,dg,heads)


MESH = pl.DeviceIdType.MESH
FLIGHT = 3


def ring_index(position, wide):
    if wide != 8:
        return position
    turn = position // 4
    return (1 - turn) * 2 * position + turn * (2 * (7 - position) + 1)


def ring_position(index, wide):
    if wide != 8:
        return index
    return index // 2 + index % 2 * (7 - 2 * (index // 2))


def gather_kernel(dp, wide, dp_pieces, wide_chunks, *refs):
    dp_count, wide_count = len(dp_pieces), len(wide_chunks)
    inputs, refs = refs[: dp_count + wide_count], refs[dp_count + wide_count :]
    outputs, refs = refs[: dp_count + wide_count], refs[dp_count + wide_count :]
    wides, narrows, refs = refs[:dp_count], refs[dp_count : 2 * dp_count], refs[2 * dp_count :]
    x_send, x_recv, core_send, core_recv, on_send, on_recv = refs[:6]
    up_send, up_recv, down_send, down_recv, local, load = refs[6:]
    me, place = lax.axis_index("dp"), lax.axis_index("wide")
    lines = dp // 2
    line, core = me // 2, me % 2
    partner = (me + 1 - 2 * core, place)
    across = [(lax.rem(line + k, lines) * 2 + core, place) for k in range(1, lines)]
    position = ring_position(place, wide)
    after = (me, ring_index(lax.rem(position + 1, wide), wide))
    before = (me, ring_index(lax.rem(position + wide - 1, wide), wide))
    barrier = pltpu.get_barrier_semaphore()
    peers = [partner, after, before] + across
    for peer in peers:
        pl.semaphore_signal(barrier, inc=1, device_id=peer, device_id_type=MESH)
    pl.semaphore_wait(barrier, len(peers))

    def remote(source, target, send, recv, device):
        return pltpu.make_async_remote_copy(
            src_ref=source, dst_ref=target, send_sem=send, recv_sem=recv, device_id=device, device_id_type=MESH
        )

    pieces, loads, casts = [], [], []
    for a, cuts in enumerate(dp_pieces):
        rows = inputs[a].shape[1] // cuts
        for kind in range(3):
            for cut in range(cuts):
                part = pl.ds(cut * rows, rows)
                loads.append(
                    pltpu.make_async_copy(
                        inputs[a].at[kind, part], wides[a].at[kind, part], load.at[len(loads)]
                    )
                )
                casts.append((wides[a], narrows[a], kind, part))
                pieces.append(
                    (
                        narrows[a].at[kind, part],
                        lambda owner, a=a, kind=kind, part=part: outputs[a].at[owner, kind, part],
                    )
                )
    chunks = []
    for a, cuts in enumerate(wide_chunks):
        rows = inputs[dp_count + a].shape[0] // cuts
        for cut in range(cuts):
            part = pl.ds(cut * rows, rows)
            chunks.append(
                (
                    inputs[dp_count + a].at[part],
                    lambda owner, a=a, part=part: outputs[dp_count + a].at[owner, part],
                )
            )

    ups, downs = wide // 2, wide - 1 - wide // 2

    def up(hop, i):
        owner = ring_index(lax.rem(position + wide - hop, wide), wide)
        source = chunks[i][0] if hop == 0 else chunks[i][1](owner)
        return remote(source, chunks[i][1](owner), up_send.at[hop, i], up_recv.at[hop, i], after)

    def down(hop, i):
        owner = ring_index(lax.rem(position + hop, wide), wide)
        source = chunks[i][0] if hop == 0 else chunks[i][1](owner)
        return remote(source, chunks[i][1](owner), down_send.at[hop, i], down_recv.at[hop, i], before)

    def cross(k, j):
        return remote(pieces[j][0], pieces[j][1](me), x_send.at[k, j], x_recv.at[k, j], across[k])

    def pair(j):
        return remote(pieces[j][0], pieces[j][1](me), core_send.at[j], core_recv.at[j], partner)

    def onward(k, j):
        owner = lax.rem(line + lines - 1 - k, lines) * 2 + core
        return remote(pieces[j][1](owner), pieces[j][1](owner), on_send.at[k, j], on_recv.at[k, j], partner)

    for copy in loads:
        copy.start()
    for i in range(len(chunks)):
        up(0, i).start()
        if downs:
            down(0, i).start()
    copies = []
    for i, (source, target) in enumerate(chunks):
        copies.append(pltpu.make_async_copy(source, target(place), local.at[len(pieces) + i]))
        copies[-1].start()
    for j, (source, target) in enumerate(pieces):
        wide_ref, narrow_ref, kind, part = casts[j]
        loads[j].wait()
        narrow_ref[kind, part] = wide_ref[kind, part].astype(BF)
        if j < FLIGHT:
            for k in range(lines - 1):
                cross(k, j).start()
        pair(j).start()
        copies.append(pltpu.make_async_copy(source, target(me), local.at[j]))
        copies[-1].start()

    def pass_on(j):
        for k in range(lines - 1):
            cross(k, j).wait_recv()
            onward(k, j).start()
            if j + FLIGHT < len(pieces):
                cross(k, j + FLIGHT).start()

    passed = 0
    for hop in range(1, ups + 1):
        for i in range(len(chunks)):
            up(hop - 1, i).wait_recv()
            if hop < ups:
                up(hop, i).start()
            if hop <= downs:
                down(hop - 1, i).wait_recv()
                if hop < downs:
                    down(hop, i).start()
        if passed < len(pieces):
            pass_on(passed)
            passed += 1
    for j in range(passed, len(pieces)):
        pass_on(j)
    for j in range(len(pieces)):
        pair(j).wait()
        for k in range(lines - 1):
            cross(k, j).wait_send()
            onward(k, j).wait()
    for i in range(len(chunks)):
        for hop in range(ups):
            up(hop, i).wait_send()
        for hop in range(downs):
            down(hop, i).wait_send()
    for copy in copies:
        copy.wait()


def gather_all(dp_arrays, dp_pieces, wide_arrays, wide_chunks):
    dp, wide = lax.axis_size("dp"), lax.axis_size("wide")
    pieces = 3 * sum(dp_pieces)
    chunks = sum(wide_chunks)
    anywhere = pl.BlockSpec(memory_space=pl.ANY)
    dma = pltpu.SemaphoreType.DMA
    lines = dp // 2
    arrays = list(dp_arrays) + list(wide_arrays)
    shapes = [(dp,) + a.shape for a in dp_arrays] + [(wide,) + a.shape for a in wide_arrays]
    return pl.pallas_call(
        functools.partial(gather_kernel, dp, wide, tuple(dp_pieces), tuple(wide_chunks)),
        out_shape=[
            jax.ShapeDtypeStruct(s, BF if i < len(dp_arrays) else a.dtype)
            for i, (s, a) in enumerate(zip(shapes, arrays))
        ],
        in_specs=[anywhere] * len(dp_arrays) + [pl.BlockSpec(memory_space=pltpu.VMEM)] * len(wide_arrays),
        out_specs=[anywhere] * len(arrays),
        scratch_shapes=[pltpu.VMEM(a.shape, a.dtype) for a in dp_arrays]
        + [pltpu.VMEM(a.shape, BF) for a in dp_arrays]
        + [
            dma((lines - 1, pieces)),
            dma((lines - 1, pieces)),
            dma((pieces,)),
            dma((pieces,)),
            dma((lines - 1, pieces)),
            dma((lines - 1, pieces)),
            dma((wide // 2, chunks)),
            dma((wide // 2, chunks)),
            dma((wide - 1 - wide // 2, chunks)),
            dma((wide - 1 - wide // 2, chunks)),
            dma((pieces + chunks,)),
            dma((pieces,)),
        ],
        compiler_params=pltpu.CompilerParams(
            collective_id=0, has_side_effects=True, vmem_limit_bytes=40 << 20
        ),
        name="gather_all",
    )(*arrays)


def sum_wide_kernel(wide, x_ref, out_ref, got, whole, s1, r1, s2, r2):
    me, place = lax.axis_index("dp"), lax.axis_index("wide")
    step = out_ref.shape[1] // wide
    barrier = pltpu.get_barrier_semaphore()
    peers = [lax.rem(place + k, wide) for k in range(1, wide)]
    for peer in peers:
        pl.semaphore_signal(barrier, inc=1, device_id=(me, peer), device_id_type=MESH)
    pl.semaphore_wait(barrier, wide - 1)

    def columns(index):
        return pl.ds(pl.multiple_of(index * step, step), step)

    def give(k):
        return pltpu.make_async_remote_copy(
            src_ref=x_ref.at[:, columns(peers[k - 1])],
            dst_ref=got.at[k],
            send_sem=s1.at[k],
            recv_sem=r1.at[k],
            device_id=(me, peers[k - 1]),
            device_id_type=MESH,
        )

    def spread(k):
        return pltpu.make_async_remote_copy(
            src_ref=whole,
            dst_ref=out_ref.at[:, columns(place)],
            send_sem=s2.at[k],
            recv_sem=r2.at[k],
            device_id=(me, peers[k - 1]),
            device_id_type=MESH,
        )

    order = sorted(range(1, wide), key=lambda k: -min(k, wide - k))
    for k in order:
        give(k).start()
    total = x_ref[:, columns(place)].astype(F32)
    for k in reversed(order):
        give(k).wait_recv()
        total = total + got[k].astype(F32)
    whole[...] = total.astype(BF)
    for k in order:
        spread(k).start()
    out_ref[:, columns(place)] = whole[...]
    for k in range(1, wide):
        spread(k).wait()
        give(k).wait_send()


def sum_wide(x, collective_id):
    wide = lax.axis_size("wide")
    rows, span = x.shape
    vmem = pl.BlockSpec(memory_space=pltpu.VMEM)
    dma = pltpu.SemaphoreType.DMA
    return pl.pallas_call(
        functools.partial(sum_wide_kernel, wide),
        out_shape=jax.ShapeDtypeStruct((rows, span), BF),
        in_specs=[vmem],
        out_specs=vmem,
        scratch_shapes=[
            pltpu.VMEM((wide, rows, span // wide), x.dtype),
            pltpu.VMEM((rows, span // wide), BF),
            dma((wide,)),
            dma((wide,)),
            dma((wide,)),
            dma((wide,)),
        ],
        compiler_params=pltpu.CompilerParams(
            collective_id=collective_id, has_side_effects=True, vmem_limit_bytes=32 << 20
        ),
        name="sum_wide",
    )(x)


def contract(left, right, left_dim, right_dim):
    return lax.dot_general(
        left, right, (((left_dim,), (right_dim,)), ((), ())), preferred_element_type=F32
    )


def segment_of(places, bounds):
    return jnp.sum((places[:, None] >= bounds[None, :]).astype(jnp.int32), axis=1)


def conv_masks(places, bounds, width):
    segment = segment_of(places, bounds)
    return [
        ((places >= offset) & (segment_of(places - offset, bounds) == segment)).astype(F32)
        for offset in range(width)
    ]


def silu_slope(values):
    sigma = jax.nn.sigmoid(values)
    return sigma * (1.0 + values * (1.0 - sigma))


def split_kinds(rows, kinds, parts):
    count, depth = rows.shape
    pieces = rows.reshape(count, parts, 1, depth // parts)
    picked = kinds[:, None, :, None]
    return jnp.where(picked, pieces, jnp.zeros((), rows.dtype)).reshape(count, 3 * depth)


def gather_master(master):
    rows = lax.all_gather(jnp.transpose(master.astype(BF), (1, 0, 2)), "dp", axis=0)
    return rows.reshape(-1, master.shape[2])


def scatter_master(grad, rows):
    parts = lax.axis_size("dp")
    kept = lax.psum_scatter(
        grad.reshape(parts, 3, rows, grad.shape[1]), "dp", scatter_dimension=0, tiled=False
    )
    return jnp.transpose(kept, (1, 0, 2))


def hop(block, flip):
    devices = lax.axis_size("dp")
    return lax.ppermute(block, "dp", [(d, flip(d)) for d in range(devices)])


def from_partners(block):
    lines = lax.axis_size("dp") // 2
    blocks = [block, hop(block, lambda d: d ^ 1)]
    for k in range(1, lines):
        far = hop(block, lambda d: (d // 2 + k) % lines * 2 + d % 2)
        blocks += [far, hop(far, lambda d: d ^ 1)]
    return blocks


def swap_features(rows):
    devices = lax.axis_size("dp")
    lines = devices // 2
    depth = rows.shape[1] // devices
    me = lax.axis_index("dp")

    def part(owner):
        return lax.dynamic_slice_in_dim(rows, owner * depth, depth, 1)

    core = me % 2
    blocks = [part(me), hop(part(me + 1 - 2 * core), lambda d: d ^ 1)]
    for k in range(1, lines):
        line = (me // 2 + k) % lines
        blocks.append(hop(part(line * 2 + core), lambda d: (d // 2 + k) % lines * 2 + d % 2))
        blocks.append(
            hop(part(line * 2 + 1 - core), lambda d: (d // 2 + k) % lines * 2 + 1 - d % 2)
        )
    return blocks


def halves_out(block, wide):
    half = wide // 2
    columns = block.shape[1] // 2
    low = lax.axis_index("wide") < half
    first, second = block[:, :columns], block[:, columns:]
    even = [(v, 2 * v) if v < half else (v, 2 * (v - half) + 1) for v in range(wide)]
    odd = [(v, 2 * v + 1) if v < half else (v, 2 * (v - half)) for v in range(wide)]
    got_a = lax.ppermute(jnp.where(low, first, second), "wide", even)
    got_b = lax.ppermute(jnp.where(low, second, first), "wide", odd)
    is_even = lax.axis_index("wide") % 2 == 0
    return jnp.where(is_even, got_a, got_b), jnp.where(is_even, got_b, got_a)


def halves_back(xs, z, wide):
    half = wide // 2
    low = lax.axis_index("wide") < half
    even = [(2 * v, v) if v < half else (2 * (v - half) + 1, v) for v in range(wide)]
    odd = [(2 * v + 1, v) if v < half else (2 * (v - half), v) for v in range(wide)]
    is_even = lax.axis_index("wide") % 2 == 0
    got_a = lax.ppermute(jnp.where(is_even, xs, z), "wide", even)
    got_b = lax.ppermute(jnp.where(is_even, z, xs), "wide", odd)
    return jnp.concatenate([jnp.where(low, got_a, got_b), jnp.where(low, got_b, got_a)], axis=1)


def body(
    x_in,
    lengths,
    modality,
    norm_gain,
    conv_weight,
    conv_bias,
    a_log,
    d_skip,
    in_master,
    xproj_master,
    dtproj_master,
    dt_bias,
    out_master,
    cotangent,
):
    wide, dp = lax.axis_size("wide"), lax.axis_size("dp")
    place = lax.axis_index("wide")
    count = x_in.shape[0]
    span = count * wide
    channels = INNER // wide
    width = conv_weight.shape[0]
    own = lambda table: lax.dynamic_slice_in_dim(table, place * channels, channels, table.ndim - 1)

    bounds = jnp.cumsum(lengths.reshape(-1))
    places = jnp.arange(span, dtype=jnp.int32)
    living = places < bounds[-1]
    masks = conv_masks(places, bounds, width)
    later = conv_masks(jnp.arange(span + width - 1, dtype=jnp.int32), bounds, width)
    alive_here = (place * count + jnp.arange(count, dtype=jnp.int32)) < bounds[-1]

    scale = lax.rsqrt(jnp.mean(x_in * x_in, axis=1, keepdims=True) + EPSILON)
    normed = (x_in * scale * norm_gain[None, :]).astype(BF)
    d_branch = jnp.where(alive_here[:, None], cotangent, 0.0).astype(BF)
    rank_rows, step_rows = xproj_master.shape[0], dtproj_master.shape[0]
    small = jnp.concatenate([xproj_master, dtproj_master], axis=0)
    small = jnp.pad(small, ((0, -small.shape[0] % 16), (0, 0), (0, 0)))
    w_in, w_small, normed_all, kinds_all = gather_all(
        [jnp.transpose(in_master, (1, 0, 2)), jnp.transpose(small, (1, 0, 2))],
        [2, 1],
        [normed, jnp.broadcast_to(modality[None], (8, count))],
        [2, 1],
    )
    w_in = w_in.reshape(-1, in_master.shape[2])
    normed_all = normed_all.reshape(span, -1)
    kinds_all = kinds_all[:, 0].reshape(span)
    w_x_kinds = w_small[:, :, :rank_rows].transpose(1, 0, 2, 3).reshape(3, -1, channels)
    w_dt_kinds = w_small[:, :, rank_rows : rank_rows + step_rows].transpose(1, 0, 2, 3)
    w_dt_kinds = w_dt_kinds.reshape(3, DT_RANK, channels)
    w_out = gather_master(out_master)
    d_branch_all = lax.all_gather(d_branch, "wide", axis=0, tiled=True)
    kinds = (kinds_all[:, None] == jnp.arange(3, dtype=jnp.int32)[None, :]) & living[:, None]

    normed_kinds = split_kinds(normed_all, kinds, dp)
    kinds_parts = from_partners(kinds.astype(BF))
    feature_kinds = [
        split_kinds(rows, tags > 0, 1)
        for rows, tags in zip(swap_features(normed_all), kinds_parts)
    ]
    mixed = contract(normed_kinds, w_in, 1, 0).astype(BF)
    xs, z = halves_out(mixed, wide)

    taps = own(conv_weight)
    xs_value = xs.astype(F32)
    extended = jnp.concatenate([jnp.zeros((width - 1, channels), F32), xs_value], axis=0)
    pre = own(conv_bias)[None, :]
    for offset in range(width):
        begin = width - 1 - offset
        pre = (
            pre + taps[begin][None, :] * extended[begin : begin + span] * masks[offset][:, None]
        )
    inner = jax.nn.silu(pre).astype(BF)

    rank = w_x_kinds.shape[1]
    across = kinds.T[:, None, :]
    by_kind = contract(w_x_kinds.reshape(3 * rank, channels), inner, 1, 1).reshape(3, rank, span)
    proj = sum_wide(jnp.sum(jnp.where(across, by_kind, 0.0), axis=0), 1)
    rates = proj[:DT_RANK].T
    maps = proj[DT_RANK:].astype(F32)
    rates_kinds = split_kinds(rates, kinds, 1)
    bias = jnp.where(kinds[:, :, None], dt_bias.astype(BF).astype(F32)[None], 0.0).sum(axis=1)
    dtp = (contract(rates_kinds, w_dt_kinds.reshape(3 * DT_RANK, channels), 1, 0) + bias).astype(BF)

    blocks = span // STEPS
    to_columns = lambda rows: rows.reshape(-1, blocks, STEPS).transpose(1, 0, 2)
    b_columns = to_columns(maps[:STATE])
    c_columns = to_columns(maps[STATE:])
    keep = masks[1][:, None]
    a_own = own(a_log)
    skip_own = own(d_skip)[None, :]
    gated, y_value, heads = scan_forward(dtp, inner, b_columns, c_columns, keep, a_own, skip_own, z)

    d_branch_kinds = split_kinds(d_branch_all, kinds, dp)
    d_gated = contract(d_branch_kinds, w_out, 1, 0).astype(BF)
    w_out_kinds = w_out.reshape(dp, 3, -1, channels)
    branch = jnp.zeros((span, x_in.shape[1]), F32)
    for kind in range(3):
        picked = jnp.where(kinds[:, kind : kind + 1], gated, jnp.zeros((), BF))
        branch = branch + contract(picked, w_out_kinds[:, kind].reshape(-1, channels), 1, 1)
    branch = lax.psum_scatter(branch.astype(BF), "wide", scatter_dimension=0, tiled=True)
    result = x_in + branch.astype(F32)
    grad_out = contract(d_branch_kinds, gated, 0, 0)
    out_grad = scatter_master(grad_out.astype(BF), out_master.shape[0]).astype(F32)

    d_dtp, d_scan, d_z, d_columns, alog_part, skip_part = scan_backward(
        dtp, inner, b_columns, c_columns, keep, a_own, skip_own, z, y_value, d_gated, heads
    )
    d_dtp = jnp.where(living[:, None], d_dtp, jnp.zeros((), BF))
    d_maps = d_columns.transpose(1, 0, 2).reshape(2 * STATE, span)
    by_kind = contract(w_dt_kinds.reshape(3 * DT_RANK, channels), d_dtp, 1, 1)
    d_rates = jnp.sum(jnp.where(across, by_kind.reshape(3, DT_RANK, span), 0.0), axis=0)
    d_proj = sum_wide(jnp.concatenate([d_rates, d_maps], axis=0), 2)
    d_proj = jnp.where(living[None], d_proj, jnp.zeros((), BF)).T
    grad_dt = contract(rates_kinds, d_dtp, 0, 0).reshape(3, dp, step_rows, channels)
    grad_dt = grad_dt.transpose(1, 0, 2, 3).reshape(-1, channels)
    bias_part = jnp.stack(
        [jnp.sum(jnp.where(kinds[:, k : k + 1], d_dtp.astype(F32), 0.0), axis=0) for k in range(3)]
    )
    d_proj_kinds = split_kinds(d_proj, kinds, 1)
    d_inner = contract(d_proj_kinds, w_x_kinds.reshape(3 * rank, channels), 1, 0).astype(BF)
    grad_x = contract(d_proj_kinds, inner, 0, 0)
    grad_x = grad_x.reshape(3, dp, rank_rows, channels).transpose(1, 0, 2, 3).reshape(-1, channels)
    xproj_grad = scatter_master(grad_x, rank_rows)
    dtproj_grad = scatter_master(grad_dt, step_rows)

    d_pre = (d_inner.astype(F32) + d_scan) * silu_slope(pre)
    further = jnp.concatenate([d_pre, jnp.zeros((width - 1, channels), F32)], axis=0)
    conv_rows = []
    d_xs = jnp.zeros_like(xs_value)
    for offset in range(width):
        begin = width - 1 - offset
        conv_rows.append(
            jnp.sum(d_pre * masks[offset][:, None] * extended[begin : begin + span], axis=0)
        )
        masked = further * later[offset][:, None]
        d_xs = d_xs + taps[begin][None, :] * masked[offset : offset + span]
    conv_part = jnp.stack(conv_rows[::-1], axis=0)
    conv_bias_part = jnp.sum(d_pre, axis=0)
    d_xs = jnp.where(living[:, None], d_xs, 0.0).astype(BF)
    d_z = jnp.where(living[:, None], d_z, jnp.zeros((), BF))
    d_mixed = halves_back(d_xs, d_z, wide)
    mixed_parts = from_partners(d_mixed)
    grad_in = 0.0
    for pair in range(0, dp, 2):
        left = jnp.concatenate(feature_kinds[pair : pair + 2], axis=0)
        grad_in = grad_in + contract(left, jnp.concatenate(mixed_parts[pair : pair + 2], axis=0), 0, 0)
    in_grad = jnp.transpose(grad_in.reshape(3, -1, d_mixed.shape[1]), (1, 0, 2))

    d_normed = jnp.zeros((span, x_in.shape[1]), F32)
    w_in_kinds = w_in.reshape(dp, 3, -1, w_in.shape[1])
    for kind in range(3):
        picked = jnp.where(kinds[:, kind : kind + 1], d_mixed, jnp.zeros((), BF))
        d_normed = d_normed + contract(
            picked, w_in_kinds[:, kind].reshape(-1, w_in.shape[1]), 1, 1
        )
    d_normed = lax.psum_scatter(d_normed.astype(BF), "wide", scatter_dimension=0, tiled=True)
    d_normed = d_normed.astype(F32)
    gain_part = jnp.sum(d_normed * x_in * scale, axis=0)
    scaled_back = d_normed * norm_gain[None, :]
    x_grad = cotangent + scale * (
        scaled_back - x_in * scale * scale * jnp.mean(scaled_back * x_in, axis=1, keepdims=True)
    )

    shared = jnp.concatenate([conv_part, conv_bias_part[None], alog_part, skip_part, bias_part], axis=0)
    shared = lax.psum(shared, "dp")
    table = lax.all_gather(shared[: width + STATE + 2], "wide", axis=1, tiled=True)
    gain_grad = lax.psum(gain_part, ("dp", "wide"))
    return (
        result,
        x_grad,
        gain_grad,
        table[:width],
        table[width],
        table[width + 1 : width + 1 + STATE],
        table[width + 1 + STATE],
        in_grad,
        xproj_grad,
        dtproj_grad,
        shared[width + STATE + 2 :],
        out_grad,
    )


def solution(mesh):
    in_specs = (
        P(("dp", "wide"), None),
        P("dp", None),
        P(("dp", "wide")),
        P(),
        P(),
        P(),
        P(),
        P(),
        P("dp", None, "wide"),
        P("dp", None, "wide"),
        P("dp", None, "wide"),
        P(None, "wide"),
        P("dp", None, "wide"),
        P(("dp", "wide"), None),
    )
    out_specs = (
        P(("dp", "wide"), None),
        P(("dp", "wide"), None),
        P(),
        P(),
        P(),
        P(),
        P(),
        P("dp", None, "wide"),
        P("dp", None, "wide"),
        P("dp", None, "wide"),
        P(None, "wide"),
        P("dp", None, "wide"),
    )
    return jax.shard_map(body, mesh=mesh, in_specs=in_specs, out_specs=out_specs, check_vma=False)
```

```python
import functools

import jax
import jax.numpy as jnp
from jax import lax
from jax.experimental import pallas as pl
from jax.experimental.pallas import tpu as pltpu
from jax.sharding import PartitionSpec as P

F32 = jnp.float32
BF = jnp.bfloat16
INNER = 4096
STATE = 16
DT_RANK = 128
EPSILON = 1e-05


STEPS=32
HUGE=1e30

def scan_forward_kernel(dtp_ref,u_ref,b_ref,c_ref,keep_ref,alog_ref,skip_ref,z_ref, gated_ref,y_ref,heads_ref, st, dec, inj, ys, a2):
    T,C=u_ref.shape
    @pl.when(pl.program_id(0)==0)
    def _():
        st[...]=jnp.zeros_like(st)
        a2[...]=-jnp.exp(alog_ref[...])*1.4426950408889634
    delta=jax.nn.softplus(dtp_ref[...].astype(F32))
    u=u_ref[...].astype(F32)
    dec[...]=jnp.where(keep_ref[...]>0,delta,HUGE)
    inj[...]=delta*u
    def chunk(k,state):
        heads_ref[k]=state
        b=b_ref[k]; c=c_ref[k]
        an=a2[...]
        base=pl.multiple_of(k*STEPS,STEPS)
        for j in range(STEPS):
            d=dec[pl.ds(base+j,1),:]
            v=inj[pl.ds(base+j,1),:]
            state=jnp.exp2(d*an)*state+b[:,j:j+1]*v
            ys[pl.ds(base+j,1),:]=jnp.sum(c[:,j:j+1]*state,axis=0,keepdims=True)
        return state
    st[...]=lax.fori_loop(0,T//STEPS,chunk,st[...])
    y=ys[...]+skip_ref[...]*u
    y_ref[...]=y
    z=z_ref[...].astype(F32)
    gated_ref[...]=(y*(z*jax.nn.sigmoid(z))).astype(BF)

def scan_forward(dtp,u,b,c,keep,alog,skip,z,T=128):
    N,C=u.shape
    S=alog.shape[0]
    nk=N//STEPS; tk=T//STEPS
    row=pl.BlockSpec((T,C),lambda i:(i,0))
    col=pl.BlockSpec((tk,S,STEPS),lambda i:(i,0,0))
    whole=lambda s: pl.BlockSpec(s,lambda i:(0,0))
    return pl.pallas_call(scan_forward_kernel,grid=(N//T,),
      in_specs=[row,row,col,col,pl.BlockSpec((T,1),lambda i:(i,0)),whole((S,C)),whole((1,C)),row],
      out_specs=[row,row,pl.BlockSpec((tk,S,C),lambda i:(i,0,0))],
      out_shape=[jax.ShapeDtypeStruct((N,C),BF),jax.ShapeDtypeStruct((N,C),F32),jax.ShapeDtypeStruct((nk,S,C),F32)],
      scratch_shapes=[pltpu.VMEM((S,C),F32),pltpu.VMEM((T,C),F32),pltpu.VMEM((T,C),F32),pltpu.VMEM((T,C),F32),pltpu.VMEM((S,C),F32)],
      compiler_params=pltpu.CompilerParams(vmem_limit_bytes=48<<20),
      name="scan_forward")(dtp,u,b,c,keep,alog,skip,z)

def fold_lanes(values):
    total=values[:,:128]
    for k in range(128,values.shape[1],128):
        total=total+values[:,k:k+128]
    return total

def sum_lanes(ref):
    values=ref[...].reshape(-1,128)
    high=values.astype(BF)
    rest=(values-high.astype(F32)).astype(BF)
    ones=jnp.ones((8,128),BF)
    dims=(((1,),(1,)),((),()))
    return (lax.dot_general(ones,high,dims,preferred_element_type=F32)+lax.dot_general(ones,rest,dims,preferred_element_type=F32))[:1]

def scan_backward_kernel(dtp_ref,u_ref,b_ref,c_ref,keep_ref,alog_ref,skip_ref,z_ref,y_ref,dg_ref,heads_ref,
        ddtp_ref,dus_ref,dz_ref,dm_ref,dalog_ref,dskip_ref, run, dec, inj, dly, dys, sq, wa, sts, dcs, an2, an1, acc, pb, pc):
    T,C=u_ref.shape
    S=alog_ref.shape[0]
    first=pl.program_id(0)==0
    last=pl.program_id(0)==pl.num_programs(0)-1
    @pl.when(first)
    def _():
        run[...]=jnp.zeros_like(run)
        acc[...]=jnp.zeros_like(acc)
        dskip_ref[...]=jnp.zeros_like(dskip_ref)
        an1[...]=-jnp.exp(alog_ref[...])
        an2[...]=an1[...]*1.4426950408889634
    dtp=dtp_ref[...].astype(F32)
    delta=jax.nn.softplus(dtp)
    u=u_ref[...].astype(F32)
    dec[...]=jnp.where(keep_ref[...]>0,delta,HUGE)
    dly[...]=delta
    inj[...]=delta*u
    z=z_ref[...].astype(F32)
    sg=jax.nn.sigmoid(z)
    dg=dg_ref[...].astype(F32)
    dy=dg*(z*sg)
    dys[...]=dy
    dz_ref[...]=(dg*y_ref[...]*(sg*(1.0+z*(1.0-sg)))).astype(BF)
    dskip_ref[...]+=jnp.sum(dy*u,axis=0,keepdims=True)
    def chunk(i,running):
        k=T//STEPS-1-i
        b=b_ref[k]; c=c_ref[k]
        base=pl.multiple_of(k*STEPS,STEPS)
        state=heads_ref[k]
        an=an2[...]
        for j in range(STEPS):
            d=dec[pl.ds(base+j,1),:]
            v=inj[pl.ds(base+j,1),:]
            dc=jnp.exp2(d*an)
            sd=dc*state
            state=sd+b[:,j:j+1]*v
            dcs[j]=dc
            sts[j]=sd
        for j in range(STEPS-1,-1,-1):
            g=dys[pl.ds(base+j,1),:]
            v=inj[pl.ds(base+j,1),:]
            bj=b[:,j:j+1]
            ds=c[:,j:j+1]*g+running
            sd=sts[j]
            w=ds*sd
            sq[pl.ds(base+j,1),:]=jnp.sum(ds*bj,axis=0,keepdims=True)
            wa[pl.ds(base+j,1),:]=jnp.sum(w*an1[...],axis=0,keepdims=True)
            acc[...]+=w*dly[pl.ds(base+j,1),:]
            pb[base+j]=fold_lanes(ds*v)
            pc[base+j]=fold_lanes(g*(sd+bj*v))
            running=dcs[j]*ds
        return running
    run[...]=lax.fori_loop(0,T//STEPS,chunk,run[...])
    dm_ref[0,0:1]=sum_lanes(pb)
    dm_ref[0,1:2]=sum_lanes(pc)
    dd=wa[...]+u*sq[...]
    ddtp_ref[...]=(dd*jax.nn.sigmoid(dtp)).astype(BF)
    dus_ref[...]=delta*sq[...]+dy*skip_ref[...]
    @pl.when(last)
    def _():
        dalog_ref[...]=acc[...]*an1[...]

def scan_backward(dtp,u,b,c,keep,alog,skip,z,y,dg,heads,T=128):
    N,C=u.shape
    S=alog.shape[0]
    nk=N//STEPS; tk=T//STEPS; nb=N//T
    row=pl.BlockSpec((T,C),lambda i:(nb-1-i,0))
    col=pl.BlockSpec((tk,S,STEPS),lambda i:(nb-1-i,0,0))
    whole=lambda s: pl.BlockSpec(s,lambda i:(0,0))
    sc=lambda *s: pltpu.VMEM(s,F32)
    return pl.pallas_call(scan_backward_kernel,grid=(nb,),
      in_specs=[row,row,col,col,pl.BlockSpec((T,1),lambda i:(nb-1-i,0)),whole((S,C)),whole((1,C)),row,row,row,pl.BlockSpec((tk,S,C),lambda i:(nb-1-i,0,0))],
      out_specs=[row,row,row,pl.BlockSpec((1,2,T*S),lambda i:(nb-1-i,0,0)),whole((S,C)),whole((1,C))],
      out_shape=[jax.ShapeDtypeStruct((N,C),BF),jax.ShapeDtypeStruct((N,C),F32),jax.ShapeDtypeStruct((N,C),BF),jax.ShapeDtypeStruct((nb,2,T*S),F32),jax.ShapeDtypeStruct((S,C),F32),jax.ShapeDtypeStruct((1,C),F32)],
      scratch_shapes=[sc(S,C),sc(T,C),sc(T,C),sc(T,C),sc(T,C),sc(T,C),sc(T,C),sc(STEPS,S,C),sc(STEPS,S,C),sc(S,C),sc(S,C),sc(S,C),sc(T,S,128),sc(T,S,128)],
      compiler_params=pltpu.CompilerParams(vmem_limit_bytes=48<<20),
      name="scan_backward")(dtp,u,b,c,keep,alog,skip,z,y,dg,heads)


CUTS = 2
MESH = pl.DeviceIdType.MESH
FLIGHT = 6
TILE = 256
SMALL, OUTER = 100, 200


def ring_index(position, wide):
    if wide != 8:
        return position
    turn = position // 4
    return (1 - turn) * 2 * position + turn * (2 * (7 - position) + 1)


def ring_position(index, wide):
    if wide != 8:
        return index
    return index // 2 + index % 2 * (7 - 2 * (index // 2))


def remote(source, target, send, recv, device):
    return pltpu.make_async_remote_copy(
        src_ref=source, dst_ref=target, send_sem=send, recv_sem=recv, device_id=device, device_id_type=MESH
    )


def sum_over_wide(wide, me, place, x_ref, out_ref, got, whole, s1, r1, s2, r2):
    step = out_ref.shape[1] // wide
    peers = [lax.rem(place + k, wide) for k in range(1, wide)]

    def columns(index):
        return pl.ds(pl.multiple_of(index * step, step), step)

    def give(k):
        device = (me, peers[k - 1])
        return remote(x_ref.at[:, columns(peers[k - 1])], got.at[k], s1.at[k], r1.at[k], device)

    def spread(k):
        device = (me, peers[k - 1])
        return remote(whole, out_ref.at[:, columns(place)], s2.at[k], r2.at[k], device)

    order = sorted(range(1, wide), key=lambda k: -min(k, wide - k))
    for k in order:
        give(k).start()
    total = x_ref[:, columns(place)].astype(F32)
    for k in reversed(order):
        give(k).wait_recv()
        total = total + got[k].astype(F32)
    whole[...] = total.astype(BF)
    for k in order:
        spread(k).start()
    out_ref[:, columns(place)] = whole[...]
    for k in range(1, wide):
        spread(k).wait()
        give(k).wait_send()


class Spread:
    def __init__(self, wide, me, place, arrays, sems):
        self.wide, self.me, self.place, self.arrays = wide, me, place, arrays
        self.up_send, self.up_recv, self.down_send, self.down_recv, self.all_send, self.all_recv = sems
        self.z, self.y = place // 2, place % 2

    def copy(self, i, owner, source, send, recv, target):
        ref = self.arrays[i][0] if source else self.arrays[i][1].at[owner]
        return remote(ref, self.arrays[i][1].at[owner], send, recv, (self.me, target))

    def up(self, i, hop):
        owner = (self.z - hop) * 2 + self.y
        return self.copy(i, owner, hop == 0, self.up_send.at[hop, i], self.up_recv.at[hop, i], self.place + 2)

    def down(self, i, hop):
        owner = (self.z + hop) * 2 + self.y
        return self.copy(i, owner, hop == 0, self.down_send.at[hop, i], self.down_recv.at[hop, i], self.place - 2)

    def beside(self, i, z, own=False):
        owner = z * 2 + self.y
        return self.copy(i, owner, own, self.all_send.at[z, i], self.all_recv.at[z, i], self.place + 1 - 2 * self.y)

    def direct(self, i, k):
        target = lax.rem(self.place + k, self.wide)
        return self.copy(i, self.place, True, self.all_send.at[k, i], self.all_recv.at[k, i], target)

    def begin(self, i):
        if self.wide != 8:
            for k in range(1, self.wide):
                self.direct(i, k).start()
            return

        @pl.when(self.z < 3)
        def _():
            self.up(i, 0).start()

        @pl.when(self.z > 0)
        def _():
            self.down(i, 0).start()

        self.beside(i, self.z, True).start()

    def step(self, i, hop):
        if self.wide != 8:
            return

        @pl.when(self.z > hop)
        def _():
            self.up(i, hop).wait_recv()
            if hop < 2:

                @pl.when(self.z < 3)
                def _():
                    self.up(i, hop + 1).start()

            self.beside(i, self.z - 1 - hop).start()

        @pl.when(self.z + hop < 3)
        def _():
            self.down(i, hop).wait_recv()
            if hop < 2:

                @pl.when(self.z > 0)
                def _():
                    self.down(i, hop + 1).start()

            self.beside(i, self.z + 1 + hop).start()

    def end(self, i):
        if self.wide != 8:
            for k in range(1, self.wide):
                self.direct(i, k).wait_recv()
            return
        for z in range(4):
            self.beside(i, z).wait_recv()

    def sent(self):
        for i in range(len(self.arrays)):
            if self.wide != 8:
                for k in range(1, self.wide):
                    self.direct(i, k).wait_send()
                continue
            for hop in range(3):

                @pl.when((self.z >= hop) & (self.z < 3))
                def _():
                    self.up(i, hop).wait_send()

                @pl.when((self.z + hop <= 3) & (self.z > 0))
                def _():
                    self.down(i, hop).wait_send()

            for z in range(4):
                self.beside(i, z).wait_send()


def front_kernel(dp, wide, rank_rows, *refs):
    win_ref, wout_ref, small_ref, normed_ref, back_ref, tag_ref, masks_ref, taps_ref, bias_ref, refs = *refs[:9], refs[9:]
    wall_out, wout_out, wsmall_out, nall_out, ball_out, tags_out, xs_out, z_out, u_ref, proj_ref, refs = *refs[:10], refs[10:]
    stage, stage_out, wout_low, wall, wsmall, nall, tags, mixed, xz, part, part_low, got, whole, refs = *refs[:13], refs[13:]
    x_send, x_recv, core_send, core_recv, on_send, on_recv, refs = *refs[:6], refs[6:]
    h_send, h_recv, h_local, load, keep = refs[:5]
    s1, r1, s2, r2 = refs[5:9]
    me, place = lax.axis_index("dp"), lax.axis_index("wide")
    cuts, span, narrow = mixed.shape
    half = wide // 2
    count = normed_ref.shape[0]
    rows = win_ref.shape[1]
    lines = dp // 2
    line, core = me // 2, me % 2
    partner = (me + 1 - 2 * core, place)
    across = [(lax.rem(line + k, lines) * 2 + core, place) for k in range(1, lines)]
    barrier = pltpu.get_barrier_semaphore()
    for peer in [partner] + across + [(me, lax.rem(place + k, wide)) for k in range(1, wide)]:
        pl.semaphore_signal(barrier, inc=1, device_id=peer, device_id_type=MESH)
    pl.semaphore_wait(barrier, lines + wide - 1)

    turns = [h * (cuts // 2) + i for i in range(cuts // 2) for h in range(2)]
    pieces = [(q, kind) for q in turns for kind in range(3)]
    pieces += [(SMALL, kind) for kind in range(3)]
    pieces += [(OUTER + h, kind) for kind in range(3) for h in range(2)]
    height = wout_ref.shape[1] // 2

    def slot(j, owner):
        q, kind = pieces[j]
        if q >= OUTER:
            return wout_out.at[owner, kind, pl.ds((q - OUTER) * height, height)]
        if q == SMALL:
            return wsmall.at[owner, kind]
        return wall.at[owner, kind, :, pl.ds(q * narrow, narrow)]

    def mine(j):
        q, kind = pieces[j]
        if q >= OUTER:
            return wout_low.at[kind, pl.ds((q - OUTER) * height, height)]
        return slot(j, me)

    def cross(k, j):
        return remote(mine(j), slot(j, me), x_send.at[k, j], x_recv.at[k, j], across[k])

    def pair(j):
        return remote(mine(j), slot(j, me), core_send.at[j], core_recv.at[j], partner)

    def onward(k, j):
        owner = lax.rem(line + lines - 1 - k, lines) * 2 + core
        return remote(slot(j, owner), slot(j, owner), on_send.at[k, j], on_recv.at[k, j], partner)

    loads = []
    for q in turns:
        part_columns = pl.ds(q * narrow, narrow)
        loads.append(pltpu.make_async_copy(win_ref.at[:, :, part_columns], stage.at[:, :, part_columns], load.at[q]))
        loads[-1].start()
    loads.append(pltpu.make_async_copy(wout_ref, stage_out, load.at[cuts]))
    loads[-1].start()

    nall[place] = normed_ref[...]
    tags[place] = tag_ref[...]
    kept = [pltpu.make_async_copy(back_ref, ball_out.at[place], keep.at[0])]
    kept[-1].start()
    spread = Spread(
        wide,
        me,
        place,
        [
            (nall.at[place, pl.ds(0, count // 2)], nall.at[:, pl.ds(0, count // 2)]),
            (nall.at[place, pl.ds(count // 2, count // 2)], nall.at[:, pl.ds(count // 2, count // 2)]),
            (tags.at[place], tags),
            (back_ref, ball_out),
        ],
        refs[9:],
    )
    for i in range(3):
        spread.begin(i)
    for j, (q, kind) in enumerate(pieces):
        if q >= OUTER:
            if j == 3 * cuts + 3:
                loads[cuts].wait()
            part_rows = pl.ds((q - OUTER) * height, height)
            wout_low[kind, part_rows] = stage_out[kind, part_rows].astype(BF)
        elif q == SMALL:
            wsmall[me, kind] = small_ref[kind].astype(BF)
        else:
            if kind == 0:
                loads[turns.index(q)].wait()
            wall[me, kind, :, q * narrow : (q + 1) * narrow] = stage[
                kind, :, q * narrow : (q + 1) * narrow
            ].astype(BF)
        if j < FLIGHT:
            for k in range(lines - 1):
                cross(k, j).start()
        pair(j).start()

    kept.append(pltpu.make_async_copy(wout_low, wout_out.at[me], keep.at[1]))
    kept[-1].start()
    state = {"passed": 0}

    def pass_on(until):
        for j in range(state["passed"], min(until, len(pieces))):
            for k in range(lines - 1):
                cross(k, j).wait_recv()
                onward(k, j).start()
                if j < 3 * cuts and j + FLIGHT < len(pieces):
                    cross(k, j + FLIGHT).start()
                if j == 3 * cuts - 1:
                    for later in range(j + FLIGHT + 1, len(pieces)):
                        cross(k, later).start()
            state["passed"] = j + 1

    for hop in range(3):
        for i in range(3):
            spread.step(i, hop)
        pass_on(2 * (hop + 1))
    for i in range(3):
        spread.end(i)
    spread.begin(3)

    low = place // half
    home = place % half

    def deliver(q):
        return remote(
            mixed.at[q], xz.at[low, q % (cuts // 2)], h_send.at[q], h_recv.at[low, q % (cuts // 2)],
            (me, 2 * home + q // (cuts // 2)),
        )

    def stay(q):
        return pltpu.make_async_copy(mixed.at[q], xz.at[low, q % (cuts // 2)], h_local.at[q])

    blocks = TILE // count
    for turn, q in enumerate(turns):
        pass_on((turn + 1) * 3)
        for j in range(3 * turn, 3 * turn + 3):
            pair(j).wait_recv()
            for k in range(lines - 1):
                onward(k, j).wait_recv()

        def tile(t, carry, q=q):
            left = nall[pl.ds(t * blocks, blocks)].reshape(TILE, -1)
            tag = tags[pl.ds(t * blocks, blocks)].reshape(TILE, -1)[:, :1].astype(F32)
            total = jnp.zeros((TILE, narrow), F32)
            for kind in range(3):
                product = jnp.zeros((TILE, narrow), F32)
                for owner in range(dp):
                    product += jnp.dot(
                        left[:, owner * rows : (owner + 1) * rows],
                        wall[owner, kind, :, q * narrow : (q + 1) * narrow],
                        preferred_element_type=F32,
                    )
                total = total + jnp.where(tag == kind, product, 0.0)
            mixed[q, pl.ds(pl.multiple_of(t * TILE, TILE), TILE)] = total.astype(BF)
            return carry

        lax.fori_loop(0, span // TILE, tile, 0)
        target = 2 * home + q // (cuts // 2)

        @pl.when(target != place)
        def _(q=q):
            deliver(q).start()

        @pl.when(target == place)
        def _(q=q):
            stay(q).start()

        if turn > 0:
            spread.step(3, turn - 1)
        if turn == 0:
            for source, sink in ((nall, nall_out), (tags, tags_out)):
                kept.append(pltpu.make_async_copy(source, sink, keep.at[len(kept)]))
                kept[-1].start()
    pass_on(3 * cuts + 3)
    kept.append(pltpu.make_async_copy(wall, wall_out, keep.at[len(kept)]))
    kept[-1].start()

    def arrive(kind, i):
        source = kind * half + place // 2
        q = place % 2 * (cuts // 2) + i

        @pl.when(source != place)
        def _():
            remote(mixed.at[0], xz.at[kind, i], h_send.at[0], h_recv.at[kind, i], partner).wait_recv()

        @pl.when(source == place)
        def _():
            pltpu.make_async_copy(mixed.at[q], xz.at[kind, i], h_local.at[q]).wait()

    taps_all = taps_ref[...]
    width = taps_all.shape[0]
    for i in range(cuts // 2):
        arrive(0, i)
        taps = taps_all[:, i * narrow : (i + 1) * narrow]
        bias = bias_ref[:, i * narrow : (i + 1) * narrow]

        def conv(t, carry, i=i, taps=taps, bias=bias):
            at = pl.multiple_of(t * 128, 128)
            behind = pl.multiple_of(jnp.maximum(t * 128 - 16, 0), 16)
            here = xz[0, i, pl.ds(at, 128)].astype(F32)
            both = jnp.concatenate([xz[0, i, pl.ds(behind, 16)].astype(F32), here], axis=0)
            masks = masks_ref[pl.ds(at, 128)]
            pre = bias + taps[width - 1 : width] * here
            for offset in range(1, width):
                pre = pre + taps[width - 1 - offset : width - offset] * (
                    both[16 - offset : 144 - offset] * masks[:, offset : offset + 1]
                )
            u_ref[pl.ds(at, 128), i * narrow : (i + 1) * narrow] = (pre * jax.nn.sigmoid(pre)).astype(BF)
            return carry

        lax.fori_loop(0, span // 128, conv, 0)

    for j in range(3 * cuts, 3 * cuts + 3):
        pair(j).wait_recv()
        for k in range(lines - 1):
            onward(k, j).wait_recv()

    def project(t, carry):
        at = pl.multiple_of(t * TILE, TILE)
        inner = u_ref[pl.ds(at, TILE)].astype(F32)
        tag = tags[pl.ds(t * blocks, blocks)].reshape(TILE, -1)[:, :1].astype(F32)
        chosen = [jnp.where(tag == kind, inner, 0.0).astype(BF) for kind in range(3)]
        for owner in range(dp):
            total = jnp.zeros((wsmall.shape[2], TILE), F32)
            for kind in range(3):
                total += lax.dot_general(
                    wsmall[owner, kind], chosen[kind], (((1,), (1,)), ((), ())), preferred_element_type=F32
                )
            part[owner * rank_rows : (owner + 1) * rank_rows, pl.ds(at, TILE)] = total[:rank_rows]
        return carry

    pass_on(3 * cuts + 6)
    lax.fori_loop(0, span // TILE, project, 0)
    part_low[...] = part[...].astype(BF)
    sum_over_wide(wide, me, place, part_low, proj_ref, got, whole, s1, r1, s2, r2)

    pass_on(len(pieces))
    for hop in range(cuts - 1, 3):
        spread.step(3, hop)
    spread.end(3)
    kept.append(pltpu.make_async_copy(wsmall, wsmall_out, keep.at[len(kept)]))
    kept[-1].start()
    for i in range(cuts // 2):
        arrive(1, i)
    for i in range(cuts // 2):
        xs_out[:, i * narrow : (i + 1) * narrow] = xz[0, i]
        z_out[:, i * narrow : (i + 1) * narrow] = xz[1, i]
    for j in range(3 * cuts + 3, len(pieces)):
        pair(j).wait_recv()
        for k in range(lines - 1):
            onward(k, j).wait_recv()
    for j in range(len(pieces)):
        pair(j).wait_send()
        for k in range(lines - 1):
            cross(k, j).wait_send()
            onward(k, j).wait_send()
    spread.sent()
    for q in range(cuts):

        @pl.when(2 * home + q // (cuts // 2) != place)
        def _(q=q):
            deliver(q).wait_send()

    for copy in kept:
        copy.wait()


def front(win, wout, small, normed, back, tag, masks, taps, bias, rank_rows, collective_id):
    dp, wide = lax.axis_size("dp"), lax.axis_size("wide")
    kinds, rows, columns = win.shape
    cuts = 4 if columns >= 512 else 2
    narrow = columns // cuts
    count, depth = normed.shape
    span = count * wide
    channels = small.shape[2]
    rank = rank_rows * dp
    lines = dp // 2
    pieces = 3 * cuts + 9
    vmem = pl.BlockSpec(memory_space=pltpu.VMEM)
    anywhere = pl.BlockSpec(memory_space=pl.ANY)
    dma = pltpu.SemaphoreType.DMA
    shape = jax.ShapeDtypeStruct
    far, near = dma((lines - 1, pieces)), dma((pieces,))
    hops = dma((3, 4)) if wide == 8 else dma((1, 4))
    every = dma((4, 4)) if wide == 8 else dma((wide, 4))
    return pl.pallas_call(
        functools.partial(front_kernel, dp, wide, rank_rows),
        out_shape=[
            shape((dp, 3, rows, columns), BF),
            shape((dp,) + wout.shape, BF),
            shape((dp,) + small.shape, BF),
            shape((wide, count, depth), BF),
            shape((wide, count, depth), BF),
            shape((wide,) + tag.shape, BF),
            shape((span, channels), BF),
            shape((span, channels), BF),
            shape((span, channels), BF),
            shape((rank, span), BF),
        ],
        in_specs=[anywhere] * 2 + [vmem] * 7,
        out_specs=[anywhere] * 6 + [vmem] * 4,
        scratch_shapes=[
            pltpu.VMEM(win.shape, F32),
            pltpu.VMEM(wout.shape, F32),
            pltpu.VMEM(wout.shape, BF),
            pltpu.VMEM((dp, 3, rows, columns), BF),
            pltpu.VMEM((dp,) + small.shape, BF),
            pltpu.VMEM((wide, count, depth), BF),
            pltpu.VMEM((wide,) + tag.shape, BF),
            pltpu.VMEM((cuts, span, narrow), BF),
            pltpu.VMEM((2, cuts // 2, span, narrow), BF),
            pltpu.VMEM((rank, span), F32),
            pltpu.VMEM((rank, span), BF),
            pltpu.VMEM((wide, rank, count), BF),
            pltpu.VMEM((rank, count), BF),
            far, far, near, near, far, far,
            dma((cuts,)), dma((2, cuts // 2)), dma((cuts,)), dma((cuts + 1,)), dma((6,)),
            dma((wide,)), dma((wide,)), dma((wide,)), dma((wide,)),
            hops, hops, hops, hops, every, every,
        ],
        compiler_params=pltpu.CompilerParams(
            collective_id=collective_id, has_side_effects=True, vmem_limit_bytes=60 << 20
        ),
        name="front",
    )(win, wout, small, normed, back, tag, masks, taps, bias)


def sum_wide_kernel(wide, x_ref, out_ref, got, whole, s1, r1, s2, r2):
    me, place = lax.axis_index("dp"), lax.axis_index("wide")
    step = out_ref.shape[1] // wide
    barrier = pltpu.get_barrier_semaphore()
    peers = [lax.rem(place + k, wide) for k in range(1, wide)]
    for peer in peers:
        pl.semaphore_signal(barrier, inc=1, device_id=(me, peer), device_id_type=MESH)
    pl.semaphore_wait(barrier, wide - 1)

    def columns(index):
        return pl.ds(pl.multiple_of(index * step, step), step)

    def give(k):
        return pltpu.make_async_remote_copy(
            src_ref=x_ref.at[:, columns(peers[k - 1])],
            dst_ref=got.at[k],
            send_sem=s1.at[k],
            recv_sem=r1.at[k],
            device_id=(me, peers[k - 1]),
            device_id_type=MESH,
        )

    def spread(k):
        return pltpu.make_async_remote_copy(
            src_ref=whole,
            dst_ref=out_ref.at[:, columns(place)],
            send_sem=s2.at[k],
            recv_sem=r2.at[k],
            device_id=(me, peers[k - 1]),
            device_id_type=MESH,
        )

    order = sorted(range(1, wide), key=lambda k: -min(k, wide - k))
    for k in order:
        give(k).start()
    total = x_ref[:, columns(place)].astype(F32)
    for k in reversed(order):
        give(k).wait_recv()
        total = total + got[k].astype(F32)
    whole[...] = total.astype(BF)
    for k in order:
        spread(k).start()
    out_ref[:, columns(place)] = whole[...]
    for k in range(1, wide):
        spread(k).wait()
        give(k).wait_send()


def sum_wide(x, collective_id):
    wide = lax.axis_size("wide")
    rows, span = x.shape
    vmem = pl.BlockSpec(memory_space=pltpu.VMEM)
    dma = pltpu.SemaphoreType.DMA
    return pl.pallas_call(
        functools.partial(sum_wide_kernel, wide),
        out_shape=jax.ShapeDtypeStruct((rows, span), BF),
        in_specs=[vmem],
        out_specs=vmem,
        scratch_shapes=[
            pltpu.VMEM((wide, rows, span // wide), x.dtype),
            pltpu.VMEM((rows, span // wide), BF),
            dma((wide,)),
            dma((wide,)),
            dma((wide,)),
            dma((wide,)),
        ],
        compiler_params=pltpu.CompilerParams(
            collective_id=collective_id, has_side_effects=True, vmem_limit_bytes=32 << 20
        ),
        name="sum_wide",
    )(x)

def finish_kernel(dp, wide, part_ref, table_ref, small_ref, rows_ref, tables_ref, sums_ref, *refs):
    flow_a, flow_b, got_tables, got_small = refs[:4]
    a_send, a_recv, b_send, b_recv, t_send, t_recv, s_send, s_recv, w_send, w_recv = refs[4:]
    me, place = lax.axis_index("dp"), lax.axis_index("wide")
    position = ring_position(place, wide)
    after = (me, ring_index(lax.rem(position + 1, wide), wide))
    before = (me, ring_index(lax.rem(position + wide - 1, wide), wide))
    mates = [lax.rem(me + k, dp) for k in range(1, dp)]
    peers = [lax.rem(place + k, wide) for k in range(1, wide)]
    barrier = pltpu.get_barrier_semaphore()
    for mate in mates:
        pl.semaphore_signal(barrier, inc=1, device_id=(mate, place), device_id_type=MESH)
    for peer in peers:
        pl.semaphore_signal(barrier, inc=1, device_id=(me, peer), device_id_type=MESH)
    pl.semaphore_wait(barrier, dp + wide - 2)

    def remote(source, target, send, recv, device):
        return pltpu.make_async_remote_copy(
            src_ref=source, dst_ref=target, send_sem=send, recv_sem=recv, device_id=device, device_id_type=MESH
        )

    half = part_ref.shape[2] // 2
    cut = half // CUTS

    def columns(side, i):
        return pl.ds(side * half + i * cut, cut)

    def owner(side, hop):
        step = position + wide - 1 - hop if side == 0 else position + 1 + hop
        return ring_index(lax.rem(step, wide), wide)

    flows = ((flow_a, a_send, a_recv, after), (flow_b, b_send, b_recv, before))

    def turn(side, hop, i):
        flow, send, recv, device = flows[side]
        if hop == 0:
            source = part_ref.at[owner(side, 0), :, columns(side, i)]
        else:
            source = flow.at[hop - 1, i]
        return remote(source, flow.at[hop, i], send.at[hop, i], recv.at[hop, i], device)

    for i in range(CUTS):
        for side in range(2):
            turn(side, 0, i).start()

    def lend_table(k):
        return remote(table_ref, got_tables.at[k], t_send.at[k], t_recv.at[k], (mates[k], place))

    def lend_small(k):
        return remote(small_ref.at[mates[k]], got_small.at[k], s_send.at[k], s_recv.at[k], (mates[k], place))

    def show(k):
        return remote(tables_ref.at[place], tables_ref.at[place], w_send.at[k], w_recv.at[k], (me, peers[k]))

    for k in range(dp - 1):
        lend_table(k).start()
    for k in range(dp - 1):
        lend_small(k).start()

    for hop in range(1, wide):
        for i in range(CUTS):
            for side in range(2):
                turn(side, hop - 1, i).wait_recv()
                flow = flows[side][0]
                own = part_ref[owner(side, hop), :, columns(side, i)].astype(F32)
                total = flow[hop - 1, i].astype(F32) + own
                if hop < wide - 1:
                    flow[hop - 1, i] = total.astype(BF)
                    turn(side, hop, i).start()
                else:
                    rows_ref[:, columns(side, i)] = total
        if hop == 1:
            total = table_ref[...]
            for k in range(dp - 1):
                lend_table(k).wait_recv()
                total = total + got_tables[k]
            tables_ref[place] = total
            for k in range(wide - 1):
                show(k).start()
        if hop == min(3, wide - 1):
            for kind in range(3):
                sums_ref[kind] = small_ref[me, kind].astype(F32)
            for k in range(dp - 1):
                lend_small(k).wait_recv()
                for kind in range(3):
                    sums_ref[kind] += got_small[k, kind].astype(F32)

    for k in range(dp - 1):
        lend_table(k).wait_send()
        lend_small(k).wait_send()
    for k in range(wide - 1):
        show(k).wait()
    for hop in range(wide - 1):
        for i in range(CUTS):
            for side in range(2):
                turn(side, hop, i).wait_send()


def finish(part, table, small, collective_id):
    dp, wide = lax.axis_size("dp"), lax.axis_size("wide")
    rows, depth = part.shape[1:]
    vmem = pl.BlockSpec(memory_space=pltpu.VMEM)
    dma = pltpu.SemaphoreType.DMA
    flow = pltpu.VMEM((wide - 1, CUTS, rows, depth // 2 // CUTS), BF)
    hops = dma((wide - 1, CUTS))
    return pl.pallas_call(
        functools.partial(finish_kernel, dp, wide),
        out_shape=[
            jax.ShapeDtypeStruct((rows, depth), F32),
            jax.ShapeDtypeStruct((wide,) + table.shape, F32),
            jax.ShapeDtypeStruct(small.shape[1:], F32),
        ],
        in_specs=[vmem] * 3,
        out_specs=[vmem] * 3,
        scratch_shapes=[
            flow,
            flow,
            pltpu.VMEM((dp - 1,) + table.shape, F32),
            pltpu.VMEM((dp - 1,) + small.shape[1:], small.dtype),
            hops,
            hops,
            hops,
            hops,
            dma((dp - 1,)),
            dma((dp - 1,)),
            dma((dp - 1,)),
            dma((dp - 1,)),
            dma((wide - 1,)),
            dma((wide - 1,)),
        ],
        compiler_params=pltpu.CompilerParams(
            collective_id=collective_id, has_side_effects=True, vmem_limit_bytes=56 << 20
        ),
        name="finish",
    )(part, table, small)


def gate_kernel(back_ref, gated_ref, tag_ref, w_ref, branch_ref, dgated_ref, grad_ref, chosen):
    dp, kinds, rows, channels = w_ref.shape
    span = gated_ref.shape[0]
    blocks = TILE // tag_ref.shape[1]

    def tile(t, carry):
        at = pl.ds(pl.multiple_of(t * TILE, TILE), TILE)
        tag = tag_ref[pl.ds(t * blocks, blocks)].reshape(TILE, -1)[:, :1].astype(F32)
        gated = gated_ref[at].astype(F32)
        for kind in range(3):
            chosen[kind, at] = jnp.where(tag == kind, gated, 0.0).astype(BF)
        for owner in range(dp):
            branch = jnp.zeros((TILE, rows), F32)
            for kind in range(3):
                branch += lax.dot_general(
                    chosen[kind, at], w_ref[owner, kind], (((1,), (1,)), ((), ())), preferred_element_type=F32
                )
            branch_ref[at, owner * rows : (owner + 1) * rows] = branch.astype(BF)
        total = jnp.zeros((TILE, channels), F32)
        for kind in range(3):
            product = jnp.zeros((TILE, channels), F32)
            for owner in range(dp):
                product += jnp.dot(
                    back_ref[at, owner * rows : (owner + 1) * rows], w_ref[owner, kind], preferred_element_type=F32
                )
            total = total + jnp.where(tag == kind, product, 0.0)
        dgated_ref[at] = total.astype(BF)
        return carry

    lax.fori_loop(0, span // TILE, tile, 0)

    def grad(owner, carry):
        columns = pl.ds(pl.multiple_of(owner * rows, rows), rows)
        for kind in range(3):
            grad_ref[owner, kind] = lax.dot_general(
                back_ref[:, columns], chosen[kind], (((0,), (0,)), ((), ())), preferred_element_type=F32
            ).astype(BF)
        return carry

    lax.fori_loop(0, dp, grad, 0)


def gate(back, gated, tags, w_out):
    span, channels = gated.shape
    dp, kinds, rows, _ = w_out.shape
    vmem = pl.BlockSpec(memory_space=pltpu.VMEM)
    flops = 6 * 3 * span * channels * back.shape[1]
    return pl.pallas_call(
        gate_kernel,
        out_shape=[
            jax.ShapeDtypeStruct(back.shape, BF),
            jax.ShapeDtypeStruct(gated.shape, BF),
            jax.ShapeDtypeStruct(w_out.shape, BF),
        ],
        in_specs=[vmem] * 4,
        out_specs=[vmem] * 3,
        scratch_shapes=[pltpu.VMEM((3, span, channels), BF)],
        compiler_params=pltpu.CompilerParams(vmem_limit_bytes=58 << 20),
        cost_estimate=pl.CostEstimate(flops=flops, bytes_accessed=24 << 20, transcendentals=0),
        name="gate",
    )(back, gated, tags, w_out)


def contract(left, right, left_dim, right_dim):
    return lax.dot_general(
        left, right, (((left_dim,), (right_dim,)), ((), ())), preferred_element_type=F32
    )


def segment_of(places, bounds):
    return jnp.sum((places[:, None] >= bounds[None, :]).astype(jnp.int32), axis=1)


def conv_masks(places, bounds, width):
    segment = segment_of(places, bounds)
    return [
        ((places >= offset) & (segment_of(places - offset, bounds) == segment)).astype(F32)
        for offset in range(width)
    ]


def silu_slope(values):
    sigma = jax.nn.sigmoid(values)
    return sigma * (1.0 + values * (1.0 - sigma))


def split_kinds(rows, kinds, parts):
    count, depth = rows.shape
    pieces = rows.reshape(count, parts, 1, depth // parts)
    picked = kinds[:, None, :, None]
    return jnp.where(picked, pieces, jnp.zeros((), rows.dtype)).reshape(count, 3 * depth)


def scatter_master(grad):
    return jnp.transpose(lax.psum_scatter(grad, "dp", scatter_dimension=0), (1, 0, 2))


def hop(block, flip):
    devices = lax.axis_size("dp")
    return lax.ppermute(block, "dp", [(d, flip(d)) for d in range(devices)])


def from_partners(block):
    lines = lax.axis_size("dp") // 2
    blocks = [block, hop(block, lambda d: d ^ 1)]
    for k in range(1, lines):
        far = hop(block, lambda d: (d // 2 + k) % lines * 2 + d % 2)
        blocks += [far, hop(far, lambda d: d ^ 1)]
    return blocks


def swap_features(rows):
    devices = lax.axis_size("dp")
    lines = devices // 2
    depth = rows.shape[1] // devices
    me = lax.axis_index("dp")

    def part(owner):
        return lax.dynamic_slice_in_dim(rows, owner * depth, depth, 1)

    core = me % 2
    blocks = [part(me), hop(part(me + 1 - 2 * core), lambda d: d ^ 1)]
    for k in range(1, lines):
        line = (me // 2 + k) % lines
        blocks.append(hop(part(line * 2 + core), lambda d: (d // 2 + k) % lines * 2 + d % 2))
        blocks.append(
            hop(part(line * 2 + 1 - core), lambda d: (d // 2 + k) % lines * 2 + 1 - d % 2)
        )
    return blocks


def halves_back(xs, z, wide):
    half = wide // 2
    low = lax.axis_index("wide") < half
    even = [(2 * v, v) if v < half else (2 * (v - half) + 1, v) for v in range(wide)]
    odd = [(2 * v + 1, v) if v < half else (2 * (v - half), v) for v in range(wide)]
    is_even = lax.axis_index("wide") % 2 == 0
    got_a = lax.ppermute(jnp.where(is_even, xs, z), "wide", even)
    got_b = lax.ppermute(jnp.where(is_even, z, xs), "wide", odd)
    return jnp.concatenate([jnp.where(low, got_a, got_b), jnp.where(low, got_b, got_a)], axis=1)


def body(
    x_in,
    lengths,
    modality,
    norm_gain,
    conv_weight,
    conv_bias,
    a_log,
    d_skip,
    in_master,
    xproj_master,
    dtproj_master,
    dt_bias,
    out_master,
    cotangent,
):
    wide, dp = lax.axis_size("wide"), lax.axis_size("dp")
    place = lax.axis_index("wide")
    count = x_in.shape[0]
    span = count * wide
    channels = INNER // wide
    width = conv_weight.shape[0]
    own = lambda table: lax.dynamic_slice_in_dim(table, place * channels, channels, table.ndim - 1)

    bounds = jnp.cumsum(lengths.reshape(-1))
    places = jnp.arange(span, dtype=jnp.int32)
    living = places < bounds[-1]
    masks = conv_masks(places, bounds, width)
    later = conv_masks(jnp.arange(span + width - 1, dtype=jnp.int32), bounds, width)
    alive_here = (place * count + jnp.arange(count, dtype=jnp.int32)) < bounds[-1]

    scale = lax.rsqrt(jnp.mean(x_in * x_in, axis=1, keepdims=True) + EPSILON)
    normed = (x_in * scale * norm_gain[None, :]).astype(BF)
    d_branch = jnp.where(alive_here[:, None], cotangent, 0.0).astype(BF)
    rank_rows, step_rows = xproj_master.shape[0], dtproj_master.shape[0]
    small = jnp.concatenate([xproj_master, dtproj_master], axis=0)
    small = jnp.pad(small, ((0, -small.shape[0] % 16), (0, 0), (0, 0)))
    tag = jnp.where(alive_here, modality, 3).astype(BF)
    w_in, w_out, w_small, normed_all, d_branch_all, tags_all, xs, z, inner, proj = front(
        jnp.transpose(in_master, (1, 0, 2)),
        jnp.transpose(out_master, (1, 0, 2)),
        jnp.transpose(small, (1, 0, 2)),
        normed,
        d_branch,
        jnp.broadcast_to(tag[:, None], (count, 128)),
        jnp.stack(masks, axis=1),
        own(conv_weight),
        own(conv_bias)[None, :],
        rank_rows,
        0,
    )
    w_in = w_in.reshape(-1, in_master.shape[2])
    normed_all = normed_all.reshape(span, -1)
    kinds_all = tags_all[:, :, 0].reshape(span)
    w_x_kinds = w_small[:, :, :rank_rows].transpose(1, 0, 2, 3).reshape(3, -1, channels)
    w_dt_kinds = w_small[:, :, rank_rows : rank_rows + step_rows].transpose(1, 0, 2, 3)
    w_dt_kinds = w_dt_kinds.reshape(3, DT_RANK, channels)
    kinds = kinds_all[:, None] == jnp.arange(3, dtype=BF)[None, :]

    kinds_parts = from_partners(kinds_all[:, None])
    features = swap_features(normed_all)

    taps = own(conv_weight)
    xs_value = xs.astype(F32)
    extended = jnp.concatenate([jnp.zeros((width - 1, channels), F32), xs_value], axis=0)
    pre = own(conv_bias)[None, :]
    for offset in range(width):
        begin = width - 1 - offset
        pre = (
            pre + taps[begin][None, :] * extended[begin : begin + span] * masks[offset][:, None]
        )

    rank = w_x_kinds.shape[1]
    across = kinds.T[:, None, :]
    rates = proj[:DT_RANK].T
    maps = proj[DT_RANK:].astype(F32)
    rates_kinds = split_kinds(rates, kinds, 1)
    bias = jnp.where(kinds[:, :, None], dt_bias.astype(BF).astype(F32)[None], 0.0).sum(axis=1)
    dtp = (contract(rates_kinds, w_dt_kinds.reshape(3 * DT_RANK, channels), 1, 0) + bias).astype(BF)

    blocks = span // STEPS
    to_columns = lambda rows: rows.reshape(-1, blocks, STEPS).transpose(1, 0, 2)
    b_columns = to_columns(maps[:STATE])
    c_columns = to_columns(maps[STATE:])
    keep = masks[1][:, None]
    a_own = own(a_log)
    skip_own = own(d_skip)[None, :]
    gated, y_value, heads = scan_forward(dtp, inner, b_columns, c_columns, keep, a_own, skip_own, z)

    branch, d_gated, grad_out = gate(d_branch_all.reshape(span, -1), gated, tags_all, w_out)
    branch = lax.psum_scatter(branch, "wide", scatter_dimension=0, tiled=True)
    result = x_in + branch.astype(F32)
    out_grad = scatter_master(grad_out).astype(F32)

    d_dtp, d_scan, d_z, d_columns, alog_part, skip_part = scan_backward(
        dtp, inner, b_columns, c_columns, keep, a_own, skip_own, z, y_value, d_gated, heads
    )
    d_dtp = jnp.where(living[:, None], d_dtp, jnp.zeros((), BF))
    d_dtp, features, kinds_parts = lax.optimization_barrier((d_dtp, features, kinds_parts))
    feature_kinds = [
        split_kinds(rows, tags == jnp.arange(3, dtype=BF)[None, :], 1)
        for rows, tags in zip(features, kinds_parts)
    ]
    d_maps = d_columns.reshape(-1, 2, d_columns.shape[2] // STATE, STATE)
    d_maps = d_maps.transpose(1, 3, 0, 2).reshape(2 * STATE, span)
    by_kind = contract(w_dt_kinds.reshape(3 * DT_RANK, channels), d_dtp, 1, 1)
    d_rates = jnp.sum(jnp.where(across, by_kind.reshape(3, DT_RANK, span), 0.0), axis=0)
    d_proj = sum_wide(jnp.concatenate([d_rates, d_maps], axis=0).astype(BF), 2)
    d_proj = jnp.where(living[None], d_proj, jnp.zeros((), BF)).T
    grad_dt = contract(rates_kinds, d_dtp, 0, 0).reshape(3, dp, step_rows, channels)
    bias_part = jnp.stack(
        [jnp.sum(jnp.where(kinds[:, k : k + 1], d_dtp.astype(F32), 0.0), axis=0) for k in range(3)]
    )
    d_proj_kinds = split_kinds(d_proj, kinds, 1)
    d_inner = contract(d_proj_kinds, w_x_kinds.reshape(3 * rank, channels), 1, 0).astype(BF)
    grad_x = contract(d_proj_kinds, inner, 0, 0)
    grad_x = grad_x.reshape(3, dp, rank_rows, channels)

    d_pre = (d_inner.astype(F32) + d_scan) * silu_slope(pre)
    further = jnp.concatenate([d_pre, jnp.zeros((width - 1, channels), F32)], axis=0)
    conv_rows = []
    d_xs = jnp.zeros_like(xs_value)
    for offset in range(width):
        begin = width - 1 - offset
        conv_rows.append(
            jnp.sum(d_pre * masks[offset][:, None] * extended[begin : begin + span], axis=0)
        )
        masked = further * later[offset][:, None]
        d_xs = d_xs + taps[begin][None, :] * masked[offset : offset + span]
    conv_part = jnp.stack(conv_rows[::-1], axis=0)
    conv_bias_part = jnp.sum(d_pre, axis=0)
    d_xs = jnp.where(living[:, None], d_xs, 0.0).astype(BF)
    d_z = jnp.where(living[:, None], d_z, jnp.zeros((), BF))
    d_mixed = halves_back(d_xs, d_z, wide)
    mixed_parts = from_partners(d_mixed)
    grad_in = 0.0
    for pair in range(0, dp, 2):
        left = jnp.concatenate(feature_kinds[pair : pair + 2], axis=0)
        grad_in = grad_in + contract(left, jnp.concatenate(mixed_parts[pair : pair + 2], axis=0), 0, 0)
    in_grad = jnp.transpose(grad_in.reshape(3, -1, d_mixed.shape[1]), (1, 0, 2))

    d_normed = jnp.zeros((span, x_in.shape[1]), F32)
    w_in_kinds = w_in.reshape(dp, 3, -1, w_in.shape[1])
    for kind in range(3):
        picked = jnp.where(kinds[:, kind : kind + 1], d_mixed, jnp.zeros((), BF))
        d_normed = d_normed + contract(
            picked, w_in_kinds[:, kind].reshape(-1, w_in.shape[1]), 1, 1
        )
    d_normed = d_normed.astype(BF)
    gain_part = jnp.sum(d_normed.astype(F32) * normed_all.astype(F32), axis=0) / norm_gain
    table = [conv_part, conv_bias_part[None], alog_part, skip_part, bias_part]
    table.append(gain_part.reshape(-1, channels))
    table = jnp.concatenate(table, axis=0)
    kept = table.shape[0]
    table = jnp.pad(table, ((0, -kept % 8), (0, 0)))
    small = jnp.concatenate([grad_x, grad_dt], axis=2).transpose(1, 0, 2, 3)
    small = jnp.pad(small, ((0, 0), (0, 0), (0, -small.shape[2] % 16), (0, 0))).astype(BF)
    d_normed, tables, small = finish(d_normed.reshape(wide, count, -1), table, small, 3)
    xproj_grad = jnp.transpose(small[:, :rank_rows], (1, 0, 2))
    dtproj_grad = jnp.transpose(small[:, rank_rows : rank_rows + step_rows], (1, 0, 2))
    d_normed = d_normed.astype(BF).astype(F32)
    scaled_back = d_normed * norm_gain[None, :]
    x_grad = cotangent + scale * (
        scaled_back - x_in * scale * scale * jnp.mean(scaled_back * x_in, axis=1, keepdims=True)
    )

    edge = width + 1 + STATE + 1
    shared = tables[:, :edge].transpose(1, 0, 2).reshape(edge, INNER)
    bias_grad = lax.dynamic_index_in_dim(tables, place, 0, False)[edge : edge + 3]
    gain_grad = jnp.sum(tables[:, edge + 3 : kept], axis=0).reshape(-1)
    return (
        result,
        x_grad,
        gain_grad,
        shared[:width],
        shared[width],
        shared[width + 1 : width + 1 + STATE],
        shared[width + 1 + STATE],
        in_grad,
        xproj_grad,
        dtproj_grad,
        bias_grad,
        out_grad,
    )


def solution(mesh):
    in_specs = (
        P(("dp", "wide"), None),
        P("dp", None),
        P(("dp", "wide")),
        P(),
        P(),
        P(),
        P(),
        P(),
        P("dp", None, "wide"),
        P("dp", None, "wide"),
        P("dp", None, "wide"),
        P(None, "wide"),
        P("dp", None, "wide"),
        P(("dp", "wide"), None),
    )
    out_specs = (
        P(("dp", "wide"), None),
        P(("dp", "wide"), None),
        P(),
        P(),
        P(),
        P(),
        P(),
        P("dp", None, "wide"),
        P("dp", None, "wide"),
        P("dp", None, "wide"),
        P(None, "wide"),
        P("dp", None, "wide"),
    )
    return jax.shard_map(body, mesh=mesh, in_specs=in_specs, out_specs=out_specs, check_vma=False)
```

```python
import functools

import jax
import jax.numpy as jnp
from jax import lax
from jax.experimental import pallas as pl
from jax.experimental.pallas import tpu as pltpu
from jax.sharding import PartitionSpec as P

F32 = jnp.float32
BF = jnp.bfloat16
INNER = 4096
STATE = 16
DT_RANK = 128
EPSILON = 1e-05


STEPS=32
HUGE=1e30

def own_lanes(channels):
    return pl.ds(pl.multiple_of(lax.axis_index("wide")*channels,channels),channels)

def split_columns(proj_ref,first,cols):
    rows=proj_ref[first:first+cols.shape[1]].astype(F32)
    for k in range(cols.shape[0]):
        cols[k]=rows[:,k*STEPS:(k+1)*STEPS]

def scan_forward_kernel(proj_ref,wdt_ref,dtb_ref,tag_ref,u_ref,masks_ref,alog_ref,skip_ref,z_ref, dtp_ref,gated_ref,y_ref,heads_ref, st, dec, inj, ys, a2, b_ref, c_ref):
    T,C=u_ref.shape
    R=wdt_ref.shape[1]
    S=alog_ref.shape[0]
    @pl.when(pl.program_id(0)==0)
    def _():
        st[...]=jnp.zeros_like(st)
        a2[...]=-jnp.exp(alog_ref[:,own_lanes(C)])*1.4426950408889634
    split_columns(proj_ref,R,b_ref)
    split_columns(proj_ref,R+S,c_ref)
    tag=tag_ref[:,:1].astype(F32)
    rates=proj_ref[:R]
    dtp=jnp.zeros((T,C),F32)
    for kind in range(3):
        step=lax.dot_general(rates,wdt_ref[kind],(((0,),(0,)),((),())),preferred_element_type=F32)
        step=step+dtb_ref[kind:kind+1].astype(BF).astype(F32)
        dtp=dtp+jnp.where(tag==kind,step,0.0)
    dtp=dtp.astype(BF)
    dtp_ref[...]=dtp
    delta=jax.nn.softplus(dtp.astype(F32))
    u=u_ref[...].astype(F32)
    dec[...]=jnp.where(masks_ref[:,1:2]>0,delta,HUGE)
    inj[...]=delta*u
    def chunk(k,state):
        heads_ref[k]=state
        b=b_ref[k]; c=c_ref[k]
        an=a2[...]
        base=pl.multiple_of(k*STEPS,STEPS)
        for j in range(STEPS):
            d=dec[pl.ds(base+j,1),:]
            v=inj[pl.ds(base+j,1),:]
            state=jnp.exp2(d*an)*state+b[:,j:j+1]*v
            ys[pl.ds(base+j,1),:]=jnp.sum(c[:,j:j+1]*state,axis=0,keepdims=True)
        return state
    st[...]=lax.fori_loop(0,T//STEPS,chunk,st[...])
    y=ys[...]+skip_ref[:,own_lanes(C)]*u
    y_ref[...]=y
    z=z_ref[...].astype(F32)
    gated_ref[...]=(y*(z*jax.nn.sigmoid(z))).astype(BF)

def scan_forward(proj,wdt,dtb,tags,u,masks,alog,skip,z,T=128):
    N,C=u.shape
    S=alog.shape[0]
    nk=N//STEPS; tk=T//STEPS
    row=pl.BlockSpec((T,C),lambda i:(i,0))
    whole=lambda s: pl.BlockSpec(s,lambda i:(0,)*len(s))
    tile=lambda lanes: pl.BlockSpec((T,lanes),lambda i:(i,0))
    return pl.pallas_call(scan_forward_kernel,grid=(N//T,),
      in_specs=[pl.BlockSpec((proj.shape[0],T),lambda i:(0,i)),whole(wdt.shape),whole(dtb.shape),tile(tags.shape[1]),row,tile(masks.shape[1]),whole(alog.shape),whole(skip.shape),row],
      out_specs=[row,row,row,pl.BlockSpec((tk,S,C),lambda i:(i,0,0))],
      out_shape=[jax.ShapeDtypeStruct((N,C),BF),jax.ShapeDtypeStruct((N,C),BF),jax.ShapeDtypeStruct((N,C),F32),jax.ShapeDtypeStruct((nk,S,C),F32)],
      scratch_shapes=[pltpu.VMEM((S,C),F32),pltpu.VMEM((T,C),F32),pltpu.VMEM((T,C),F32),pltpu.VMEM((T,C),F32),pltpu.VMEM((S,C),F32),pltpu.VMEM((tk,S,STEPS),F32),pltpu.VMEM((tk,S,STEPS),F32)],
      compiler_params=pltpu.CompilerParams(vmem_limit_bytes=48<<20),
      cost_estimate=pl.CostEstimate(flops=2500*N*C*S,bytes_accessed=16<<20,transcendentals=N*C*S),
      name="scan_forward")(proj,wdt,dtb,tags,u,masks,alog,skip,z)

def fold_lanes(values):
    total=values[:,:128]
    for k in range(128,values.shape[1],128):
        total=total+values[:,k:k+128]
    return total

def sum_lanes(ref):
    values=ref[...].reshape(-1,128)
    high=values.astype(BF)
    rest=(values-high.astype(F32)).astype(BF)
    ones=jnp.ones((8,128),BF)
    dims=(((1,),(1,)),((),()))
    return (lax.dot_general(ones,high,dims,preferred_element_type=F32)+lax.dot_general(ones,rest,dims,preferred_element_type=F32))[:1]

def scan_backward_kernel(dtp_ref,u_ref,proj_ref,masks_ref,alog_ref,skip_ref,z_ref,y_ref,dg_ref,heads_ref,
        ddtp_ref,dus_ref,dz_ref,dm_ref,extra_ref, run, dec, inj, dly, dys, sq, wa, sts, dcs, an2, an1, acc, pb, pc, b_ref, c_ref):
    T,C=u_ref.shape
    S=alog_ref.shape[0]
    first=pl.program_id(0)==0
    last=pl.program_id(0)==pl.num_programs(0)-1
    @pl.when(first)
    def _():
        run[...]=jnp.zeros_like(run)
        acc[...]=jnp.zeros_like(acc)
        extra_ref[...]=jnp.zeros_like(extra_ref)
        an1[...]=-jnp.exp(alog_ref[:,own_lanes(C)])
        an2[...]=an1[...]*1.4426950408889634
    R=proj_ref.shape[0]-2*S
    split_columns(proj_ref,R,b_ref)
    split_columns(proj_ref,R+S,c_ref)
    dtp=dtp_ref[...].astype(F32)
    delta=jax.nn.softplus(dtp)
    u=u_ref[...].astype(F32)
    dec[...]=jnp.where(masks_ref[:,1:2]>0,delta,HUGE)
    dly[...]=delta
    inj[...]=delta*u
    z=z_ref[...].astype(F32)
    sg=jax.nn.sigmoid(z)
    dg=dg_ref[...].astype(F32)
    dy=dg*(z*sg)
    dys[...]=dy
    dz_ref[...]=(dg*y_ref[...]*(sg*(1.0+z*(1.0-sg)))).astype(BF)
    extra_ref[S:S+1]+=jnp.sum(dy*u,axis=0,keepdims=True)
    def chunk(i,running):
        k=T//STEPS-1-i
        b=b_ref[k]; c=c_ref[k]
        base=pl.multiple_of(k*STEPS,STEPS)
        state=heads_ref[k]
        an=an2[...]
        for j in range(STEPS):
            d=dec[pl.ds(base+j,1),:]
            v=inj[pl.ds(base+j,1),:]
            dc=jnp.exp2(d*an)
            sd=dc*state
            state=sd+b[:,j:j+1]*v
            dcs[j]=dc
            sts[j]=sd
        for j in range(STEPS-1,-1,-1):
            g=dys[pl.ds(base+j,1),:]
            v=inj[pl.ds(base+j,1),:]
            bj=b[:,j:j+1]
            ds=c[:,j:j+1]*g+running
            sd=sts[j]
            w=ds*sd
            sq[pl.ds(base+j,1),:]=jnp.sum(ds*bj,axis=0,keepdims=True)
            wa[pl.ds(base+j,1),:]=jnp.sum(w*an1[...],axis=0,keepdims=True)
            acc[...]+=w*dly[pl.ds(base+j,1),:]
            pb[base+j]=fold_lanes(ds*v)
            pc[base+j]=fold_lanes(g*(sd+bj*v))
            running=dcs[j]*ds
        return running
    run[...]=lax.fori_loop(0,T//STEPS,chunk,run[...])
    dm_ref[0,0:1]=sum_lanes(pb)
    dm_ref[0,1:2]=sum_lanes(pc)
    dd=wa[...]+u*sq[...]
    ddtp_ref[...]=(dd*jax.nn.sigmoid(dtp)).astype(BF)
    dus_ref[...]=delta*sq[...]+dy*skip_ref[:,own_lanes(C)]
    @pl.when(last)
    def _():
        extra_ref[:S]=acc[...]*an1[...]

def scan_backward(dtp,u,proj,masks,alog,skip,z,y,dg,heads,T=128):
    N,C=u.shape
    S=alog.shape[0]
    nk=N//STEPS; tk=T//STEPS; nb=N//T
    row=pl.BlockSpec((T,C),lambda i:(nb-1-i,0))
    whole=lambda s: pl.BlockSpec(s,lambda i:(0,0))
    sc=lambda *s: pltpu.VMEM(s,F32)
    return pl.pallas_call(scan_backward_kernel,grid=(nb,),
      in_specs=[row,row,pl.BlockSpec((proj.shape[0],T),lambda i:(0,nb-1-i)),pl.BlockSpec((T,masks.shape[1]),lambda i:(nb-1-i,0)),whole(alog.shape),whole(skip.shape),row,row,row,pl.BlockSpec((tk,S,C),lambda i:(nb-1-i,0,0))],
      out_specs=[row,row,row,pl.BlockSpec((1,2,T*S),lambda i:(nb-1-i,0,0)),whole((S+1,C))],
      out_shape=[jax.ShapeDtypeStruct((N,C),BF),jax.ShapeDtypeStruct((N,C),F32),jax.ShapeDtypeStruct((N,C),BF),jax.ShapeDtypeStruct((nb,2,T*S),F32),jax.ShapeDtypeStruct((S+1,C),F32)],
      scratch_shapes=[sc(S,C),sc(T,C),sc(T,C),sc(T,C),sc(T,C),sc(T,C),sc(T,C),sc(STEPS,S,C),sc(STEPS,S,C),sc(S,C),sc(S,C),sc(S,C),sc(T,S,128),sc(T,S,128),sc(tk,S,STEPS),sc(tk,S,STEPS)],
      compiler_params=pltpu.CompilerParams(vmem_limit_bytes=48<<20),
      cost_estimate=pl.CostEstimate(flops=6000*N*C*S,bytes_accessed=24<<20,transcendentals=N*C*S),
      name="scan_backward")(dtp,u,proj,masks,alog,skip,z,y,dg,heads)


CUTS = 2
MESH = pl.DeviceIdType.MESH
FLIGHT = 6
TILE = 256
SMALL, OUTER = 100, 200


def ring_index(position, wide):
    if wide != 8:
        return position
    turn = position // 4
    return (1 - turn) * 2 * position + turn * (2 * (7 - position) + 1)


def ring_position(index, wide):
    if wide != 8:
        return index
    return index // 2 + index % 2 * (7 - 2 * (index // 2))


def remote(source, target, send, recv, device):
    return pltpu.make_async_remote_copy(
        src_ref=source, dst_ref=target, send_sem=send, recv_sem=recv, device_id=device, device_id_type=MESH
    )


def sum_over_wide(wide, me, place, x_ref, out_ref, got, whole, s1, r1, s2, r2):
    step = out_ref.shape[1] // wide
    peers = [lax.rem(place + k, wide) for k in range(1, wide)]

    def columns(index):
        return pl.ds(pl.multiple_of(index * step, step), step)

    def give(k):
        device = (me, peers[k - 1])
        return remote(x_ref.at[:, columns(peers[k - 1])], got.at[k], s1.at[k], r1.at[k], device)

    def spread(k):
        device = (me, peers[k - 1])
        return remote(whole, out_ref.at[:, columns(place)], s2.at[k], r2.at[k], device)

    order = sorted(range(1, wide), key=lambda k: -min(k, wide - k))
    for k in order:
        give(k).start()
    total = x_ref[:, columns(place)].astype(F32)
    for k in reversed(order):
        give(k).wait_recv()
        total = total + got[k].astype(F32)
    whole[...] = total.astype(BF)
    for k in order:
        spread(k).start()
    out_ref[:, columns(place)] = whole[...]
    for k in range(1, wide):
        spread(k).wait()
        give(k).wait_send()


class Spread:
    def __init__(self, wide, me, place, arrays, sems):
        self.wide, self.me, self.place, self.arrays = wide, me, place, arrays
        self.up_send, self.up_recv, self.down_send, self.down_recv, self.all_send, self.all_recv = sems
        self.z, self.y = place // 2, place % 2

    def copy(self, i, owner, source, send, recv, target):
        ref = self.arrays[i][0] if source else self.arrays[i][1].at[owner]
        return remote(ref, self.arrays[i][1].at[owner], send, recv, (self.me, target))

    def up(self, i, hop):
        owner = (self.z - hop) * 2 + self.y
        return self.copy(i, owner, hop == 0, self.up_send.at[hop, i], self.up_recv.at[hop, i], self.place + 2)

    def down(self, i, hop):
        owner = (self.z + hop) * 2 + self.y
        return self.copy(i, owner, hop == 0, self.down_send.at[hop, i], self.down_recv.at[hop, i], self.place - 2)

    def beside(self, i, z, own=False):
        owner = z * 2 + self.y
        return self.copy(i, owner, own, self.all_send.at[z, i], self.all_recv.at[z, i], self.place + 1 - 2 * self.y)

    def direct(self, i, k):
        target = lax.rem(self.place + k, self.wide)
        return self.copy(i, self.place, True, self.all_send.at[k, i], self.all_recv.at[k, i], target)

    def begin(self, i):
        if self.wide != 8:
            for k in range(1, self.wide):
                self.direct(i, k).start()
            return

        @pl.when(self.z < 3)
        def _():
            self.up(i, 0).start()

        @pl.when(self.z > 0)
        def _():
            self.down(i, 0).start()

        self.beside(i, self.z, True).start()

    def step(self, i, hop):
        if self.wide != 8:
            return

        @pl.when(self.z > hop)
        def _():
            self.up(i, hop).wait_recv()
            if hop < 2:

                @pl.when(self.z < 3)
                def _():
                    self.up(i, hop + 1).start()

            self.beside(i, self.z - 1 - hop).start()

        @pl.when(self.z + hop < 3)
        def _():
            self.down(i, hop).wait_recv()
            if hop < 2:

                @pl.when(self.z > 0)
                def _():
                    self.down(i, hop + 1).start()

            self.beside(i, self.z + 1 + hop).start()

    def end(self, i):
        if self.wide != 8:
            for k in range(1, self.wide):
                self.direct(i, k).wait_recv()
            return
        for z in range(4):
            self.beside(i, z).wait_recv()

    def sent(self):
        for i in range(len(self.arrays)):
            if self.wide != 8:
                for k in range(1, self.wide):
                    self.direct(i, k).wait_send()
                continue
            for hop in range(3):

                @pl.when((self.z >= hop) & (self.z < 3))
                def _():
                    self.up(i, hop).wait_send()

                @pl.when((self.z + hop <= 3) & (self.z > 0))
                def _():
                    self.down(i, hop).wait_send()

            for z in range(4):
                self.beside(i, z).wait_send()


def front_kernel(dp, wide, rank_rows, *refs):
    win_ref, wout_ref, small_ref, x_ref, cot_ref, gain_ref, tag_ref, masks_ref, taps_ref, bias_ref, refs = (
        *refs[:10],
        refs[10:],
    )
    wall_out, wout_out, nall_out, ball_out, tags_out, wx_ref, wdt_ref, xs_out, z_out, u_ref, proj_ref, refs = (
        *refs[:11],
        refs[11:],
    )
    stage, stage_out, wout_low, wall, wsmall, nall, back_ref, tags, mixed, xz, part, part_low, got, whole, tall, refs = (
        *refs[:15],
        refs[15:],
    )
    x_send, x_recv, core_send, core_recv, on_send, on_recv, refs = *refs[:6], refs[6:]
    h_send, h_recv, h_local, load, keep = refs[:5]
    s1, r1, s2, r2 = refs[5:9]
    me, place = lax.axis_index("dp"), lax.axis_index("wide")
    cuts, span, narrow = mixed.shape
    half = wide // 2
    count = x_ref.shape[0]
    rows = win_ref.shape[1]
    lines = dp // 2
    line, core = me // 2, me % 2
    partner = (me + 1 - 2 * core, place)
    across = [(lax.rem(line + k, lines) * 2 + core, place) for k in range(1, lines)]
    barrier = pltpu.get_barrier_semaphore()
    for peer in [partner] + across + [(me, lax.rem(place + k, wide)) for k in range(1, wide)]:
        pl.semaphore_signal(barrier, inc=1, device_id=peer, device_id_type=MESH)
    pl.semaphore_wait(barrier, lines + wide - 1)

    turns = [h * (cuts // 2) + i for i in range(cuts // 2) for h in range(2)]
    pieces = [(q, kind) for q in turns for kind in range(3)]
    pieces += [(SMALL, kind) for kind in range(3)]
    pieces += [(OUTER + h, kind) for kind in range(3) for h in range(2)]
    height = wout_ref.shape[1] // 2

    def slot(j, owner):
        q, kind = pieces[j]
        if q >= OUTER:
            return wout_out.at[owner, kind, pl.ds((q - OUTER) * height, height)]
        if q == SMALL:
            return wsmall.at[owner, kind]
        return wall.at[owner, kind, :, pl.ds(q * narrow, narrow)]

    def mine(j):
        q, kind = pieces[j]
        if q >= OUTER:
            return wout_low.at[kind, pl.ds((q - OUTER) * height, height)]
        return slot(j, me)

    def cross(k, j):
        return remote(mine(j), slot(j, me), x_send.at[k, j], x_recv.at[k, j], across[k])

    def pair(j):
        return remote(mine(j), slot(j, me), core_send.at[j], core_recv.at[j], partner)

    def onward(k, j):
        owner = lax.rem(line + lines - 1 - k, lines) * 2 + core
        return remote(slot(j, owner), slot(j, owner), on_send.at[k, j], on_recv.at[k, j], partner)

    loads = []
    for q in turns:
        part_columns = pl.ds(q * narrow, narrow)
        loads.append(pltpu.make_async_copy(win_ref.at[:, :, part_columns], stage.at[:, :, part_columns], load.at[q]))
        loads[-1].start()
    loads.append(pltpu.make_async_copy(wout_ref, stage_out, load.at[cuts]))
    loads[-1].start()

    x = x_ref[...]
    scale = lax.rsqrt(jnp.mean(x * x, axis=1, keepdims=True) + EPSILON)
    nall[place] = (x * scale * gain_ref[...]).astype(BF)
    tags[place] = tag_ref[...]
    back_ref[...] = jnp.where(tag_ref[:, :1].astype(F32) < 3.0, cot_ref[...], 0.0).astype(BF)
    kept = [pltpu.make_async_copy(back_ref, ball_out.at[place], keep.at[0])]
    kept[-1].start()
    spread = Spread(
        wide,
        me,
        place,
        [
            (nall.at[place, pl.ds(0, count // 2)], nall.at[:, pl.ds(0, count // 2)]),
            (nall.at[place, pl.ds(count // 2, count // 2)], nall.at[:, pl.ds(count // 2, count // 2)]),
            (tags.at[place], tags),
            (back_ref, ball_out),
        ],
        refs[9:],
    )
    for i in range(3):
        spread.begin(i)
    for j, (q, kind) in enumerate(pieces):
        if q >= OUTER:
            if j == 3 * cuts + 3:
                loads[cuts].wait()
            part_rows = pl.ds((q - OUTER) * height, height)
            wout_low[kind, part_rows] = stage_out[kind, part_rows].astype(BF)
        elif q == SMALL:
            wsmall[me, kind] = small_ref[kind].astype(BF)
        else:
            if kind == 0:
                loads[turns.index(q)].wait()
            wall[me, kind, :, q * narrow : (q + 1) * narrow] = stage[
                kind, :, q * narrow : (q + 1) * narrow
            ].astype(BF)
        if j < FLIGHT:
            for k in range(lines - 1):
                cross(k, j).start()
        pair(j).start()

    kept.append(pltpu.make_async_copy(wout_low, wout_out.at[me], keep.at[1]))
    kept[-1].start()
    state = {"passed": 0}

    def pass_on(until):
        for j in range(state["passed"], min(until, len(pieces))):
            for k in range(lines - 1):
                cross(k, j).wait_recv()
                onward(k, j).start()
                if j < 3 * cuts and j + FLIGHT < len(pieces):
                    cross(k, j + FLIGHT).start()
                if j == 3 * cuts - 1:
                    for later in range(j + FLIGHT + 1, len(pieces)):
                        cross(k, later).start()
            state["passed"] = j + 1

    for hop in range(3):
        for i in range(3):
            spread.step(i, hop)
        pass_on(2 * (hop + 1))
    for i in range(3):
        spread.end(i)
    spread.begin(3)

    low = place // half
    home = place % half

    def deliver(q):
        return remote(
            mixed.at[q], xz.at[low, q % (cuts // 2)], h_send.at[q], h_recv.at[low, q % (cuts // 2)],
            (me, 2 * home + q // (cuts // 2)),
        )

    def stay(q):
        return pltpu.make_async_copy(mixed.at[q], xz.at[low, q % (cuts // 2)], h_local.at[q])

    blocks = TILE // count
    for turn, q in enumerate(turns):
        pass_on((turn + 1) * 3)
        for j in range(3 * turn, 3 * turn + 3):
            pair(j).wait_recv()
            for k in range(lines - 1):
                onward(k, j).wait_recv()

        def tile(t, carry, q=q):
            left = nall[pl.ds(t * blocks, blocks)].reshape(TILE, -1)
            tag = tags[pl.ds(t * blocks, blocks)].reshape(TILE, -1)[:, :1].astype(F32)
            total = jnp.zeros((TILE, narrow), F32)
            for kind in range(3):
                product = jnp.zeros((TILE, narrow), F32)
                for owner in range(dp):
                    product += jnp.dot(
                        left[:, owner * rows : (owner + 1) * rows],
                        wall[owner, kind, :, q * narrow : (q + 1) * narrow],
                        preferred_element_type=F32,
                    )
                total = total + jnp.where(tag == kind, product, 0.0)
            mixed[q, pl.ds(pl.multiple_of(t * TILE, TILE), TILE)] = total.astype(BF)
            return carry

        lax.fori_loop(0, span // TILE, tile, 0)
        target = 2 * home + q // (cuts // 2)

        @pl.when(target != place)
        def _(q=q):
            deliver(q).start()

        @pl.when(target == place)
        def _(q=q):
            stay(q).start()

        if turn > 0:
            spread.step(3, turn - 1)
        if turn == 0:
            for source, sink in ((nall, nall_out), (tags, tags_out)):
                kept.append(pltpu.make_async_copy(source, sink, keep.at[len(kept)]))
                kept[-1].start()
    pass_on(3 * cuts + 3)
    kept.append(pltpu.make_async_copy(wall, wall_out, keep.at[len(kept)]))
    kept[-1].start()

    def arrive(kind, i):
        source = kind * half + place // 2
        q = place % 2 * (cuts // 2) + i

        @pl.when(source != place)
        def _():
            remote(mixed.at[0], xz.at[kind, i], h_send.at[0], h_recv.at[kind, i], partner).wait_recv()

        @pl.when(source == place)
        def _():
            pltpu.make_async_copy(mixed.at[q], xz.at[kind, i], h_local.at[q]).wait()

    channels = u_ref.shape[1]
    own = pl.ds(pl.multiple_of(place * channels, channels), channels)
    taps_all, bias_all = taps_ref[:, own], bias_ref[:, own]
    width = taps_all.shape[0]
    for i in range(cuts // 2):
        arrive(0, i)
        taps = taps_all[:, i * narrow : (i + 1) * narrow]
        bias = bias_all[:, i * narrow : (i + 1) * narrow]

        def conv(t, carry, i=i, taps=taps, bias=bias):
            at = pl.multiple_of(t * 128, 128)
            behind = pl.multiple_of(jnp.maximum(t * 128 - 16, 0), 16)
            here = xz[0, i, pl.ds(at, 128)].astype(F32)
            both = jnp.concatenate([xz[0, i, pl.ds(behind, 16)].astype(F32), here], axis=0)
            masks = masks_ref[pl.ds(at, 128)]
            pre = bias + taps[width - 1 : width] * here
            for offset in range(1, width):
                pre = pre + taps[width - 1 - offset : width - offset] * (
                    both[16 - offset : 144 - offset] * masks[:, offset : offset + 1]
                )
            u_ref[pl.ds(at, 128), i * narrow : (i + 1) * narrow] = (pre * jax.nn.sigmoid(pre)).astype(BF)
            return carry

        lax.fori_loop(0, span // 128, conv, 0)

    for j in range(3 * cuts, 3 * cuts + 3):
        pair(j).wait_recv()
        for k in range(lines - 1):
            onward(k, j).wait_recv()

    def project(t, carry):
        at = pl.multiple_of(t * TILE, TILE)
        inner = u_ref[pl.ds(at, TILE)].astype(F32)
        tag = tags[pl.ds(t * blocks, blocks)].reshape(TILE, -1)[:, :1].astype(F32)
        chosen = [jnp.where(tag == kind, inner, 0.0).astype(BF) for kind in range(3)]
        for owner in range(dp):
            total = jnp.zeros((wsmall.shape[2], TILE), F32)
            for kind in range(3):
                total += lax.dot_general(
                    wsmall[owner, kind], chosen[kind], (((1,), (1,)), ((), ())), preferred_element_type=F32
                )
            part[owner * rank_rows : (owner + 1) * rank_rows, pl.ds(at, TILE)] = total[:rank_rows]
        return carry

    pass_on(3 * cuts + 6)
    lax.fori_loop(0, span // TILE, project, 0)
    part_low[...] = part[...].astype(BF)
    sum_over_wide(wide, me, place, part_low, proj_ref, got, whole, s1, r1, s2, r2)

    pass_on(len(pieces))
    for hop in range(cuts - 1, 3):
        spread.step(3, hop)
    spread.end(3)
    step_rows = wdt_ref.shape[1] // dp
    rank = rank_rows * dp
    for kind in range(3):
        for owner in range(dp):
            rows_here = wsmall[owner, kind].astype(F32)
            tall[owner * rank_rows : (owner + 1) * rank_rows] = rows_here[:rank_rows]
            tall[rank + owner * step_rows : rank + (owner + 1) * step_rows] = rows_here[rank_rows : rank_rows + step_rows]
        wx_ref[kind] = tall[:rank].astype(BF)
        wdt_ref[kind] = tall[rank:].astype(BF)
    for i in range(cuts // 2):
        arrive(1, i)
    for i in range(cuts // 2):
        xs_out[:, i * narrow : (i + 1) * narrow] = xz[0, i]
        z_out[:, i * narrow : (i + 1) * narrow] = xz[1, i]
    for j in range(3 * cuts + 3, len(pieces)):
        pair(j).wait_recv()
        for k in range(lines - 1):
            onward(k, j).wait_recv()
    for j in range(len(pieces)):
        pair(j).wait_send()
        for k in range(lines - 1):
            cross(k, j).wait_send()
            onward(k, j).wait_send()
    spread.sent()
    for q in range(cuts):

        @pl.when(2 * home + q // (cuts // 2) != place)
        def _(q=q):
            deliver(q).wait_send()

    for copy in kept:
        copy.wait()


def front(win, wout, small, x, cotangent, gain, tag, masks, taps, bias, rank_rows, step_rows, collective_id):
    dp, wide = lax.axis_size("dp"), lax.axis_size("wide")
    kinds, rows, columns = win.shape
    cuts = 4 if columns >= 512 else 2
    narrow = columns // cuts
    count, depth = x.shape
    span = count * wide
    channels = small.shape[2]
    rank = rank_rows * dp
    lines = dp // 2
    pieces = 3 * cuts + 9
    vmem = pl.BlockSpec(memory_space=pltpu.VMEM)
    anywhere = pl.BlockSpec(memory_space=pl.ANY)
    dma = pltpu.SemaphoreType.DMA
    shape = jax.ShapeDtypeStruct
    far, near = dma((lines - 1, pieces)), dma((pieces,))
    hops = dma((3, 4)) if wide == 8 else dma((1, 4))
    every = dma((4, 4)) if wide == 8 else dma((wide, 4))
    return pl.pallas_call(
        functools.partial(front_kernel, dp, wide, rank_rows),
        out_shape=[
            shape((dp, 3, rows, columns), BF),
            shape((dp,) + wout.shape, BF),
            shape((wide, count, depth), BF),
            shape((wide, count, depth), BF),
            shape((wide,) + tag.shape, BF),
            shape((3, rank, channels), BF),
            shape((3, step_rows * dp, channels), BF),
            shape((span, channels), BF),
            shape((span, channels), BF),
            shape((span, channels), BF),
            shape((rank, span), BF),
        ],
        in_specs=[anywhere] * 2 + [vmem] * 8,
        out_specs=[anywhere] * 5 + [vmem] * 6,
        scratch_shapes=[
            pltpu.VMEM(win.shape, F32),
            pltpu.VMEM(wout.shape, F32),
            pltpu.VMEM(wout.shape, BF),
            pltpu.VMEM((dp, 3, rows, columns), BF),
            pltpu.VMEM((dp,) + small.shape, BF),
            pltpu.VMEM((wide, count, depth), BF),
            pltpu.VMEM((count, depth), BF),
            pltpu.VMEM((wide,) + tag.shape, BF),
            pltpu.VMEM((cuts, span, narrow), BF),
            pltpu.VMEM((2, cuts // 2, span, narrow), BF),
            pltpu.VMEM((rank, span), F32),
            pltpu.VMEM((rank, span), BF),
            pltpu.VMEM((wide, rank, count), BF),
            pltpu.VMEM((rank, count), BF),
            pltpu.VMEM((rank + step_rows * dp, channels), F32),
            far, far, near, near, far, far,
            dma((cuts,)), dma((2, cuts // 2)), dma((cuts,)), dma((cuts + 1,)), dma((6,)),
            dma((wide,)), dma((wide,)), dma((wide,)), dma((wide,)),
            hops, hops, hops, hops, every, every,
        ],
        compiler_params=pltpu.CompilerParams(
            collective_id=collective_id, has_side_effects=True, vmem_limit_bytes=60 << 20
        ),
        name="front",
    )(win, wout, small, x, cotangent, gain, tag, masks, taps, bias)


def sum_wide_kernel(wide, x_ref, out_ref, got, whole, s1, r1, s2, r2):
    me, place = lax.axis_index("dp"), lax.axis_index("wide")
    step = out_ref.shape[1] // wide
    barrier = pltpu.get_barrier_semaphore()
    peers = [lax.rem(place + k, wide) for k in range(1, wide)]
    for peer in peers:
        pl.semaphore_signal(barrier, inc=1, device_id=(me, peer), device_id_type=MESH)
    pl.semaphore_wait(barrier, wide - 1)

    def columns(index):
        return pl.ds(pl.multiple_of(index * step, step), step)

    def give(k):
        return pltpu.make_async_remote_copy(
            src_ref=x_ref.at[:, columns(peers[k - 1])],
            dst_ref=got.at[k],
            send_sem=s1.at[k],
            recv_sem=r1.at[k],
            device_id=(me, peers[k - 1]),
            device_id_type=MESH,
        )

    def spread(k):
        return pltpu.make_async_remote_copy(
            src_ref=whole,
            dst_ref=out_ref.at[:, columns(place)],
            send_sem=s2.at[k],
            recv_sem=r2.at[k],
            device_id=(me, peers[k - 1]),
            device_id_type=MESH,
        )

    order = sorted(range(1, wide), key=lambda k: -min(k, wide - k))
    for k in order:
        give(k).start()
    total = x_ref[:, columns(place)].astype(F32)
    for k in reversed(order):
        give(k).wait_recv()
        total = total + got[k].astype(F32)
    whole[...] = total.astype(BF)
    for k in order:
        spread(k).start()
    out_ref[:, columns(place)] = whole[...]
    for k in range(1, wide):
        spread(k).wait()
        give(k).wait_send()


def sum_wide(x, collective_id):
    wide = lax.axis_size("wide")
    rows, span = x.shape
    vmem = pl.BlockSpec(memory_space=pltpu.VMEM)
    dma = pltpu.SemaphoreType.DMA
    return pl.pallas_call(
        functools.partial(sum_wide_kernel, wide),
        out_shape=jax.ShapeDtypeStruct((rows, span), BF),
        in_specs=[vmem],
        out_specs=vmem,
        scratch_shapes=[
            pltpu.VMEM((wide, rows, span // wide), x.dtype),
            pltpu.VMEM((rows, span // wide), BF),
            dma((wide,)),
            dma((wide,)),
            dma((wide,)),
            dma((wide,)),
        ],
        compiler_params=pltpu.CompilerParams(
            collective_id=collective_id, has_side_effects=True, vmem_limit_bytes=32 << 20
        ),
        name="sum_wide",
    )(x)

def finish_kernel(dp, wide, part_ref, table_ref, small_ref, rows_ref, tables_ref, sums_ref, *refs):
    flow_a, flow_b, got_tables, got_small = refs[:4]
    a_send, a_recv, b_send, b_recv, t_send, t_recv, s_send, s_recv, w_send, w_recv = refs[4:]
    me, place = lax.axis_index("dp"), lax.axis_index("wide")
    position = ring_position(place, wide)
    after = (me, ring_index(lax.rem(position + 1, wide), wide))
    before = (me, ring_index(lax.rem(position + wide - 1, wide), wide))
    mates = [lax.rem(me + k, dp) for k in range(1, dp)]
    peers = [lax.rem(place + k, wide) for k in range(1, wide)]
    barrier = pltpu.get_barrier_semaphore()
    for mate in mates:
        pl.semaphore_signal(barrier, inc=1, device_id=(mate, place), device_id_type=MESH)
    for peer in peers:
        pl.semaphore_signal(barrier, inc=1, device_id=(me, peer), device_id_type=MESH)
    pl.semaphore_wait(barrier, dp + wide - 2)

    def remote(source, target, send, recv, device):
        return pltpu.make_async_remote_copy(
            src_ref=source, dst_ref=target, send_sem=send, recv_sem=recv, device_id=device, device_id_type=MESH
        )

    half = part_ref.shape[2] // 2
    cut = half // CUTS

    def columns(side, i):
        return pl.ds(side * half + i * cut, cut)

    def owner(side, hop):
        step = position + wide - 1 - hop if side == 0 else position + 1 + hop
        return ring_index(lax.rem(step, wide), wide)

    flows = ((flow_a, a_send, a_recv, after), (flow_b, b_send, b_recv, before))

    def turn(side, hop, i):
        flow, send, recv, device = flows[side]
        if hop == 0:
            source = part_ref.at[owner(side, 0), :, columns(side, i)]
        else:
            source = flow.at[hop - 1, i]
        return remote(source, flow.at[hop, i], send.at[hop, i], recv.at[hop, i], device)

    for i in range(CUTS):
        for side in range(2):
            turn(side, 0, i).start()

    def lend_table(k):
        return remote(table_ref, got_tables.at[k], t_send.at[k], t_recv.at[k], (mates[k], place))

    def lend_small(k):
        return remote(small_ref.at[mates[k]], got_small.at[k], s_send.at[k], s_recv.at[k], (mates[k], place))

    def show(k):
        return remote(tables_ref.at[place], tables_ref.at[place], w_send.at[k], w_recv.at[k], (me, peers[k]))

    for k in range(dp - 1):
        lend_table(k).start()
    for k in range(dp - 1):
        lend_small(k).start()

    for hop in range(1, wide):
        for i in range(CUTS):
            for side in range(2):
                turn(side, hop - 1, i).wait_recv()
                flow = flows[side][0]
                own = part_ref[owner(side, hop), :, columns(side, i)].astype(F32)
                total = flow[hop - 1, i].astype(F32) + own
                if hop < wide - 1:
                    flow[hop - 1, i] = total.astype(BF)
                    turn(side, hop, i).start()
                else:
                    rows_ref[:, columns(side, i)] = total
        if hop == 1:
            total = table_ref[...]
            for k in range(dp - 1):
                lend_table(k).wait_recv()
                total = total + got_tables[k]
            tables_ref[place] = total
            for k in range(wide - 1):
                show(k).start()
        if hop == min(3, wide - 1):
            for kind in range(3):
                sums_ref[kind] = small_ref[me, kind].astype(F32)
            for k in range(dp - 1):
                lend_small(k).wait_recv()
                for kind in range(3):
                    sums_ref[kind] += got_small[k, kind].astype(F32)

    for k in range(dp - 1):
        lend_table(k).wait_send()
        lend_small(k).wait_send()
    for k in range(wide - 1):
        show(k).wait()
    for hop in range(wide - 1):
        for i in range(CUTS):
            for side in range(2):
                turn(side, hop, i).wait_send()


def finish(part, table, small, collective_id):
    dp, wide = lax.axis_size("dp"), lax.axis_size("wide")
    rows, depth = part.shape[1:]
    vmem = pl.BlockSpec(memory_space=pltpu.VMEM)
    dma = pltpu.SemaphoreType.DMA
    flow = pltpu.VMEM((wide - 1, CUTS, rows, depth // 2 // CUTS), BF)
    hops = dma((wide - 1, CUTS))
    return pl.pallas_call(
        functools.partial(finish_kernel, dp, wide),
        out_shape=[
            jax.ShapeDtypeStruct((rows, depth), F32),
            jax.ShapeDtypeStruct((wide,) + table.shape, F32),
            jax.ShapeDtypeStruct(small.shape[1:], F32),
        ],
        in_specs=[vmem] * 3,
        out_specs=[vmem] * 3,
        scratch_shapes=[
            flow,
            flow,
            pltpu.VMEM((dp - 1,) + table.shape, F32),
            pltpu.VMEM((dp - 1,) + small.shape[1:], small.dtype),
            hops,
            hops,
            hops,
            hops,
            dma((dp - 1,)),
            dma((dp - 1,)),
            dma((dp - 1,)),
            dma((dp - 1,)),
            dma((wide - 1,)),
            dma((wide - 1,)),
        ],
        compiler_params=pltpu.CompilerParams(
            collective_id=collective_id, has_side_effects=True, vmem_limit_bytes=56 << 20
        ),
        name="finish",
    )(part, table, small)


def back_kernel(dp, wide, rank_rows, step_rows, *refs):
    feat_refs, kind_refs, refs = refs[:dp], refs[dp : 2 * dp], refs[2 * dp :]
    win_ref, normed_ref, ddtp_ref, dscan_ref, dz_ref, xs_ref, u_ref, refs = *refs[:7], refs[7:]
    dmaps_ref, rates_ref, wx_ref, wdt_ref, tags_ref, line_ref, masks_ref, taps_ref, bias_ref, extra_ref, refs = (
        *refs[:10],
        refs[10:],
    )
    ingrad_ref, rows_ref, tables_ref, sums_ref, refs = *refs[:4], refs[4:]
    wall, feats, nbuf, part, got, whole, dproj, dpre, leave, gm, dn, refs = *refs[:11], refs[11:]
    first, flow_a, flow_b, stage, table, got_tables, dt_grad, small, got_small, refs = *refs[:9], refs[9:]
    s1, r1, s2, r2, load, nload, d_send, d_recv, d_local, refs = *refs[:9], refs[9:]
    x_send, x_recv, core_send, core_recv, on_send, on_recv, o_send, refs = *refs[:7], refs[7:]
    a_send, a_recv, b_send, b_recv, t_send, t_recv, l_send, l_recv, w_send, w_recv = refs
    me, place = lax.axis_index("dp"), lax.axis_index("wide")
    _, cuts, span, narrow = gm.shape
    channels = xs_ref.shape[1]
    rows = win_ref.shape[2]
    count, depth = rows_ref.shape
    half = wide // 2
    quarters = cuts // 2
    low, home = place // half, place % half
    lines = dp // 2
    line, core = me // 2, me % 2
    partner = (me + 1 - 2 * core, place)
    across = [(lax.rem(line + k, lines) * 2 + core, place) for k in range(1, lines)]
    mates = [lax.rem(me + k, dp) for k in range(1, dp)]
    peers = [lax.rem(place + k, wide) for k in range(1, wide)]
    position = ring_position(place, wide)
    after = (me, ring_index(lax.rem(position + 1, wide), wide))
    before = (me, ring_index(lax.rem(position + wide - 1, wide), wide))
    barrier = pltpu.get_barrier_semaphore()
    for peer in [(mate, place) for mate in mates] + [(me, peer) for peer in peers]:
        pl.semaphore_signal(barrier, inc=1, device_id=peer, device_id_type=MESH)
    pl.semaphore_wait(barrier, dp + wide - 2)

    loads = [pltpu.make_async_copy(win_ref, wall, load.at[dp])]
    for k in range(dp):
        loads.append(pltpu.make_async_copy(feat_refs[k], feats.at[k], load.at[k]))
    for copy in loads:
        copy.start()

    def slot(i):
        return place % 2 * quarters + i

    def source(kind, i):
        if kind == 0:
            return leave.at[i]
        return dz_ref.at[:, pl.ds(i * narrow, narrow)]

    def deliver(kind, i):
        target = (me, kind * half + place // 2)
        return remote(source(kind, i), gm.at[me, slot(i)], d_send.at[kind, i], d_recv.at[slot(i)], target)

    def stay(kind, i):
        return pltpu.make_async_copy(source(kind, i), gm.at[me, slot(i)], d_local.at[i])

    def hand_over(kind, i):
        @pl.when(kind * half + place // 2 != place)
        def _():
            deliver(kind, i).start()

        @pl.when(kind * half + place // 2 == place)
        def _():
            stay(kind, i).start()

    def arrive(q):
        sender = 2 * home + q // quarters

        @pl.when(sender != place)
        def _():
            remote(leave.at[0], gm.at[me, q], d_send.at[0, 0], d_recv.at[q], partner).wait_recv()

        @pl.when(sender == place)
        def _():
            pltpu.make_async_copy(leave.at[0], gm.at[me, q], d_local.at[q % quarters]).wait()

    blocks = TILE // count
    steps = wdt_ref.shape[1]

    def columns(index):
        return pl.ds(pl.multiple_of(index * count, count), count)

    def give(k):
        device = (me, peers[k - 1])
        return remote(part.at[:, columns(peers[k - 1])], got.at[k], s1.at[k], r1.at[k], device)

    def share(k):
        device = (me, peers[k - 1])
        return remote(whole, dproj.at[:, columns(place)], s2.at[k], r2.at[k], device)

    def rates_back(t, carry):
        at = pl.ds(pl.multiple_of(t * TILE, TILE), TILE)
        tag = tags_ref[pl.ds(t * blocks, blocks)].reshape(TILE, -1)[:, :1].astype(F32)
        value = ddtp_ref[at].astype(F32)
        total = jnp.zeros((steps, TILE), F32)
        for kind in range(3):
            total += lax.dot_general(
                wdt_ref[kind],
                jnp.where(tag == kind, value, 0.0).astype(BF),
                (((1,), (1,)), ((), ())),
                preferred_element_type=F32,
            )
        part[:steps, at] = total.astype(BF)
        return carry

    lax.fori_loop(0, span // TILE, rates_back, 0)
    part[steps:] = dmaps_ref[...].astype(BF)
    order = sorted(range(1, wide), key=lambda k: -min(k, wide - k))
    for k in order:
        give(k).start()
    dn[...] = jnp.zeros_like(dn)
    dpre[span:] = jnp.zeros_like(dpre[span:])
    width = taps_ref.shape[0]
    states = extra_ref.shape[0] - 1
    table[...] = jnp.zeros_like(table)
    table[width + 1 : width + 2 + states] = extra_ref[...]
    dead = line_ref[0:1].astype(F32)
    for kind in range(3):
        chosen_rates = jnp.where(dead == kind, rates_ref[:steps].astype(F32), 0.0).astype(BF)
        grad = jnp.dot(chosen_rates, ddtp_ref[...], preferred_element_type=F32)
        dt_grad[kind] = grad
        picked = jnp.where(line_ref[...].astype(F32) == kind, 1.0, 0.0).astype(BF)
        at = width + 2 + states + kind
        table[at : at + 1] = jnp.dot(picked, ddtp_ref[...], preferred_element_type=F32)[:1]
    total = part[:, columns(place)].astype(F32)
    for k in reversed(order):
        give(k).wait_recv()
        total = total + got[k].astype(F32)
    whole[...] = total.astype(BF)
    for k in order:
        share(k).start()
    dproj[:, columns(place)] = whole[...]
    for k in range(1, wide):
        share(k).wait_recv()
    for i in range(quarters):
        hand_over(1, i)

    own = pl.ds(pl.multiple_of(place * channels, channels), channels)
    taps_all, conv_bias = taps_ref[:, own], bias_ref[:, own]

    def through(t, carry):
        at = pl.multiple_of(t * 128, 128)
        behind = pl.multiple_of(jnp.maximum(t * 128 - 16, 0), 16)
        tag = tags_ref[pl.ds(t * 128 // count, 128 // count)].reshape(128, -1)[:, :1].astype(F32)
        piece = dproj[:, pl.ds(at, 128)]
        du = jnp.zeros((128, channels), F32)
        for kind in range(3):
            product = lax.dot_general(
                piece, wx_ref[kind], (((0,), (0,)), ((), ())), preferred_element_type=F32
            )
            du = du + jnp.where(tag == kind, product, 0.0)
        du = du.astype(BF).astype(F32) + dscan_ref[pl.ds(at, 128)]
        here = xs_ref[pl.ds(at, 128)].astype(F32)
        both = jnp.concatenate([xs_ref[pl.ds(behind, 16)].astype(F32), here], axis=0)
        masks = masks_ref[pl.ds(at, 128)]
        terms = [here] + [both[16 - k : 144 - k] * masks[:, k : k + 1] for k in range(1, width)]
        pre = conv_bias
        for k in range(width):
            pre = pre + taps_all[width - 1 - k : width - k] * terms[k]
        sigma = jax.nn.sigmoid(pre)
        slope = du * (sigma * (1.0 + pre * (1.0 - sigma)))
        dpre[pl.ds(at, 128)] = slope
        for k in range(width):
            table[width - 1 - k : width - k] += jnp.sum(slope * terms[k], axis=0, keepdims=True)
        table[width : width + 1] += jnp.sum(slope, axis=0, keepdims=True)
        return carry

    lax.fori_loop(0, span // 128, through, 0)

    for i in range(quarters):
        lanes = slice(i * narrow, (i + 1) * narrow)

        def conv_back(t, carry, i=i, lanes=lanes):
            at = pl.multiple_of(t * 128, 128)
            ahead = pl.multiple_of(t * 128 + 128, 16)
            known = pl.multiple_of(jnp.minimum(t * 128 + 128, span - 16), 16)
            here = dpre[pl.ds(at, 128), lanes]
            both = jnp.concatenate([here, dpre[pl.ds(ahead, 16), lanes]], axis=0)
            masks = jnp.concatenate([masks_ref[pl.ds(at, 128)], masks_ref[pl.ds(known, 16)]], axis=0)
            back = taps_all[width - 1 : width, lanes] * here
            for k in range(1, width):
                masked = both * masks[:, k : k + 1]
                back = back + taps_all[width - 1 - k : width - k, lanes] * masked[k : 128 + k]
            leave[i, pl.ds(at, 128)] = back.astype(BF)
            return carry

        lax.fori_loop(0, span // 128, conv_back, 0)
        hand_over(0, i)

    for kind in range(3):
        chosen_proj = jnp.where(dead == kind, dproj[...].astype(F32), 0.0).astype(BF)
        grad = jnp.dot(chosen_proj, u_ref[...], preferred_element_type=F32)
        filler = jnp.zeros((small.shape[2] - rank_rows - step_rows, channels), F32)
        for owner in range(dp):
            ranks = grad[owner * rank_rows : (owner + 1) * rank_rows]
            sizes = dt_grad[kind, owner * step_rows : (owner + 1) * step_rows]
            small[owner, kind] = jnp.concatenate([ranks, sizes, filler], axis=0).astype(BF)

    def lend_table(k):
        return remote(table, got_tables.at[k], t_send.at[k], t_recv.at[k], (mates[k], place))

    def lend_small(k):
        return remote(small.at[mates[k]], got_small.at[k], l_send.at[k], l_recv.at[k], (mates[k], place))

    for k in range(dp - 1):
        lend_small(k).start()

    def cross(k, q):
        return remote(gm.at[me, q], gm.at[me, q], x_send.at[k, q], x_recv.at[k, q], across[k])

    def pair(q):
        return remote(gm.at[me, q], gm.at[me, q], core_send.at[q], core_recv.at[q], partner)

    def onward(k, q):
        owner = lax.rem(line + lines - 1 - k, lines) * 2 + core
        return remote(gm.at[owner, q], gm.at[owner, q], on_send.at[k, q], on_recv.at[k, q], partner)

    def pass_on(q):
        for k in range(lines - 1):
            cross(k, q).wait_recv()
            onward(k, q).start()

    owners = [me, me + 1 - 2 * core]
    for k in range(1, lines):
        far = lax.rem(line + k, lines) * 2
        owners += [far + core, far + 1 - core]

    outs = []

    def master_grad(number, q):
        pair(q).wait_recv()
        for k in range(lines - 1):
            onward(k, q).wait_recv()
        if len(outs) >= 2:
            outs[number - 2].wait()

        def one_kind(kind, carry):
            total = jnp.zeros((rows, narrow), F32)
            for k, owner in enumerate(owners):
                tag = kind_refs[k][...].astype(F32)
                right = jnp.where(tag == kind.astype(F32), gm[owner, q].astype(F32), 0.0).astype(BF)
                total += lax.dot_general(feats[k], right, (((0,), (0,)), ((), ())), preferred_element_type=F32)
            stage[number % 2, kind] = total
            return carry

        lax.fori_loop(0, 3, one_kind, 0)
        out = pltpu.make_async_copy(
            stage.at[number % 2], ingrad_ref.at[:, :, pl.ds(q * narrow, narrow)], o_send.at[number % 2]
        )
        out.start()
        outs.append(out)

    turns = [h * quarters + i for i in range(quarters) for h in range(2)]
    for copy in loads:
        copy.wait()
    for number, q in enumerate(turns):
        arrive(q)
        for k in range(lines - 1):
            cross(k, q).start()
        pair(q).start()

        def pick(t, carry, q=q):
            at = pl.ds(pl.multiple_of(t * TILE, TILE), TILE)
            tag = tags_ref[pl.ds(t * blocks, blocks)].reshape(TILE, -1)[:, :1].astype(F32)
            value = gm[me, q, at].astype(F32)
            left = [jnp.where(tag == kind, value, 0.0).astype(BF) for kind in range(3)]
            for owner in range(dp):
                total = dn[at, owner * rows : (owner + 1) * rows]
                for kind in range(3):
                    total += lax.dot_general(
                        left[kind],
                        wall[owner, kind, :, q * narrow : (q + 1) * narrow],
                        (((1,), (1,)), ((), ())),
                        preferred_element_type=F32,
                    )
                dn[at, owner * rows : (owner + 1) * rows] = total
            return carry

        lax.fori_loop(0, span // TILE, pick, 0)
        if 0 < number < cuts - 1:
            pass_on(turns[number - 1])
        if 1 < number < cuts - 1:
            master_grad(number - 2, turns[number - 2])

    half_columns = depth // 2
    cut = half_columns // CUTS

    def lanes_of(side, i):
        return slice(side * half_columns + i * cut, side * half_columns + (i + 1) * cut)

    def block(side, hop):
        step = position + wide - 1 - hop if side == 0 else position + 1 + hop
        owner = ring_index(lax.rem(step, wide), wide)
        return pl.ds(pl.multiple_of(owner * count, count), count)

    flows = ((flow_a, a_send, a_recv, after), (flow_b, b_send, b_recv, before))

    def turn(side, hop, i):
        flow, send, recv, device = flows[side]
        origin = first.at[side, i] if hop == 0 else flow.at[hop - 1, i]
        return remote(origin, flow.at[hop, i], send.at[hop, i], recv.at[hop, i], device)

    for i in range(CUTS):
        for side in range(2):
            first[side, i] = dn[block(side, 0), lanes_of(side, i)].astype(BF)
            turn(side, 0, i).start()

    def normed_copy(b):
        return pltpu.make_async_copy(normed_ref.at[b], nbuf.at[b % 2], nload.at[b % 2])

    normed_copy(0).start()
    pass_on(turns[cuts - 2])
    gain = jnp.zeros((1, depth), F32)
    for b in range(wide):
        if b + 1 < wide:
            normed_copy(b + 1).start()
        normed_copy(b).wait()
        gain = gain + jnp.sum(
            dn[b * count : (b + 1) * count] * nbuf[b % 2].astype(F32), axis=0, keepdims=True
        )
    for k in range(depth // channels):
        at = width + 5 + states + k
        table[at : at + 1] = gain[:, k * channels : (k + 1) * channels]
    for k in range(dp - 1):
        lend_table(k).start()

    def show(k):
        return remote(tables_ref.at[place], tables_ref.at[place], w_send.at[k], w_recv.at[k], (me, peers[k]))

    for hop in range(1, wide):
        for i in range(CUTS):
            for side in range(2):
                turn(side, hop - 1, i).wait_recv()
                flow = flows[side][0]
                total = flow[hop - 1, i].astype(F32) + dn[block(side, hop), lanes_of(side, i)]
                if hop < wide - 1:
                    flow[hop - 1, i] = total.astype(BF)
                    turn(side, hop, i).start()
                else:
                    rows_ref[:, lanes_of(side, i)] = total
        if hop == 1:
            master_grad(cuts - 3, turns[cuts - 3])
            pass_on(turns[cuts - 1])
        if hop == 2:
            total = table[...]
            for k in range(dp - 1):
                lend_table(k).wait_recv()
                total = total + got_tables[k]
            tables_ref[place] = total
            for k in range(wide - 1):
                show(k).start()
        if hop == 3:
            master_grad(cuts - 2, turns[cuts - 2])
        if hop == 5:
            master_grad(cuts - 1, turns[cuts - 1])
        if hop == 4:
            for kind in range(3):
                sums_ref[kind] = small[me, kind].astype(F32)
            for k in range(dp - 1):
                lend_small(k).wait_recv()
                for kind in range(3):
                    sums_ref[kind] += got_small[k, kind].astype(F32)

    for k in range(dp - 1):
        lend_table(k).wait_send()
        lend_small(k).wait_send()
    for k in range(wide - 1):
        show(k).wait()
    for k in range(1, wide):
        share(k).wait_send()
        give(k).wait_send()
    for hop in range(wide - 1):
        for i in range(CUTS):
            for side in range(2):
                turn(side, hop, i).wait_send()
    for q in range(cuts):
        pair(q).wait_send()
        for k in range(lines - 1):
            cross(k, q).wait_send()
            onward(k, q).wait_send()
    for kind in range(2):
        for i in range(quarters):

            @pl.when(kind * half + place // 2 != place)
            def _(kind=kind, i=i):
                deliver(kind, i).wait_send()

    for out in outs[-2:]:
        out.wait()


def back(win, feats, normed, kinds, vmem_args, rank_rows, step_rows, collective_id):
    dp, wide = lax.axis_size("dp"), lax.axis_size("wide")
    _, _, rows, columns = win.shape
    _, count, depth = normed.shape
    cuts = 4
    narrow = columns // cuts
    quarters = cuts // 2
    span, channels = vmem_args[0].shape
    rank, steps = vmem_args[6].shape[0], vmem_args[8].shape[1]
    extra, width = vmem_args[14], vmem_args[12].shape[0]
    lines = dp // 2
    table_rows = width + 4 + extra.shape[0] + depth // channels
    table_rows += -table_rows % 8
    small_rows = rank_rows + step_rows
    small_rows += -small_rows % 16
    vmem = pl.BlockSpec(memory_space=pltpu.VMEM)
    anywhere = pl.BlockSpec(memory_space=pl.ANY)
    dma = pltpu.SemaphoreType.DMA
    shape = jax.ShapeDtypeStruct
    flow = pltpu.VMEM((wide - 1, CUTS, count, depth // 2 // CUTS), BF)
    hops, far, near = dma((wide - 1, CUTS)), dma((lines - 1, cuts)), dma((cuts,))
    mates, peers = dma((dp - 1,)), dma((wide,))
    return pl.pallas_call(
        functools.partial(back_kernel, dp, wide, rank_rows, step_rows),
        out_shape=[
            shape((3, rows, columns), F32),
            shape((count, depth), F32),
            shape((wide, table_rows, channels), F32),
            shape((3, small_rows, channels), F32),
        ],
        in_specs=[anywhere] * dp + [vmem] * dp + [anywhere] * 2 + [vmem] * len(vmem_args),
        out_specs=[anywhere] + [vmem] * 3,
        scratch_shapes=[
            pltpu.VMEM(win.shape, BF),
            pltpu.VMEM((dp,) + feats[0].shape, BF),
            pltpu.VMEM((2, count, depth), BF),
            pltpu.VMEM((rank, span), BF),
            pltpu.VMEM((wide, rank, count), BF),
            pltpu.VMEM((rank, count), BF),
            pltpu.VMEM((rank, span), BF),
            pltpu.VMEM((span + 16, channels), F32),
            pltpu.VMEM((quarters, span, narrow), BF),
            pltpu.VMEM((dp, cuts, span, narrow), BF),
            pltpu.VMEM((span, depth), F32),
            pltpu.VMEM((2, CUTS, count, depth // 2 // CUTS), BF),
            flow,
            flow,
            pltpu.VMEM((2, 3, rows, narrow), F32),
            pltpu.VMEM((table_rows, channels), F32),
            pltpu.VMEM((dp - 1, table_rows, channels), F32),
            pltpu.VMEM((3, steps, channels), F32),
            pltpu.VMEM((dp, 3, small_rows, channels), BF),
            pltpu.VMEM((dp - 1, 3, small_rows, channels), BF),
            peers, peers, peers, peers, dma((dp + 1,)), dma((2,)), dma((2, quarters)), near, dma((quarters,)),
            far, far, near, near, far, far, dma((2,)),
            hops, hops, hops, hops, mates, mates, mates, mates, peers, peers,
        ],
        compiler_params=pltpu.CompilerParams(
            collective_id=collective_id, has_side_effects=True, vmem_limit_bytes=62 << 20
        ),
        name="back",
    )(*feats, *kinds, win, normed, *vmem_args)


def branch_kernel(gated_ref, tag_ref, w_ref, branch_ref):
    dp, kinds, rows, channels = w_ref.shape
    tag = tag_ref[...][:, :1].astype(F32)
    gated = gated_ref[...].astype(F32)
    chosen = [jnp.where(tag == kind, gated, 0.0).astype(BF) for kind in range(3)]
    for owner in range(dp):
        branch = jnp.zeros((gated.shape[0], rows), F32)
        for kind in range(3):
            branch += lax.dot_general(
                chosen[kind], w_ref[owner, kind], (((1,), (1,)), ((), ())), preferred_element_type=F32
            )
        branch_ref[:, owner * rows : (owner + 1) * rows] = branch.astype(BF)


def branch_of(gated, tags, w_out, depth):
    span, channels = gated.shape
    tile = lambda lanes: pl.BlockSpec((TILE, lanes), lambda t: (t, 0))
    return pl.pallas_call(
        branch_kernel,
        grid=(span // TILE,),
        out_shape=jax.ShapeDtypeStruct((span, depth), BF),
        in_specs=[tile(channels), tile(tags.shape[1]), pl.BlockSpec(memory_space=pltpu.VMEM)],
        out_specs=tile(depth),
        compiler_params=pltpu.CompilerParams(vmem_limit_bytes=40 << 20),
        cost_estimate=pl.CostEstimate(
            flops=6 * span * channels * depth, bytes_accessed=12 << 20, transcendentals=0
        ),
        name="branch",
    )(gated, tags, w_out)


def gate_kernel(back_ref, gated_ref, tag_ref, w_ref, dgated_ref, grad_ref):
    dp, kinds, rows, channels = w_ref.shape
    span = gated_ref.shape[0]

    def tile(t, carry):
        at = pl.ds(pl.multiple_of(t * TILE, TILE), TILE)
        tag = tag_ref[at][:, :1].astype(F32)
        total = jnp.zeros((TILE, channels), F32)
        for kind in range(3):
            product = jnp.zeros((TILE, channels), F32)
            for owner in range(dp):
                product += jnp.dot(
                    back_ref[at, owner * rows : (owner + 1) * rows], w_ref[owner, kind], preferred_element_type=F32
                )
            total = total + jnp.where(tag == kind, product, 0.0)
        dgated_ref[at] = total.astype(BF)
        return carry

    lax.fori_loop(0, span // TILE, tile, 0)

    def grad(owner, carry):
        columns = pl.ds(pl.multiple_of(owner * rows, rows), rows)
        for kind in range(3):
            tag = tag_ref[...][:, :1].astype(F32)
            chosen = jnp.where(tag == kind, gated_ref[...].astype(F32), 0.0).astype(BF)
            grad_ref[owner, kind] = lax.dot_general(
                back_ref[:, columns], chosen, (((0,), (0,)), ((), ())), preferred_element_type=F32
            ).astype(BF)
        return carry

    lax.fori_loop(0, dp, grad, 0)


def gate(back, gated, tags, w_out):
    span, channels = gated.shape
    vmem = pl.BlockSpec(memory_space=pltpu.VMEM)
    return pl.pallas_call(
        gate_kernel,
        out_shape=[
            jax.ShapeDtypeStruct(gated.shape, BF),
            jax.ShapeDtypeStruct(w_out.shape, BF),
        ],
        in_specs=[vmem] * 4,
        out_specs=[vmem] * 2,
        compiler_params=pltpu.CompilerParams(vmem_limit_bytes=58 << 20),
        cost_estimate=pl.CostEstimate(
            flops=12 * span * channels * back.shape[1], bytes_accessed=20 << 20, transcendentals=0
        ),
        name="gate",
    )(back, gated, tags, w_out)


def contract(left, right, left_dim, right_dim):
    return lax.dot_general(
        left, right, (((left_dim,), (right_dim,)), ((), ())), preferred_element_type=F32
    )


def segment_of(places, bounds):
    return jnp.sum((places[:, None] >= bounds[None, :]).astype(jnp.int32), axis=1)


def conv_masks(places, bounds, width):
    segment = segment_of(places, bounds)
    return [
        ((places >= offset) & (segment_of(places - offset, bounds) == segment)).astype(F32)
        for offset in range(width)
    ]


def silu_slope(values):
    sigma = jax.nn.sigmoid(values)
    return sigma * (1.0 + values * (1.0 - sigma))


def split_kinds(rows, kinds, parts):
    count, depth = rows.shape
    pieces = rows.reshape(count, parts, 1, depth // parts)
    picked = kinds[:, None, :, None]
    return jnp.where(picked, pieces, jnp.zeros((), rows.dtype)).reshape(count, 3 * depth)


def scatter_master(grad):
    return jnp.transpose(lax.psum_scatter(grad, "dp", scatter_dimension=0), (1, 0, 2))


def hop(block, flip):
    devices = lax.axis_size("dp")
    return lax.ppermute(block, "dp", [(d, flip(d)) for d in range(devices)])


def from_partners(block):
    lines = lax.axis_size("dp") // 2
    blocks = [block, hop(block, lambda d: d ^ 1)]
    for k in range(1, lines):
        far = hop(block, lambda d: (d // 2 + k) % lines * 2 + d % 2)
        blocks += [far, hop(far, lambda d: d ^ 1)]
    return blocks


def swap_features(rows):
    devices = lax.axis_size("dp")
    lines = devices // 2
    depth = rows.shape[1] // devices
    me = lax.axis_index("dp")

    def part(owner):
        return lax.dynamic_slice_in_dim(rows, owner * depth, depth, 1)

    core = me % 2
    blocks = [part(me), hop(part(me + 1 - 2 * core), lambda d: d ^ 1)]
    for k in range(1, lines):
        line = (me // 2 + k) % lines
        blocks.append(hop(part(line * 2 + core), lambda d: (d // 2 + k) % lines * 2 + d % 2))
        blocks.append(
            hop(part(line * 2 + 1 - core), lambda d: (d // 2 + k) % lines * 2 + 1 - d % 2)
        )
    return blocks


def halves_back(xs, z, wide):
    half = wide // 2
    low = lax.axis_index("wide") < half
    even = [(2 * v, v) if v < half else (2 * (v - half) + 1, v) for v in range(wide)]
    odd = [(2 * v + 1, v) if v < half else (2 * (v - half), v) for v in range(wide)]
    is_even = lax.axis_index("wide") % 2 == 0
    got_a = lax.ppermute(jnp.where(is_even, xs, z), "wide", even)
    got_b = lax.ppermute(jnp.where(is_even, z, xs), "wide", odd)
    return jnp.concatenate([jnp.where(low, got_a, got_b), jnp.where(low, got_b, got_a)], axis=1)


def body(
    x_in,
    lengths,
    modality,
    norm_gain,
    conv_weight,
    conv_bias,
    a_log,
    d_skip,
    in_master,
    xproj_master,
    dtproj_master,
    dt_bias,
    out_master,
    cotangent,
):
    wide, dp = lax.axis_size("wide"), lax.axis_size("dp")
    place = lax.axis_index("wide")
    count = x_in.shape[0]
    span = count * wide
    channels = INNER // wide
    width = conv_weight.shape[0]
    own = lambda table: lax.dynamic_slice_in_dim(table, place * channels, channels, table.ndim - 1)

    pieces = lengths.reshape(-1)
    ends = [pieces[0]]
    for at in range(1, pieces.shape[0]):
        ends.append(ends[-1] + pieces[at])
    bounds = jnp.stack(ends)
    places = jnp.arange(span, dtype=jnp.int32)
    living = places < bounds[-1]
    masks = conv_masks(places, bounds, width)
    alive_here = (place * count + jnp.arange(count, dtype=jnp.int32)) < bounds[-1]

    scale = lax.rsqrt(jnp.mean(x_in * x_in, axis=1, keepdims=True) + EPSILON)
    rank_rows, step_rows = xproj_master.shape[0], dtproj_master.shape[0]
    small = jnp.concatenate([xproj_master, dtproj_master], axis=0)
    small = jnp.pad(small, ((0, -small.shape[0] % 16), (0, 0), (0, 0)))
    tag = jnp.where(alive_here, modality, 3).astype(BF)
    mask_table = jnp.stack(masks, axis=1)
    w_in, w_out, normed_all, d_branch_all, tags_all, w_x_kinds, w_dt_kinds, xs, z, inner, proj = front(
        jnp.transpose(in_master, (1, 0, 2)),
        jnp.transpose(out_master, (1, 0, 2)),
        jnp.transpose(small, (1, 0, 2)),
        x_in,
        cotangent,
        norm_gain[None, :],
        jnp.broadcast_to(tag[:, None], (count, 128)),
        mask_table,
        conv_weight,
        conv_bias[None, :],
        rank_rows,
        step_rows,
        0,
    )
    w_in = w_in.reshape(-1, in_master.shape[2])
    normed_all = normed_all.reshape(span, -1)
    kinds_all = tags_all[:, :, 0].reshape(span)
    kinds = kinds_all[:, None] == jnp.arange(3, dtype=BF)[None, :]

    kinds_parts = from_partners(kinds_all[:, None])
    features = swap_features(normed_all)

    rank = w_x_kinds.shape[1]
    tags_flat = tags_all.reshape(span, -1)
    skip_row = d_skip[None, :]
    dtp, gated, y_value, heads = scan_forward(
        proj, w_dt_kinds, dt_bias, tags_flat, inner, mask_table, a_log, skip_row, z
    )
    branch = branch_of(gated, tags_flat, w_out, x_in.shape[1])
    branch = lax.psum_scatter(branch, "wide", scatter_dimension=0, tiled=True)
    result = x_in + branch.astype(F32)
    d_gated, grad_out = gate(d_branch_all.reshape(span, -1), gated, tags_flat, w_out)
    out_grad = scatter_master(grad_out).astype(F32)
    d_dtp, d_scan, d_z, d_columns, extra = scan_backward(
        dtp, inner, proj, mask_table, a_log, skip_row, z, y_value, d_gated, heads
    )
    d_dtp, features, kinds_parts = lax.optimization_barrier((d_dtp, features, kinds_parts))
    d_maps = d_columns.reshape(-1, 2, d_columns.shape[2] // STATE, STATE)
    d_maps = d_maps.transpose(1, 3, 0, 2).reshape(2 * STATE, span)
    if span * x_in.shape[1] * 4 <= 12 << 20:
        in_grad, d_normed, tables, small = back(
            w_in.reshape(dp, 3, -1, w_in.shape[1]),
            features,
            normed_all.reshape(wide, count, -1),
            kinds_parts,
            (
                d_dtp,
                d_scan,
                d_z,
                xs,
                inner,
                d_maps,
                proj,
                w_x_kinds,
                w_dt_kinds,
                tags_all,
                jnp.broadcast_to(kinds_all.astype(F32)[None], (8, span)),
                mask_table,
                conv_weight,
                conv_bias[None, :],
                extra,
            ),
            rank_rows,
            step_rows,
            2,
        )
        in_grad = jnp.transpose(in_grad, (1, 0, 2))
    else:
        taps = own(conv_weight)
        across = kinds.T[:, None, :]
        rates_kinds = split_kinds(proj[:DT_RANK].T, kinds, 1)
        d_dtp = jnp.where(living[:, None], d_dtp, jnp.zeros((), BF))
        xs_value = xs.astype(F32)
        extended = jnp.concatenate([jnp.zeros((width - 1, channels), F32), xs_value], axis=0)
        pre = own(conv_bias)[None, :]
        for offset in range(width):
            begin = width - 1 - offset
            pre = (
                pre + taps[begin][None, :] * extended[begin : begin + span] * masks[offset][:, None]
            )

        feature_kinds = [
            split_kinds(rows, tags == jnp.arange(3, dtype=BF)[None, :], 1)
            for rows, tags in zip(features, kinds_parts)
        ]
        by_kind = contract(w_dt_kinds.reshape(3 * DT_RANK, channels), d_dtp, 1, 1)
        d_rates = jnp.sum(jnp.where(across, by_kind.reshape(3, DT_RANK, span), 0.0), axis=0)
        d_proj = sum_wide(jnp.concatenate([d_rates, d_maps], axis=0).astype(BF), 3)
        d_proj = jnp.where(living[None], d_proj, jnp.zeros((), BF)).T
        grad_dt = contract(rates_kinds, d_dtp, 0, 0).reshape(3, dp, step_rows, channels)
        bias_part = jnp.stack(
            [jnp.sum(jnp.where(kinds[:, k : k + 1], d_dtp.astype(F32), 0.0), axis=0) for k in range(3)]
        )
        d_proj_kinds = split_kinds(d_proj, kinds, 1)
        d_inner = contract(d_proj_kinds, w_x_kinds.reshape(3 * rank, channels), 1, 0).astype(BF)
        grad_x = contract(d_proj_kinds, inner, 0, 0)
        grad_x = grad_x.reshape(3, dp, rank_rows, channels)

        d_pre = (d_inner.astype(F32) + d_scan) * silu_slope(pre)
        later = conv_masks(jnp.arange(span + width - 1, dtype=jnp.int32), bounds, width)
        further = jnp.concatenate([d_pre, jnp.zeros((width - 1, channels), F32)], axis=0)
        conv_rows = []
        d_xs = jnp.zeros_like(xs_value)
        for offset in range(width):
            begin = width - 1 - offset
            conv_rows.append(
                jnp.sum(d_pre * masks[offset][:, None] * extended[begin : begin + span], axis=0)
            )
            masked = further * later[offset][:, None]
            d_xs = d_xs + taps[begin][None, :] * masked[offset : offset + span]
        conv_part = jnp.stack(conv_rows[::-1], axis=0)
        conv_bias_part = jnp.sum(d_pre, axis=0)
        d_xs = jnp.where(living[:, None], d_xs, 0.0).astype(BF)
        d_z = jnp.where(living[:, None], d_z, jnp.zeros((), BF))
        d_mixed = halves_back(d_xs, d_z, wide)
        mixed_parts = from_partners(d_mixed)
        grad_in = 0.0
        for pair in range(0, dp, 2):
            left = jnp.concatenate(feature_kinds[pair : pair + 2], axis=0)
            grad_in = grad_in + contract(left, jnp.concatenate(mixed_parts[pair : pair + 2], axis=0), 0, 0)
        in_grad = jnp.transpose(grad_in.reshape(3, -1, d_mixed.shape[1]), (1, 0, 2))

        d_normed = jnp.zeros((span, x_in.shape[1]), F32)
        w_in_kinds = w_in.reshape(dp, 3, -1, w_in.shape[1])
        for kind in range(3):
            picked = jnp.where(kinds[:, kind : kind + 1], d_mixed, jnp.zeros((), BF))
            d_normed = d_normed + contract(
                picked, w_in_kinds[:, kind].reshape(-1, w_in.shape[1]), 1, 1
            )
        d_normed = d_normed.astype(BF)
        gain_part = jnp.sum(d_normed.astype(F32) * normed_all.astype(F32), axis=0)
        table = [conv_part, conv_bias_part[None], extra, bias_part]
        table.append(gain_part.reshape(-1, channels))
        table = jnp.concatenate(table, axis=0)
        table = jnp.pad(table, ((0, -table.shape[0] % 8), (0, 0)))
        small = jnp.concatenate([grad_x, grad_dt], axis=2).transpose(1, 0, 2, 3)
        small = jnp.pad(small, ((0, 0), (0, 0), (0, -small.shape[2] % 16), (0, 0))).astype(BF)
        d_normed, tables, small = finish(d_normed.reshape(wide, count, -1), table, small, 4)
    xproj_grad = jnp.transpose(small[:, :rank_rows], (1, 0, 2))
    dtproj_grad = jnp.transpose(small[:, rank_rows : rank_rows + step_rows], (1, 0, 2))
    d_normed = d_normed.astype(BF).astype(F32)
    scaled_back = d_normed * norm_gain[None, :]
    x_grad = cotangent + scale * (
        scaled_back - x_in * scale * scale * jnp.mean(scaled_back * x_in, axis=1, keepdims=True)
    )

    edge = width + 1 + STATE + 1
    shared = tables[:, :edge].transpose(1, 0, 2).reshape(edge, INNER)
    bias_grad = lax.dynamic_index_in_dim(tables, place, 0, False)[edge : edge + 3]
    kept = edge + 3 + x_in.shape[1] // channels
    gain_grad = jnp.sum(tables[:, edge + 3 : kept], axis=0).reshape(-1) / norm_gain
    return (
        result,
        x_grad,
        gain_grad,
        shared[:width],
        shared[width],
        shared[width + 1 : width + 1 + STATE],
        shared[width + 1 + STATE],
        in_grad,
        xproj_grad,
        dtproj_grad,
        bias_grad,
        out_grad,
    )


def solution(mesh):
    in_specs = (
        P(("dp", "wide"), None),
        P("dp", None),
        P(("dp", "wide")),
        P(),
        P(),
        P(),
        P(),
        P(),
        P("dp", None, "wide"),
        P("dp", None, "wide"),
        P("dp", None, "wide"),
        P(None, "wide"),
        P("dp", None, "wide"),
        P(("dp", "wide"), None),
    )
    out_specs = (
        P(("dp", "wide"), None),
        P(("dp", "wide"), None),
        P(),
        P(),
        P(),
        P(),
        P(),
        P("dp", None, "wide"),
        P("dp", None, "wide"),
        P("dp", None, "wide"),
        P(None, "wide"),
        P("dp", None, "wide"),
    )
    return jax.shard_map(body, mesh=mesh, in_specs=in_specs, out_specs=out_specs, check_vma=False)
```

```python
import functools

import jax
import jax.numpy as jnp
from jax import lax
from jax.experimental import pallas as pl
from jax.experimental.pallas import tpu as pltpu
from jax.sharding import PartitionSpec as P

F32 = jnp.float32
BF = jnp.bfloat16
INNER = 4096
STATE = 16
DT_RANK = 128
EPSILON = 1e-05


STEPS=32
HUGE=1e30

def own_lanes(channels):
    return pl.ds(pl.multiple_of(lax.axis_index("wide")*channels,channels),channels)

def split_columns(proj_ref,first,cols):
    rows=proj_ref[first:first+cols.shape[1]].astype(F32)
    for k in range(cols.shape[0]):
        cols[k]=rows[:,k*STEPS:(k+1)*STEPS]

def scan_forward_kernel(proj_ref,wdt_ref,dtb_ref,tag_ref,u_ref,masks_ref,alog_ref,skip_ref,z_ref, dtp_ref,gated_ref,y_ref,heads_ref, st, dec, inj, ys, a2, b_ref, c_ref):
    T,C=u_ref.shape
    R=wdt_ref.shape[1]
    S=alog_ref.shape[0]
    @pl.when(pl.program_id(0)==0)
    def _():
        st[...]=jnp.zeros_like(st)
        a2[...]=-jnp.exp(alog_ref[:,own_lanes(C)])*1.4426950408889634
    split_columns(proj_ref,R,b_ref)
    split_columns(proj_ref,R+S,c_ref)
    tag=tag_ref[:,:1].astype(F32)
    rates=proj_ref[:R]
    dtp=jnp.zeros((T,C),F32)
    for kind in range(3):
        step=lax.dot_general(rates,wdt_ref[kind],(((0,),(0,)),((),())),preferred_element_type=F32)
        step=step+dtb_ref[kind:kind+1].astype(BF).astype(F32)
        dtp=dtp+jnp.where(tag==kind,step,0.0)
    dtp=dtp.astype(BF)
    dtp_ref[...]=dtp
    delta=jax.nn.softplus(dtp.astype(F32))
    u=u_ref[...].astype(F32)
    dec[...]=jnp.where(masks_ref[:,1:2]>0,delta,HUGE)
    inj[...]=delta*u
    def chunk(k,state):
        heads_ref[k]=state
        b=b_ref[k]; c=c_ref[k]
        an=a2[...]
        base=pl.multiple_of(k*STEPS,STEPS)
        for j in range(STEPS):
            d=dec[pl.ds(base+j,1),:]
            v=inj[pl.ds(base+j,1),:]
            state=jnp.exp2(d*an)*state+b[:,j:j+1]*v
            ys[pl.ds(base+j,1),:]=jnp.sum(c[:,j:j+1]*state,axis=0,keepdims=True)
        return state
    st[...]=lax.fori_loop(0,T//STEPS,chunk,st[...])
    y=ys[...]+skip_ref[:,own_lanes(C)]*u
    y_ref[...]=y
    z=z_ref[...].astype(F32)
    gated_ref[...]=(y*(z*jax.nn.sigmoid(z))).astype(BF)

def scan_forward(proj,wdt,dtb,tags,u,masks,alog,skip,z,T=128):
    N,C=u.shape
    S=alog.shape[0]
    nk=N//STEPS; tk=T//STEPS
    row=pl.BlockSpec((T,C),lambda i:(i,0))
    whole=lambda s: pl.BlockSpec(s,lambda i:(0,)*len(s))
    tile=lambda lanes: pl.BlockSpec((T,lanes),lambda i:(i,0))
    return pl.pallas_call(scan_forward_kernel,grid=(N//T,),
      in_specs=[pl.BlockSpec((proj.shape[0],T),lambda i:(0,i)),whole(wdt.shape),whole(dtb.shape),tile(tags.shape[1]),row,tile(masks.shape[1]),whole(alog.shape),whole(skip.shape),row],
      out_specs=[row,row,row,pl.BlockSpec((tk,S,C),lambda i:(i,0,0))],
      out_shape=[jax.ShapeDtypeStruct((N,C),BF),jax.ShapeDtypeStruct((N,C),BF),jax.ShapeDtypeStruct((N,C),F32),jax.ShapeDtypeStruct((nk,S,C),F32)],
      scratch_shapes=[pltpu.VMEM((S,C),F32),pltpu.VMEM((T,C),F32),pltpu.VMEM((T,C),F32),pltpu.VMEM((T,C),F32),pltpu.VMEM((S,C),F32),pltpu.VMEM((tk,S,STEPS),F32),pltpu.VMEM((tk,S,STEPS),F32)],
      compiler_params=pltpu.CompilerParams(vmem_limit_bytes=48<<20),
      cost_estimate=pl.CostEstimate(flops=2500*N*C*S,bytes_accessed=16<<20,transcendentals=N*C*S),
      name="scan_forward")(proj,wdt,dtb,tags,u,masks,alog,skip,z)

def fold_lanes(values):
    total=values[:,:128]
    for k in range(128,values.shape[1],128):
        total=total+values[:,k:k+128]
    return total

def sum_lanes(ref):
    values=ref[...].reshape(-1,128)
    high=values.astype(BF)
    rest=(values-high.astype(F32)).astype(BF)
    ones=jnp.ones((8,128),BF)
    dims=(((1,),(1,)),((),()))
    return (lax.dot_general(ones,high,dims,preferred_element_type=F32)+lax.dot_general(ones,rest,dims,preferred_element_type=F32))[:1]

def scan_backward_kernel(dtp_ref,u_ref,proj_ref,masks_ref,alog_ref,skip_ref,z_ref,y_ref,dg_ref,heads_ref,
        ddtp_ref,dus_ref,dz_ref,dm_ref,extra_ref, run, dec, inj, dly, dys, sq, wa, sts, dcs, an2, an1, acc, pb, pc, b_ref, c_ref):
    T,C=u_ref.shape
    S=alog_ref.shape[0]
    first=pl.program_id(0)==0
    last=pl.program_id(0)==pl.num_programs(0)-1
    @pl.when(first)
    def _():
        run[...]=jnp.zeros_like(run)
        acc[...]=jnp.zeros_like(acc)
        extra_ref[...]=jnp.zeros_like(extra_ref)
        an1[...]=-jnp.exp(alog_ref[:,own_lanes(C)])
        an2[...]=an1[...]*1.4426950408889634
    R=proj_ref.shape[0]-2*S
    split_columns(proj_ref,R,b_ref)
    split_columns(proj_ref,R+S,c_ref)
    dtp=dtp_ref[...].astype(F32)
    delta=jax.nn.softplus(dtp)
    u=u_ref[...].astype(F32)
    dec[...]=jnp.where(masks_ref[:,1:2]>0,delta,HUGE)
    dly[...]=delta
    inj[...]=delta*u
    z=z_ref[...].astype(F32)
    sg=jax.nn.sigmoid(z)
    dg=dg_ref[...].astype(F32)
    dy=dg*(z*sg)
    dys[...]=dy
    dz_ref[...]=(dg*y_ref[...]*(sg*(1.0+z*(1.0-sg)))).astype(BF)
    extra_ref[S:S+1]+=jnp.sum(dy*u,axis=0,keepdims=True)
    def chunk(i,running):
        k=T//STEPS-1-i
        b=b_ref[k]; c=c_ref[k]
        base=pl.multiple_of(k*STEPS,STEPS)
        state=heads_ref[k]
        an=an2[...]
        for j in range(STEPS):
            d=dec[pl.ds(base+j,1),:]
            v=inj[pl.ds(base+j,1),:]
            dc=jnp.exp2(d*an)
            sd=dc*state
            state=sd+b[:,j:j+1]*v
            dcs[j]=dc
            sts[j]=sd
        for j in range(STEPS-1,-1,-1):
            g=dys[pl.ds(base+j,1),:]
            v=inj[pl.ds(base+j,1),:]
            bj=b[:,j:j+1]
            ds=c[:,j:j+1]*g+running
            sd=sts[j]
            w=ds*sd
            sq[pl.ds(base+j,1),:]=jnp.sum(ds*bj,axis=0,keepdims=True)
            wa[pl.ds(base+j,1),:]=jnp.sum(w*an1[...],axis=0,keepdims=True)
            acc[...]+=w*dly[pl.ds(base+j,1),:]
            pb[base+j]=fold_lanes(ds*v)
            pc[base+j]=fold_lanes(g*(sd+bj*v))
            running=dcs[j]*ds
        return running
    run[...]=lax.fori_loop(0,T//STEPS,chunk,run[...])
    dm_ref[0,0:1]=sum_lanes(pb)
    dm_ref[0,1:2]=sum_lanes(pc)
    dd=wa[...]+u*sq[...]
    ddtp_ref[...]=(dd*jax.nn.sigmoid(dtp)).astype(BF)
    dus_ref[...]=delta*sq[...]+dy*skip_ref[:,own_lanes(C)]
    @pl.when(last)
    def _():
        extra_ref[:S]=acc[...]*an1[...]

def scan_backward(dtp,u,proj,masks,alog,skip,z,y,dg,heads,T=128):
    N,C=u.shape
    S=alog.shape[0]
    nk=N//STEPS; tk=T//STEPS; nb=N//T
    row=pl.BlockSpec((T,C),lambda i:(nb-1-i,0))
    whole=lambda s: pl.BlockSpec(s,lambda i:(0,0))
    sc=lambda *s: pltpu.VMEM(s,F32)
    return pl.pallas_call(scan_backward_kernel,grid=(nb,),
      in_specs=[row,row,pl.BlockSpec((proj.shape[0],T),lambda i:(0,nb-1-i)),pl.BlockSpec((T,masks.shape[1]),lambda i:(nb-1-i,0)),whole(alog.shape),whole(skip.shape),row,row,row,pl.BlockSpec((tk,S,C),lambda i:(nb-1-i,0,0))],
      out_specs=[row,row,row,pl.BlockSpec((1,2,T*S),lambda i:(nb-1-i,0,0)),whole((S+1,C))],
      out_shape=[jax.ShapeDtypeStruct((N,C),BF),jax.ShapeDtypeStruct((N,C),F32),jax.ShapeDtypeStruct((N,C),BF),jax.ShapeDtypeStruct((nb,2,T*S),F32),jax.ShapeDtypeStruct((S+1,C),F32)],
      scratch_shapes=[sc(S,C),sc(T,C),sc(T,C),sc(T,C),sc(T,C),sc(T,C),sc(T,C),sc(STEPS,S,C),sc(STEPS,S,C),sc(S,C),sc(S,C),sc(S,C),sc(T,S,128),sc(T,S,128),sc(tk,S,STEPS),sc(tk,S,STEPS)],
      compiler_params=pltpu.CompilerParams(vmem_limit_bytes=48<<20),
      cost_estimate=pl.CostEstimate(flops=6000*N*C*S,bytes_accessed=24<<20,transcendentals=N*C*S),
      name="scan_backward")(dtp,u,proj,masks,alog,skip,z,y,dg,heads)


CUTS = 2
MESH = pl.DeviceIdType.MESH
FLIGHT = 6
TILE = 256
SMALL, OUTER = 100, 200
SIDE, LINES = pl.ds(96, 32), (pl.ds(0, 48), pl.ds(48, 48))


def ring_index(position, wide):
    if wide != 8:
        return position
    turn = position // 4
    return (1 - turn) * 2 * position + turn * (2 * (7 - position) + 1)


def ring_position(index, wide):
    if wide != 8:
        return index
    return index // 2 + index % 2 * (7 - 2 * (index // 2))


def remote(source, target, send, recv, device):
    return pltpu.make_async_remote_copy(
        src_ref=source, dst_ref=target, send_sem=send, recv_sem=recv, device_id=device, device_id_type=MESH
    )


def sum_over_wide(wide, me, place, x_ref, out_ref, got, whole, s1, r1, s2, r2, meanwhile):
    step = out_ref.shape[1] // wide
    peers = [lax.rem(place + k, wide) for k in range(1, wide)]

    def columns(index):
        return pl.ds(pl.multiple_of(index * step, step), step)

    def give(k):
        device = (me, peers[k - 1])
        return remote(x_ref.at[:, columns(peers[k - 1])], got.at[k], s1.at[k], r1.at[k], device)

    def spread(k):
        device = (me, peers[k - 1])
        return remote(whole, out_ref.at[:, columns(place)], s2.at[k], r2.at[k], device)

    order = sorted(range(1, wide), key=lambda k: -min(k, wide - k))
    for k in order:
        give(k).start()
    meanwhile()
    total = x_ref[:, columns(place)].astype(F32)
    for k in reversed(order):
        give(k).wait_recv()
        total = total + got[k].astype(F32)
    whole[...] = total.astype(BF)
    for k in order:
        spread(k).start()
    out_ref[:, columns(place)] = whole[...]
    for k in range(1, wide):
        spread(k).wait()
        give(k).wait_send()


class Spread:
    def __init__(self, wide, me, place, chunks, sems):
        self.wide, self.me, self.place, self.chunks = wide, me, place, chunks
        self.up_send, self.up_recv, self.down_send, self.down_recv, self.all_send, self.all_recv = sems
        self.z, self.y = place // 2, place % 2

    def copy(self, i, owner, own, send, recv, target):
        ref = self.chunks[i][0] if own else self.chunks[i][1].at[owner]
        return remote(ref, self.chunks[i][1].at[owner], send, recv, (self.me, target))

    def up(self, i, hop, lane):
        owner = (self.z - hop) * 2 + self.y + lane * (1 - 2 * self.y)
        send, recv = self.up_send.at[hop, i, lane], self.up_recv.at[hop, i, lane]
        return self.copy(i, owner, hop == 0 and lane == 0, send, recv, self.place + 2)

    def down(self, i, hop, lane):
        owner = (self.z + hop) * 2 + self.y + lane * (1 - 2 * self.y)
        send, recv = self.down_send.at[hop, i, lane], self.down_recv.at[hop, i, lane]
        return self.copy(i, owner, hop == 0 and lane == 0, send, recv, self.place - 2)

    def beside(self, i, z, own=False):
        owner = z * 2 + self.y
        return self.copy(i, owner, own, self.all_send.at[z, i], self.all_recv.at[z, i], self.place + 1 - 2 * self.y)

    def direct(self, i, k):
        target = lax.rem(self.place + k, self.wide)
        return self.copy(i, self.place, True, self.all_send.at[k, i], self.all_recv.at[k, i], target)

    def lanes(self, i):
        return range(2 if self.chunks[i][2] else 1)

    def leave(self, i, lane):
        @pl.when(self.z < 3)
        def _():
            self.up(i, 0, lane).start()

        @pl.when(self.z > 0)
        def _():
            self.down(i, 0, lane).start()

    def begin(self, i):
        if self.wide != 8:
            for k in range(1, self.wide):
                self.direct(i, k).start()
            return
        self.beside(i, self.z, True).start()
        self.leave(i, 0)

    def step(self, i, hop):
        if self.wide != 8:
            return
        if hop == 0 and self.chunks[i][2]:
            self.beside(i, self.z).wait_recv()
            self.leave(i, 1)
        for lane in self.lanes(i):

            @pl.when(self.z > hop)
            def _():
                self.up(i, hop, lane).wait_recv()
                if hop < 2:

                    @pl.when(self.z < 3)
                    def _():
                        self.up(i, hop + 1, lane).start()

                if not self.chunks[i][2]:
                    self.beside(i, self.z - 1 - hop).start()

            @pl.when(self.z + hop < 3)
            def _():
                self.down(i, hop, lane).wait_recv()
                if hop < 2:

                    @pl.when(self.z > 0)
                    def _():
                        self.down(i, hop + 1, lane).start()

                if not self.chunks[i][2]:
                    self.beside(i, self.z + 1 + hop).start()

    def end(self, i):
        if self.wide != 8:
            for k in range(1, self.wide):
                self.direct(i, k).wait_recv()
        elif not self.chunks[i][2]:
            for z in range(4):
                self.beside(i, z).wait_recv()

    def sent(self):
        for i in range(len(self.chunks)):
            if self.wide != 8:
                for k in range(1, self.wide):
                    self.direct(i, k).wait_send()
                continue
            for hop in range(3):
                for lane in self.lanes(i):

                    @pl.when((self.z >= hop) & (self.z < 3))
                    def _():
                        self.up(i, hop, lane).wait_send()

                    @pl.when((self.z + hop <= 3) & (self.z > 0))
                    def _():
                        self.down(i, hop, lane).wait_send()

            if self.chunks[i][2]:
                self.beside(i, self.z).wait_send()
            else:
                for z in range(4):
                    self.beside(i, z).wait_send()


def front_kernel(dp, wide, rank_rows, *refs):
    win_ref, wout_ref, small_ref, x_ref, cot_ref, gain_ref, tag_ref, masks_ref, taps_ref, bias_ref, refs = (
        *refs[:10],
        refs[10:],
    )
    feat_outs, refs = refs[:dp], refs[dp:]
    wall_out, wout_out, ball_out, tags_out, wx_ref, wdt_ref, xs_out, z_out, u_ref, dgated_ref, proj_ref, refs = (
        *refs[:11],
        refs[11:],
    )
    stage, stage_out, wout, wall, wsmall, nall, ball, tags, mixed, xz, part, part_low, got, whole, tall, refs = (
        *refs[:15],
        refs[15:],
    )
    x_send, x_recv, core_send, core_recv, on_send, on_recv, refs = *refs[:6], refs[6:]
    h_send, h_recv, h_local, load, keep = refs[:5]
    s1, r1, s2, r2 = refs[5:9]
    me, place = lax.axis_index("dp"), lax.axis_index("wide")
    cuts, span, narrow = mixed.shape
    half = wide // 2
    count = x_ref.shape[0]
    rows = win_ref.shape[1]
    lines = dp // 2
    line, core = me // 2, me % 2
    partner = (me + 1 - 2 * core, place)
    across = [(lax.rem(line + k, lines) * 2 + core, place) for k in range(1, lines)]
    barrier = pltpu.get_barrier_semaphore()
    for peer in [partner] + across + [(me, lax.rem(place + k, wide)) for k in range(1, wide)]:
        pl.semaphore_signal(barrier, inc=1, device_id=peer, device_id_type=MESH)
    pl.semaphore_wait(barrier, lines + wide - 1)

    turns = [h * (cuts // 2) + i for i in range(cuts // 2) for h in range(2)]
    pieces = [(q, kind) for q in turns for kind in range(3)]
    pieces += [(SMALL, kind) for kind in range(3)]
    pieces += [(OUTER + h, kind) for kind in range(3) for h in range(2)]
    height = wout_ref.shape[1] // 2

    def slot(j, owner):
        q, kind = pieces[j]
        if q >= OUTER:
            return wout.at[owner, kind, pl.ds((q - OUTER) * height, height)]
        if q == SMALL:
            return wsmall.at[owner, kind]
        return wall.at[owner, kind, :, pl.ds(q * narrow, narrow)]

    def cross(k, j):
        return remote(slot(j, me), slot(j, me), x_send.at[k, j], x_recv.at[k, j], across[k])

    def pair(j):
        return remote(slot(j, me), slot(j, me), core_send.at[j], core_recv.at[j], partner)

    def onward(k, j):
        owner = lax.rem(line + lines - 1 - k, lines) * 2 + core
        return remote(slot(j, owner), slot(j, owner), on_send.at[k, j], on_recv.at[k, j], partner)

    loads = []
    for q in turns:
        part_columns = pl.ds(q * narrow, narrow)
        loads.append(pltpu.make_async_copy(win_ref.at[:, :, part_columns], stage.at[:, :, part_columns], load.at[q]))
        loads[-1].start()
    loads.append(pltpu.make_async_copy(wout_ref, stage_out, load.at[cuts]))
    loads[-1].start()

    x = x_ref[...]
    scale = lax.rsqrt(jnp.mean(x * x, axis=1, keepdims=True) + EPSILON)
    nall[place] = (x * scale * gain_ref[...]).astype(BF)
    tags[place] = tag_ref[...]
    ball[place] = jnp.where(tag_ref[:, :1].astype(F32) < 3.0, cot_ref[...], 0.0).astype(BF)
    kept = []
    spread = Spread(
        wide,
        me,
        place,
        [
            (nall.at[place, SIDE], nall.at[:, SIDE], True),
            (nall.at[place, LINES[0]], nall.at[:, LINES[0]], False),
            (nall.at[place, LINES[1]], nall.at[:, LINES[1]], False),
            (tags.at[place], tags, False),
            (ball.at[place, SIDE], ball.at[:, SIDE], True),
            (ball.at[place, LINES[0]], ball.at[:, LINES[0]], False),
            (ball.at[place, LINES[1]], ball.at[:, LINES[1]], False),
        ],
        refs[9:],
    )
    for i in range(4):
        spread.begin(i)
    for j, (q, kind) in enumerate(pieces):
        if q >= OUTER:
            if j == 3 * cuts + 3:
                loads[cuts].wait()
            part_rows = pl.ds((q - OUTER) * height, height)
            wout[me, kind, part_rows] = stage_out[kind, part_rows].astype(BF)
        elif q == SMALL:
            wsmall[me, kind] = small_ref[kind].astype(BF)
        else:
            if kind == 0:
                loads[turns.index(q)].wait()
            wall[me, kind, :, q * narrow : (q + 1) * narrow] = stage[
                kind, :, q * narrow : (q + 1) * narrow
            ].astype(BF)
        if j < FLIGHT:
            for k in range(lines - 1):
                cross(k, j).start()
        pair(j).start()

    state = {"passed": 0}

    def pass_on(until):
        for j in range(state["passed"], min(until, len(pieces))):
            for k in range(lines - 1):
                cross(k, j).wait_recv()
                onward(k, j).start()
                if j < 3 * cuts and j + FLIGHT < len(pieces):
                    cross(k, j + FLIGHT).start()
                if j == 3 * cuts - 1:
                    for later in range(j + FLIGHT + 1, len(pieces)):
                        cross(k, later).start()
            state["passed"] = j + 1

    for hop in range(3):
        for i in range(4):
            spread.step(i, hop)
        pass_on(2 * (hop + 1))
    for i in range(4):
        spread.end(i)
    for i in range(4, 7):
        spread.begin(i)

    low = place // half
    home = place % half

    def deliver(q):
        return remote(
            mixed.at[q], xz.at[low, q % (cuts // 2)], h_send.at[q], h_recv.at[low, q % (cuts // 2)],
            (me, 2 * home + q // (cuts // 2)),
        )

    def stay(q):
        return pltpu.make_async_copy(mixed.at[q], xz.at[low, q % (cuts // 2)], h_local.at[q])

    blocks = TILE // count
    for turn, q in enumerate(turns):
        pass_on((turn + 1) * 3)
        for j in range(3 * turn, 3 * turn + 3):
            pair(j).wait_recv()
            for k in range(lines - 1):
                onward(k, j).wait_recv()

        def tile(t, carry, q=q):
            left = nall[pl.ds(t * blocks, blocks)].reshape(TILE, -1)
            tag = tags[pl.ds(t * blocks, blocks)].reshape(TILE, -1)[:, :1].astype(F32)
            total = jnp.zeros((TILE, narrow), F32)
            for kind in range(3):
                product = jnp.zeros((TILE, narrow), F32)
                for owner in range(dp):
                    product += jnp.dot(
                        left[:, owner * rows : (owner + 1) * rows],
                        wall[owner, kind, :, q * narrow : (q + 1) * narrow],
                        preferred_element_type=F32,
                    )
                total = total + jnp.where(tag == kind, product, 0.0)
            mixed[q, pl.ds(pl.multiple_of(t * TILE, TILE), TILE)] = total.astype(BF)
            return carry

        lax.fori_loop(0, span // TILE, tile, 0)
        target = 2 * home + q // (cuts // 2)

        @pl.when(target != place)
        def _(q=q):
            deliver(q).start()

        @pl.when(target == place)
        def _(q=q):
            stay(q).start()

        if turn > 0:
            for i in range(4, 7):
                spread.step(i, turn - 1)
        if turn == 0:
            mates = [me, me + 1 - 2 * core]
            for k in range(1, lines):
                far = lax.rem(line + k, lines) * 2
                mates += [far + core, far + 1 - core]
            sinks = [(tags, tags_out)]
            for k, mate in enumerate(mates):
                sinks.append((nall.at[:, :, pl.ds(pl.multiple_of(mate * rows, rows), rows)], feat_outs[k]))
            for origin, sink in sinks:
                kept.append(pltpu.make_async_copy(origin, sink, keep.at[len(kept)]))
                kept[-1].start()
    pass_on(3 * cuts + 3)
    kept.append(pltpu.make_async_copy(wall, wall_out, keep.at[len(kept)]))
    kept[-1].start()

    def arrive(kind, i):
        source = kind * half + place // 2
        q = place % 2 * (cuts // 2) + i

        @pl.when(source != place)
        def _():
            remote(mixed.at[0], xz.at[kind, i], h_send.at[0], h_recv.at[kind, i], partner).wait_recv()

        @pl.when(source == place)
        def _():
            pltpu.make_async_copy(mixed.at[q], xz.at[kind, i], h_local.at[q]).wait()

    channels = u_ref.shape[1]
    own = pl.ds(pl.multiple_of(place * channels, channels), channels)
    taps_all, bias_all = taps_ref[:, own], bias_ref[:, own]
    width = taps_all.shape[0]
    for i in range(cuts // 2):
        arrive(0, i)
        taps = taps_all[:, i * narrow : (i + 1) * narrow]
        bias = bias_all[:, i * narrow : (i + 1) * narrow]

        def conv(t, carry, i=i, taps=taps, bias=bias):
            at = pl.multiple_of(t * 128, 128)
            behind = pl.multiple_of(jnp.maximum(t * 128 - 16, 0), 16)
            here = xz[0, i, pl.ds(at, 128)].astype(F32)
            both = jnp.concatenate([xz[0, i, pl.ds(behind, 16)].astype(F32), here], axis=0)
            masks = masks_ref[pl.ds(at, 128)]
            pre = bias + taps[width - 1 : width] * here
            for offset in range(1, width):
                pre = pre + taps[width - 1 - offset : width - offset] * (
                    both[16 - offset : 144 - offset] * masks[:, offset : offset + 1]
                )
            u_ref[pl.ds(at, 128), i * narrow : (i + 1) * narrow] = (pre * jax.nn.sigmoid(pre)).astype(BF)
            return carry

        lax.fori_loop(0, span // 128, conv, 0)

    for j in range(3 * cuts, 3 * cuts + 3):
        pair(j).wait_recv()
        for k in range(lines - 1):
            onward(k, j).wait_recv()

    def project(t, carry):
        at = pl.multiple_of(t * TILE, TILE)
        inner = u_ref[pl.ds(at, TILE)].astype(F32)
        tag = tags[pl.ds(t * blocks, blocks)].reshape(TILE, -1)[:, :1].astype(F32)
        chosen = [jnp.where(tag == kind, inner, 0.0).astype(BF) for kind in range(3)]
        for owner in range(dp):
            total = jnp.zeros((wsmall.shape[2], TILE), F32)
            for kind in range(3):
                total += lax.dot_general(
                    wsmall[owner, kind], chosen[kind], (((1,), (1,)), ((), ())), preferred_element_type=F32
                )
            part[owner * rank_rows : (owner + 1) * rank_rows, pl.ds(at, TILE)] = total[:rank_rows]
        return carry

    pass_on(3 * cuts + 6)
    lax.fori_loop(0, span // TILE, project, 0)
    part_low[...] = part[...].astype(BF)

    def meanwhile():
        pass_on(len(pieces))
        for i in range(4, 7):
            for hop in range(cuts - 1, 3):
                spread.step(i, hop)
            spread.end(i)
        for j in range(3 * cuts + 3, len(pieces)):
            pair(j).wait_recv()
            for k in range(lines - 1):
                onward(k, j).wait_recv()
        for origin, sink in ((wout, wout_out), (ball, ball_out)):
            kept.append(pltpu.make_async_copy(origin, sink, keep.at[len(kept)]))
            kept[-1].start()

        def gate_back(t, carry):
            left = ball[pl.ds(t * blocks, blocks)].reshape(TILE, -1)
            tag = tags[pl.ds(t * blocks, blocks)].reshape(TILE, -1)[:, :1].astype(F32)
            total = jnp.zeros((TILE, channels), F32)
            for kind in range(3):
                product = jnp.zeros((TILE, channels), F32)
                for owner in range(dp):
                    product += jnp.dot(
                        left[:, owner * wout.shape[2] : (owner + 1) * wout.shape[2]],
                        wout[owner, kind],
                        preferred_element_type=F32,
                    )
                total = total + jnp.where(tag == kind, product, 0.0)
            dgated_ref[pl.ds(pl.multiple_of(t * TILE, TILE), TILE)] = total.astype(BF)
            return carry

        lax.fori_loop(0, span // TILE, gate_back, 0)

    sum_over_wide(wide, me, place, part_low, proj_ref, got, whole, s1, r1, s2, r2, meanwhile)

    step_rows = wdt_ref.shape[1] // dp
    rank = rank_rows * dp
    for kind in range(3):
        for owner in range(dp):
            rows_here = wsmall[owner, kind].astype(F32)
            tall[owner * rank_rows : (owner + 1) * rank_rows] = rows_here[:rank_rows]
            tall[rank + owner * step_rows : rank + (owner + 1) * step_rows] = rows_here[rank_rows : rank_rows + step_rows]
        wx_ref[kind] = tall[:rank].astype(BF)
        wdt_ref[kind] = tall[rank:].astype(BF)
    for i in range(cuts // 2):
        arrive(1, i)
    for i in range(cuts // 2):
        xs_out[:, i * narrow : (i + 1) * narrow] = xz[0, i]
        z_out[:, i * narrow : (i + 1) * narrow] = xz[1, i]
    for j in range(len(pieces)):
        pair(j).wait_send()
        for k in range(lines - 1):
            cross(k, j).wait_send()
            onward(k, j).wait_send()
    spread.sent()
    for q in range(cuts):

        @pl.when(2 * home + q // (cuts // 2) != place)
        def _(q=q):
            deliver(q).wait_send()

    for copy in kept:
        copy.wait()


def front(win, wout, small, x, cotangent, gain, tag, masks, taps, bias, rank_rows, step_rows, collective_id):
    dp, wide = lax.axis_size("dp"), lax.axis_size("wide")
    kinds, rows, columns = win.shape
    cuts = 4 if columns >= 512 else 2
    narrow = columns // cuts
    count, depth = x.shape
    span = count * wide
    channels = small.shape[2]
    rank = rank_rows * dp
    lines = dp // 2
    pieces = 3 * cuts + 9
    vmem = pl.BlockSpec(memory_space=pltpu.VMEM)
    anywhere = pl.BlockSpec(memory_space=pl.ANY)
    dma = pltpu.SemaphoreType.DMA
    shape = jax.ShapeDtypeStruct
    far, near = dma((lines - 1, pieces)), dma((pieces,))
    hops = dma((3, 7, 2))
    every = dma((4, 7)) if wide == 8 else dma((wide, 7))
    return pl.pallas_call(
        functools.partial(front_kernel, dp, wide, rank_rows),
        out_shape=[
            *[shape((wide, count, rows), BF) for _ in range(dp)],
            shape((dp, 3, rows, columns), BF),
            shape((dp,) + wout.shape, BF),
            shape((wide, count, depth), BF),
            shape((wide,) + tag.shape, BF),
            shape((3, rank, channels), BF),
            shape((3, step_rows * dp, channels), BF),
            shape((span, channels), BF),
            shape((span, channels), BF),
            shape((span, channels), BF),
            shape((span, channels), BF),
            shape((rank, span), BF),
        ],
        in_specs=[anywhere] * 2 + [vmem] * 8,
        out_specs=[anywhere] * (dp + 4) + [vmem] * 7,
        scratch_shapes=[
            pltpu.VMEM(win.shape, F32),
            pltpu.VMEM(wout.shape, F32),
            pltpu.VMEM((dp,) + wout.shape, BF),
            pltpu.VMEM((dp, 3, rows, columns), BF),
            pltpu.VMEM((dp,) + small.shape, BF),
            pltpu.VMEM((wide, count, depth), BF),
            pltpu.VMEM((wide, count, depth), BF),
            pltpu.VMEM((wide,) + tag.shape, BF),
            pltpu.VMEM((cuts, span, narrow), BF),
            pltpu.VMEM((2, cuts // 2, span, narrow), BF),
            pltpu.VMEM((rank, span), F32),
            pltpu.VMEM((rank, span), BF),
            pltpu.VMEM((wide, rank, count), BF),
            pltpu.VMEM((rank, count), BF),
            pltpu.VMEM((rank + step_rows * dp, channels), F32),
            far, far, near, near, far, far,
            dma((cuts,)), dma((2, cuts // 2)), dma((cuts,)), dma((cuts + 1,)), dma((dp + 4,)),
            dma((wide,)), dma((wide,)), dma((wide,)), dma((wide,)),
            hops, hops, hops, hops, every, every,
        ],
        compiler_params=pltpu.CompilerParams(
            collective_id=collective_id, has_side_effects=True, vmem_limit_bytes=60 << 20
        ),
        name="front",
    )(win, wout, small, x, cotangent, gain, tag, masks, taps, bias)


def sum_wide_kernel(wide, x_ref, out_ref, got, whole, s1, r1, s2, r2):
    me, place = lax.axis_index("dp"), lax.axis_index("wide")
    step = out_ref.shape[1] // wide
    barrier = pltpu.get_barrier_semaphore()
    peers = [lax.rem(place + k, wide) for k in range(1, wide)]
    for peer in peers:
        pl.semaphore_signal(barrier, inc=1, device_id=(me, peer), device_id_type=MESH)
    pl.semaphore_wait(barrier, wide - 1)

    def columns(index):
        return pl.ds(pl.multiple_of(index * step, step), step)

    def give(k):
        return pltpu.make_async_remote_copy(
            src_ref=x_ref.at[:, columns(peers[k - 1])],
            dst_ref=got.at[k],
            send_sem=s1.at[k],
            recv_sem=r1.at[k],
            device_id=(me, peers[k - 1]),
            device_id_type=MESH,
        )

    def spread(k):
        return pltpu.make_async_remote_copy(
            src_ref=whole,
            dst_ref=out_ref.at[:, columns(place)],
            send_sem=s2.at[k],
            recv_sem=r2.at[k],
            device_id=(me, peers[k - 1]),
            device_id_type=MESH,
        )

    order = sorted(range(1, wide), key=lambda k: -min(k, wide - k))
    for k in order:
        give(k).start()
    total = x_ref[:, columns(place)].astype(F32)
    for k in reversed(order):
        give(k).wait_recv()
        total = total + got[k].astype(F32)
    whole[...] = total.astype(BF)
    for k in order:
        spread(k).start()
    out_ref[:, columns(place)] = whole[...]
    for k in range(1, wide):
        spread(k).wait()
        give(k).wait_send()


def sum_wide(x, collective_id):
    wide = lax.axis_size("wide")
    rows, span = x.shape
    vmem = pl.BlockSpec(memory_space=pltpu.VMEM)
    dma = pltpu.SemaphoreType.DMA
    return pl.pallas_call(
        functools.partial(sum_wide_kernel, wide),
        out_shape=jax.ShapeDtypeStruct((rows, span), BF),
        in_specs=[vmem],
        out_specs=vmem,
        scratch_shapes=[
            pltpu.VMEM((wide, rows, span // wide), x.dtype),
            pltpu.VMEM((rows, span // wide), BF),
            dma((wide,)),
            dma((wide,)),
            dma((wide,)),
            dma((wide,)),
        ],
        compiler_params=pltpu.CompilerParams(
            collective_id=collective_id, has_side_effects=True, vmem_limit_bytes=32 << 20
        ),
        name="sum_wide",
    )(x)

def finish_kernel(dp, wide, part_ref, table_ref, small_ref, rows_ref, tables_ref, sums_ref, *refs):
    flow_a, flow_b, got_tables, got_small = refs[:4]
    a_send, a_recv, b_send, b_recv, t_send, t_recv, s_send, s_recv, w_send, w_recv = refs[4:]
    me, place = lax.axis_index("dp"), lax.axis_index("wide")
    position = ring_position(place, wide)
    after = (me, ring_index(lax.rem(position + 1, wide), wide))
    before = (me, ring_index(lax.rem(position + wide - 1, wide), wide))
    mates = [lax.rem(me + k, dp) for k in range(1, dp)]
    peers = [lax.rem(place + k, wide) for k in range(1, wide)]
    barrier = pltpu.get_barrier_semaphore()
    for mate in mates:
        pl.semaphore_signal(barrier, inc=1, device_id=(mate, place), device_id_type=MESH)
    for peer in peers:
        pl.semaphore_signal(barrier, inc=1, device_id=(me, peer), device_id_type=MESH)
    pl.semaphore_wait(barrier, dp + wide - 2)

    def remote(source, target, send, recv, device):
        return pltpu.make_async_remote_copy(
            src_ref=source, dst_ref=target, send_sem=send, recv_sem=recv, device_id=device, device_id_type=MESH
        )

    half = part_ref.shape[2] // 2
    cut = half // CUTS

    def columns(side, i):
        return pl.ds(side * half + i * cut, cut)

    def owner(side, hop):
        step = position + wide - 1 - hop if side == 0 else position + 1 + hop
        return ring_index(lax.rem(step, wide), wide)

    flows = ((flow_a, a_send, a_recv, after), (flow_b, b_send, b_recv, before))

    def turn(side, hop, i):
        flow, send, recv, device = flows[side]
        if hop == 0:
            source = part_ref.at[owner(side, 0), :, columns(side, i)]
        else:
            source = flow.at[hop - 1, i]
        return remote(source, flow.at[hop, i], send.at[hop, i], recv.at[hop, i], device)

    for i in range(CUTS):
        for side in range(2):
            turn(side, 0, i).start()

    def lend_table(k):
        return remote(table_ref, got_tables.at[k], t_send.at[k], t_recv.at[k], (mates[k], place))

    def lend_small(k):
        return remote(small_ref.at[mates[k]], got_small.at[k], s_send.at[k], s_recv.at[k], (mates[k], place))

    def show(k):
        return remote(tables_ref.at[place], tables_ref.at[place], w_send.at[k], w_recv.at[k], (me, peers[k]))

    for k in range(dp - 1):
        lend_table(k).start()
    for k in range(dp - 1):
        lend_small(k).start()

    for hop in range(1, wide):
        for i in range(CUTS):
            for side in range(2):
                turn(side, hop - 1, i).wait_recv()
                flow = flows[side][0]
                own = part_ref[owner(side, hop), :, columns(side, i)].astype(F32)
                total = flow[hop - 1, i].astype(F32) + own
                if hop < wide - 1:
                    flow[hop - 1, i] = total.astype(BF)
                    turn(side, hop, i).start()
                else:
                    rows_ref[:, columns(side, i)] = total
        if hop == 1:
            total = table_ref[...]
            for k in range(dp - 1):
                lend_table(k).wait_recv()
                total = total + got_tables[k]
            tables_ref[place] = total
            for k in range(wide - 1):
                show(k).start()
        if hop == min(3, wide - 1):
            for kind in range(3):
                sums_ref[kind] = small_ref[me, kind].astype(F32)
            for k in range(dp - 1):
                lend_small(k).wait_recv()
                for kind in range(3):
                    sums_ref[kind] += got_small[k, kind].astype(F32)

    for k in range(dp - 1):
        lend_table(k).wait_send()
        lend_small(k).wait_send()
    for k in range(wide - 1):
        show(k).wait()
    for hop in range(wide - 1):
        for i in range(CUTS):
            for side in range(2):
                turn(side, hop, i).wait_send()


def finish(part, table, small, collective_id):
    dp, wide = lax.axis_size("dp"), lax.axis_size("wide")
    rows, depth = part.shape[1:]
    vmem = pl.BlockSpec(memory_space=pltpu.VMEM)
    dma = pltpu.SemaphoreType.DMA
    flow = pltpu.VMEM((wide - 1, CUTS, rows, depth // 2 // CUTS), BF)
    hops = dma((wide - 1, CUTS))
    return pl.pallas_call(
        functools.partial(finish_kernel, dp, wide),
        out_shape=[
            jax.ShapeDtypeStruct((rows, depth), F32),
            jax.ShapeDtypeStruct((wide,) + table.shape, F32),
            jax.ShapeDtypeStruct(small.shape[1:], F32),
        ],
        in_specs=[vmem] * 3,
        out_specs=[vmem] * 3,
        scratch_shapes=[
            flow,
            flow,
            pltpu.VMEM((dp - 1,) + table.shape, F32),
            pltpu.VMEM((dp - 1,) + small.shape[1:], small.dtype),
            hops,
            hops,
            hops,
            hops,
            dma((dp - 1,)),
            dma((dp - 1,)),
            dma((dp - 1,)),
            dma((dp - 1,)),
            dma((wide - 1,)),
            dma((wide - 1,)),
        ],
        compiler_params=pltpu.CompilerParams(
            collective_id=collective_id, has_side_effects=True, vmem_limit_bytes=56 << 20
        ),
        name="finish",
    )(part, table, small)


def back_kernel(dp, wide, rank_rows, step_rows, *refs):
    feat_refs, kind_refs, normed_refs, refs = refs[:dp], refs[dp : 2 * dp], refs[2 * dp : 3 * dp], refs[3 * dp :]
    win_ref, ddtp_ref, dscan_ref, dz_ref, xs_ref, u_ref, refs = *refs[:6], refs[6:]
    dmaps_ref, rates_ref, wx_ref, wdt_ref, tags_ref, line_ref, masks_ref, taps_ref, bias_ref, extra_ref, refs = (
        *refs[:10],
        refs[10:],
    )
    ingrad_ref, rows_ref, tables_ref, sums_ref, refs = *refs[:4], refs[4:]
    wall, feats, nbuf, part, got, whole, dproj, dpre, leave, gm, dn, refs = *refs[:11], refs[11:]
    first, flow_a, flow_b, stage, table, got_tables, dt_grad, small, got_small, refs = *refs[:9], refs[9:]
    s1, r1, s2, r2, load, nload, d_send, d_recv, d_local, refs = *refs[:9], refs[9:]
    x_send, x_recv, core_send, core_recv, on_send, on_recv, o_send, refs = *refs[:7], refs[7:]
    a_send, a_recv, b_send, b_recv, t_send, t_recv, l_send, l_recv, w_send, w_recv = refs
    me, place = lax.axis_index("dp"), lax.axis_index("wide")
    _, cuts, span, narrow = gm.shape
    channels = xs_ref.shape[1]
    rows = win_ref.shape[2]
    count, depth = rows_ref.shape
    half = wide // 2
    quarters = cuts // 2
    low, home = place // half, place % half
    lines = dp // 2
    line, core = me // 2, me % 2
    partner = (me + 1 - 2 * core, place)
    across = [(lax.rem(line + k, lines) * 2 + core, place) for k in range(1, lines)]
    mates = [lax.rem(me + k, dp) for k in range(1, dp)]
    peers = [lax.rem(place + k, wide) for k in range(1, wide)]
    position = ring_position(place, wide)
    after = (me, ring_index(lax.rem(position + 1, wide), wide))
    before = (me, ring_index(lax.rem(position + wide - 1, wide), wide))
    barrier = pltpu.get_barrier_semaphore()
    for peer in [(mate, place) for mate in mates] + [(me, peer) for peer in peers]:
        pl.semaphore_signal(barrier, inc=1, device_id=peer, device_id_type=MESH)
    pl.semaphore_wait(barrier, dp + wide - 2)

    loads = [pltpu.make_async_copy(win_ref, wall, load.at[dp])]
    for k in range(dp):
        loads.append(pltpu.make_async_copy(feat_refs[k], feats.at[k], load.at[k]))
    for copy in loads:
        copy.start()

    def slot(i):
        return place % 2 * quarters + i

    def source(kind, i):
        if kind == 0:
            return leave.at[i]
        return dz_ref.at[:, pl.ds(i * narrow, narrow)]

    def deliver(kind, i):
        target = (me, kind * half + place // 2)
        return remote(source(kind, i), gm.at[me, slot(i)], d_send.at[kind, i], d_recv.at[slot(i)], target)

    def stay(kind, i):
        return pltpu.make_async_copy(source(kind, i), gm.at[me, slot(i)], d_local.at[i])

    def hand_over(kind, i):
        @pl.when(kind * half + place // 2 != place)
        def _():
            deliver(kind, i).start()

        @pl.when(kind * half + place // 2 == place)
        def _():
            stay(kind, i).start()

    def arrive(q):
        sender = 2 * home + q // quarters

        @pl.when(sender != place)
        def _():
            remote(leave.at[0], gm.at[me, q], d_send.at[0, 0], d_recv.at[q], partner).wait_recv()

        @pl.when(sender == place)
        def _():
            pltpu.make_async_copy(leave.at[0], gm.at[me, q], d_local.at[q % quarters]).wait()

    blocks = TILE // count
    steps = wdt_ref.shape[1]

    def columns(index):
        return pl.ds(pl.multiple_of(index * count, count), count)

    def give(k):
        device = (me, peers[k - 1])
        return remote(part.at[:, columns(peers[k - 1])], got.at[k], s1.at[k], r1.at[k], device)

    def share(k):
        device = (me, peers[k - 1])
        return remote(whole, dproj.at[:, columns(place)], s2.at[k], r2.at[k], device)

    def rates_back(t, carry):
        at = pl.ds(pl.multiple_of(t * TILE, TILE), TILE)
        tag = tags_ref[pl.ds(t * blocks, blocks)].reshape(TILE, -1)[:, :1].astype(F32)
        value = ddtp_ref[at].astype(F32)
        total = jnp.zeros((steps, TILE), F32)
        for kind in range(3):
            total += lax.dot_general(
                wdt_ref[kind],
                jnp.where(tag == kind, value, 0.0).astype(BF),
                (((1,), (1,)), ((), ())),
                preferred_element_type=F32,
            )
        part[:steps, at] = total.astype(BF)
        return carry

    lax.fori_loop(0, span // TILE, rates_back, 0)
    part[steps:] = dmaps_ref[...].astype(BF)
    order = sorted(range(1, wide), key=lambda k: -min(k, wide - k))
    for k in order:
        give(k).start()
    dn[...] = jnp.zeros_like(dn)
    dpre[span:] = jnp.zeros_like(dpre[span:])
    width = taps_ref.shape[0]
    states = extra_ref.shape[0] - 1
    table[...] = jnp.zeros_like(table)
    table[width + 1 : width + 2 + states] = extra_ref[...]
    dead = line_ref[0:1].astype(F32)
    for kind in range(3):
        chosen_rates = jnp.where(dead == kind, rates_ref[:steps].astype(F32), 0.0).astype(BF)
        grad = jnp.dot(chosen_rates, ddtp_ref[...], preferred_element_type=F32)
        dt_grad[kind] = grad
        picked = jnp.where(line_ref[...].astype(F32) == kind, 1.0, 0.0).astype(BF)
        at = width + 2 + states + kind
        table[at : at + 1] = jnp.dot(picked, ddtp_ref[...], preferred_element_type=F32)[:1]
    total = part[:, columns(place)].astype(F32)
    for k in reversed(order):
        give(k).wait_recv()
        total = total + got[k].astype(F32)
    whole[...] = total.astype(BF)
    for k in order:
        share(k).start()
    dproj[:, columns(place)] = whole[...]
    for k in range(1, wide):
        share(k).wait_recv()
    for i in range(quarters):
        hand_over(1, i)

    own = pl.ds(pl.multiple_of(place * channels, channels), channels)
    taps_all, conv_bias = taps_ref[:, own], bias_ref[:, own]

    def through(t, carry):
        at = pl.multiple_of(t * 128, 128)
        behind = pl.multiple_of(jnp.maximum(t * 128 - 16, 0), 16)
        tag = tags_ref[pl.ds(t * 128 // count, 128 // count)].reshape(128, -1)[:, :1].astype(F32)
        piece = dproj[:, pl.ds(at, 128)]
        du = jnp.zeros((128, channels), F32)
        for kind in range(3):
            product = lax.dot_general(
                piece, wx_ref[kind], (((0,), (0,)), ((), ())), preferred_element_type=F32
            )
            du = du + jnp.where(tag == kind, product, 0.0)
        du = du.astype(BF).astype(F32) + dscan_ref[pl.ds(at, 128)]
        here = xs_ref[pl.ds(at, 128)].astype(F32)
        both = jnp.concatenate([xs_ref[pl.ds(behind, 16)].astype(F32), here], axis=0)
        masks = masks_ref[pl.ds(at, 128)]
        terms = [here] + [both[16 - k : 144 - k] * masks[:, k : k + 1] for k in range(1, width)]
        pre = conv_bias
        for k in range(width):
            pre = pre + taps_all[width - 1 - k : width - k] * terms[k]
        sigma = jax.nn.sigmoid(pre)
        slope = du * (sigma * (1.0 + pre * (1.0 - sigma)))
        dpre[pl.ds(at, 128)] = slope
        for k in range(width):
            table[width - 1 - k : width - k] += jnp.sum(slope * terms[k], axis=0, keepdims=True)
        table[width : width + 1] += jnp.sum(slope, axis=0, keepdims=True)
        return carry

    lax.fori_loop(0, span // 128, through, 0)

    for i in range(quarters):
        lanes = slice(i * narrow, (i + 1) * narrow)

        def conv_back(t, carry, i=i, lanes=lanes):
            at = pl.multiple_of(t * 128, 128)
            ahead = pl.multiple_of(t * 128 + 128, 16)
            known = pl.multiple_of(jnp.minimum(t * 128 + 128, span - 16), 16)
            here = dpre[pl.ds(at, 128), lanes]
            both = jnp.concatenate([here, dpre[pl.ds(ahead, 16), lanes]], axis=0)
            masks = jnp.concatenate([masks_ref[pl.ds(at, 128)], masks_ref[pl.ds(known, 16)]], axis=0)
            back = taps_all[width - 1 : width, lanes] * here
            for k in range(1, width):
                masked = both * masks[:, k : k + 1]
                back = back + taps_all[width - 1 - k : width - k, lanes] * masked[k : 128 + k]
            leave[i, pl.ds(at, 128)] = back.astype(BF)
            return carry

        lax.fori_loop(0, span // 128, conv_back, 0)
        hand_over(0, i)

    for kind in range(3):
        chosen_proj = jnp.where(dead == kind, dproj[...].astype(F32), 0.0).astype(BF)
        grad = jnp.dot(chosen_proj, u_ref[...], preferred_element_type=F32)
        filler = jnp.zeros((small.shape[2] - rank_rows - step_rows, channels), F32)
        for owner in range(dp):
            ranks = grad[owner * rank_rows : (owner + 1) * rank_rows]
            sizes = dt_grad[kind, owner * step_rows : (owner + 1) * step_rows]
            small[owner, kind] = jnp.concatenate([ranks, sizes, filler], axis=0).astype(BF)

    def lend_table(k):
        return remote(table, got_tables.at[k], t_send.at[k], t_recv.at[k], (mates[k], place))

    def lend_small(k):
        return remote(small.at[mates[k]], got_small.at[k], l_send.at[k], l_recv.at[k], (mates[k], place))

    for k in range(dp - 1):
        lend_small(k).start()

    def cross(k, q):
        return remote(gm.at[me, q], gm.at[me, q], x_send.at[k, q], x_recv.at[k, q], across[k])

    def pair(q):
        return remote(gm.at[me, q], gm.at[me, q], core_send.at[q], core_recv.at[q], partner)

    def onward(k, q):
        owner = lax.rem(line + lines - 1 - k, lines) * 2 + core
        return remote(gm.at[owner, q], gm.at[owner, q], on_send.at[k, q], on_recv.at[k, q], partner)

    def pass_on(q):
        for k in range(lines - 1):
            cross(k, q).wait_recv()
            onward(k, q).start()

    owners = [me, me + 1 - 2 * core]
    for k in range(1, lines):
        far = lax.rem(line + k, lines) * 2
        owners += [far + core, far + 1 - core]

    outs = []

    def master_grad(number, q):
        pair(q).wait_recv()
        for k in range(lines - 1):
            onward(k, q).wait_recv()
        if len(outs) >= 2:
            outs[number - 2].wait()

        def one_kind(kind, carry):
            total = jnp.zeros((rows, narrow), F32)
            for k, owner in enumerate(owners):
                tag = kind_refs[k][...].astype(F32)
                right = jnp.where(tag == kind.astype(F32), gm[owner, q].astype(F32), 0.0).astype(BF)
                total += lax.dot_general(feats[k], right, (((0,), (0,)), ((), ())), preferred_element_type=F32)
            stage[number % 2, kind] = total
            return carry

        lax.fori_loop(0, 3, one_kind, 0)
        out = pltpu.make_async_copy(
            stage.at[number % 2], ingrad_ref.at[:, :, pl.ds(q * narrow, narrow)], o_send.at[number % 2]
        )
        out.start()
        outs.append(out)

    turns = [h * quarters + i for i in range(quarters) for h in range(2)]
    for copy in loads:
        copy.wait()
    for number, q in enumerate(turns):
        arrive(q)
        for k in range(lines - 1):
            cross(k, q).start()
        pair(q).start()

        def pick(t, carry, q=q):
            at = pl.ds(pl.multiple_of(t * TILE, TILE), TILE)
            tag = tags_ref[pl.ds(t * blocks, blocks)].reshape(TILE, -1)[:, :1].astype(F32)
            value = gm[me, q, at].astype(F32)
            left = [jnp.where(tag == kind, value, 0.0).astype(BF) for kind in range(3)]
            for owner in range(dp):
                total = dn[at, owner * rows : (owner + 1) * rows]
                for kind in range(3):
                    total += lax.dot_general(
                        left[kind],
                        wall[owner, kind, :, q * narrow : (q + 1) * narrow],
                        (((1,), (1,)), ((), ())),
                        preferred_element_type=F32,
                    )
                dn[at, owner * rows : (owner + 1) * rows] = total
            return carry

        lax.fori_loop(0, span // TILE, pick, 0)
        if 0 < number < cuts - 1:
            pass_on(turns[number - 1])
        if 1 < number < cuts - 1:
            master_grad(number - 2, turns[number - 2])

    half_columns = depth // 2
    cut = half_columns // CUTS

    def lanes_of(side, i):
        return slice(side * half_columns + i * cut, side * half_columns + (i + 1) * cut)

    def block(side, hop):
        step = position + wide - 1 - hop if side == 0 else position + 1 + hop
        owner = ring_index(lax.rem(step, wide), wide)
        return pl.ds(pl.multiple_of(owner * count, count), count)

    flows = ((flow_a, a_send, a_recv, after), (flow_b, b_send, b_recv, before))

    def turn(side, hop, i):
        flow, send, recv, device = flows[side]
        origin = first.at[side, i] if hop == 0 else flow.at[hop - 1, i]
        return remote(origin, flow.at[hop, i], send.at[hop, i], recv.at[hop, i], device)

    for i in range(CUTS):
        for side in range(2):
            first[side, i] = dn[block(side, 0), lanes_of(side, i)].astype(BF)
            turn(side, 0, i).start()

    def normed_copy(b):
        rows_of = normed_refs[b // 2].at[pl.ds(b % 2 * half, half)]
        return pltpu.make_async_copy(rows_of, nbuf.at[b % 2], nload.at[b % 2])

    normed_copy(0).start()
    pass_on(turns[cuts - 2])
    for k, owner in enumerate(owners):
        gain = jnp.zeros((1, rows), F32)
        lanes = pl.ds(pl.multiple_of(owner * rows, rows), rows)
        for h in range(2):
            b = 2 * k + h
            if b + 1 < 2 * dp:
                normed_copy(b + 1).start()
            normed_copy(b).wait()
            normed = nbuf[h].reshape(half * count, rows).astype(F32)
            part_rows = dn[h * half * count : (h + 1) * half * count, lanes]
            gain = gain + jnp.sum(part_rows * normed, axis=0, keepdims=True)
        for r in range(rows // channels):
            at = width + 5 + states + owner * (rows // channels) + r
            table[pl.ds(at, 1)] = gain[:, r * channels : (r + 1) * channels]
    for k in range(dp - 1):
        lend_table(k).start()

    def show(k):
        return remote(tables_ref.at[place], tables_ref.at[place], w_send.at[k], w_recv.at[k], (me, peers[k]))

    for hop in range(1, wide):
        for i in range(CUTS):
            for side in range(2):
                turn(side, hop - 1, i).wait_recv()
                flow = flows[side][0]
                total = flow[hop - 1, i].astype(F32) + dn[block(side, hop), lanes_of(side, i)]
                if hop < wide - 1:
                    flow[hop - 1, i] = total.astype(BF)
                    turn(side, hop, i).start()
                else:
                    rows_ref[:, lanes_of(side, i)] = total
        if hop == 1:
            master_grad(cuts - 3, turns[cuts - 3])
            pass_on(turns[cuts - 1])
        if hop == 2:
            total = table[...]
            for k in range(dp - 1):
                lend_table(k).wait_recv()
                total = total + got_tables[k]
            tables_ref[place] = total
            for k in range(wide - 1):
                show(k).start()
        if hop == 3:
            master_grad(cuts - 2, turns[cuts - 2])
        if hop == 5:
            master_grad(cuts - 1, turns[cuts - 1])
        if hop == 4:
            for kind in range(3):
                sums_ref[kind] = small[me, kind].astype(F32)
            for k in range(dp - 1):
                lend_small(k).wait_recv()
                for kind in range(3):
                    sums_ref[kind] += got_small[k, kind].astype(F32)

    for k in range(dp - 1):
        lend_table(k).wait_send()
        lend_small(k).wait_send()
    for k in range(wide - 1):
        show(k).wait()
    for k in range(1, wide):
        share(k).wait_send()
        give(k).wait_send()
    for hop in range(wide - 1):
        for i in range(CUTS):
            for side in range(2):
                turn(side, hop, i).wait_send()
    for q in range(cuts):
        pair(q).wait_send()
        for k in range(lines - 1):
            cross(k, q).wait_send()
            onward(k, q).wait_send()
    for kind in range(2):
        for i in range(quarters):

            @pl.when(kind * half + place // 2 != place)
            def _(kind=kind, i=i):
                deliver(kind, i).wait_send()

    for out in outs[-2:]:
        out.wait()


def back(win, feats, normed, kinds, count, vmem_args, rank_rows, step_rows, collective_id):
    dp, wide = lax.axis_size("dp"), lax.axis_size("wide")
    _, _, rows, columns = win.shape
    depth = rows * dp
    cuts = 4
    narrow = columns // cuts
    quarters = cuts // 2
    span, channels = vmem_args[0].shape
    rank, steps = vmem_args[6].shape[0], vmem_args[8].shape[1]
    extra, width = vmem_args[14], vmem_args[12].shape[0]
    lines = dp // 2
    table_rows = width + 4 + extra.shape[0] + depth // channels
    table_rows += -table_rows % 8
    small_rows = rank_rows + step_rows
    small_rows += -small_rows % 16
    vmem = pl.BlockSpec(memory_space=pltpu.VMEM)
    anywhere = pl.BlockSpec(memory_space=pl.ANY)
    dma = pltpu.SemaphoreType.DMA
    shape = jax.ShapeDtypeStruct
    flow = pltpu.VMEM((wide - 1, CUTS, count, depth // 2 // CUTS), BF)
    hops, far, near = dma((wide - 1, CUTS)), dma((lines - 1, cuts)), dma((cuts,))
    mates, peers = dma((dp - 1,)), dma((wide,))
    return pl.pallas_call(
        functools.partial(back_kernel, dp, wide, rank_rows, step_rows),
        out_shape=[
            shape((3, rows, columns), F32),
            shape((count, depth), F32),
            shape((wide, table_rows, channels), F32),
            shape((3, small_rows, channels), F32),
        ],
        in_specs=[anywhere] * dp + [vmem] * dp + [anywhere] * (dp + 1) + [vmem] * len(vmem_args),
        out_specs=[anywhere] + [vmem] * 3,
        scratch_shapes=[
            pltpu.VMEM(win.shape, BF),
            pltpu.VMEM((dp,) + feats[0].shape, BF),
            pltpu.VMEM((2, wide // 2, count, rows), BF),
            pltpu.VMEM((rank, span), BF),
            pltpu.VMEM((wide, rank, count), BF),
            pltpu.VMEM((rank, count), BF),
            pltpu.VMEM((rank, span), BF),
            pltpu.VMEM((span + 16, channels), F32),
            pltpu.VMEM((quarters, span, narrow), BF),
            pltpu.VMEM((dp, cuts, span, narrow), BF),
            pltpu.VMEM((span, depth), F32),
            pltpu.VMEM((2, CUTS, count, depth // 2 // CUTS), BF),
            flow,
            flow,
            pltpu.VMEM((2, 3, rows, narrow), F32),
            pltpu.VMEM((table_rows, channels), F32),
            pltpu.VMEM((dp - 1, table_rows, channels), F32),
            pltpu.VMEM((3, steps, channels), F32),
            pltpu.VMEM((dp, 3, small_rows, channels), BF),
            pltpu.VMEM((dp - 1, 3, small_rows, channels), BF),
            peers, peers, peers, peers, dma((dp + 1,)), dma((2,)), dma((2, quarters)), near, dma((quarters,)),
            far, far, near, near, far, far, dma((2,)),
            hops, hops, hops, hops, mates, mates, mates, mates, peers, peers,
        ],
        compiler_params=pltpu.CompilerParams(
            collective_id=collective_id, has_side_effects=True, vmem_limit_bytes=62 << 20
        ),
        cost_estimate=pl.CostEstimate(
            flops=48 * span * depth * columns, bytes_accessed=40 << 20, transcendentals=span * channels
        ),
        name="back",
    )(*feats, *kinds, *normed, win, *vmem_args)


def branch_kernel(gated_ref, tag_ref, w_ref, branch_ref):
    dp, kinds, rows, channels = w_ref.shape
    tag = tag_ref[...][:, :1].astype(F32)
    gated = gated_ref[...].astype(F32)
    chosen = [jnp.where(tag == kind, gated, 0.0).astype(BF) for kind in range(3)]
    for owner in range(dp):
        branch = jnp.zeros((gated.shape[0], rows), F32)
        for kind in range(3):
            branch += lax.dot_general(
                chosen[kind], w_ref[owner, kind], (((1,), (1,)), ((), ())), preferred_element_type=F32
            )
        branch_ref[:, owner * rows : (owner + 1) * rows] = branch.astype(BF)


def branch_of(gated, tags, w_out, depth):
    span, channels = gated.shape
    tile = lambda lanes: pl.BlockSpec((TILE, lanes), lambda t: (t, 0))
    return pl.pallas_call(
        branch_kernel,
        grid=(span // TILE,),
        out_shape=jax.ShapeDtypeStruct((span, depth), BF),
        in_specs=[tile(channels), tile(tags.shape[1]), pl.BlockSpec(memory_space=pltpu.VMEM)],
        out_specs=tile(depth),
        compiler_params=pltpu.CompilerParams(vmem_limit_bytes=40 << 20),
        cost_estimate=pl.CostEstimate(
            flops=6 * span * channels * depth, bytes_accessed=12 << 20, transcendentals=0
        ),
        name="branch",
    )(gated, tags, w_out)


def gate_kernel(dp, back_ref, gated_ref, tag_ref, mine_ref, theirs_ref):
    lines, kinds, rows, channels = mine_ref.shape
    me = lax.axis_index("dp")

    def grad(k, carry):
        line = lax.rem(me // 2 + k, lines) * 2
        for core, out_ref in ((me % 2, mine_ref), (1 - me % 2, theirs_ref)):
            columns = pl.ds(pl.multiple_of((line + core) * rows, rows), rows)
            for kind in range(3):
                tag = tag_ref[...][:, :1].astype(F32)
                chosen = jnp.where(tag == kind, gated_ref[...].astype(F32), 0.0).astype(BF)
                out_ref[k, kind] = lax.dot_general(
                    back_ref[:, columns], chosen, (((0,), (0,)), ((), ())), preferred_element_type=F32
                ).astype(BF)
        return carry

    lax.fori_loop(0, lines, grad, 0)


def gate(back, gated, tags, dp):
    span, channels = gated.shape
    vmem = pl.BlockSpec(memory_space=pltpu.VMEM)
    part = jax.ShapeDtypeStruct((dp // 2, 3, back.shape[1] // dp, channels), BF)
    return pl.pallas_call(
        functools.partial(gate_kernel, dp),
        out_shape=[part, part],
        in_specs=[vmem] * 3,
        out_specs=[vmem] * 2,
        compiler_params=pltpu.CompilerParams(vmem_limit_bytes=58 << 20),
        cost_estimate=pl.CostEstimate(
            flops=6 * span * channels * back.shape[1], bytes_accessed=12 << 20, transcendentals=0
        ),
        name="gate",
    )(back, gated, tags)


def contract(left, right, left_dim, right_dim):
    return lax.dot_general(
        left, right, (((left_dim,), (right_dim,)), ((), ())), preferred_element_type=F32
    )


def segment_of(places, bounds):
    return jnp.sum((places[:, None] >= bounds[None, :]).astype(jnp.int32), axis=1)


def conv_masks(places, bounds, width):
    segment = segment_of(places, bounds)
    return [
        ((places >= offset) & (segment_of(places - offset, bounds) == segment)).astype(F32)
        for offset in range(width)
    ]


def silu_slope(values):
    sigma = jax.nn.sigmoid(values)
    return sigma * (1.0 + values * (1.0 - sigma))


def split_kinds(rows, kinds, parts):
    count, depth = rows.shape
    pieces = rows.reshape(count, parts, 1, depth // parts)
    picked = kinds[:, None, :, None]
    return jnp.where(picked, pieces, jnp.zeros((), rows.dtype)).reshape(count, 3 * depth)


def hop(block, flip):
    devices = lax.axis_size("dp")
    return lax.ppermute(block, "dp", [(d, flip(d)) for d in range(devices)])


def from_partners(block):
    lines = lax.axis_size("dp") // 2
    blocks = [block, hop(block, lambda d: d ^ 1)]
    for k in range(1, lines):
        far = hop(block, lambda d: (d // 2 + k) % lines * 2 + d % 2)
        blocks += [far, hop(far, lambda d: d ^ 1)]
    return blocks


def swap_features(parts):
    lines = lax.axis_size("dp") // 2
    parts = [part.reshape(-1, part.shape[2]) for part in parts]
    blocks = [parts[0], hop(parts[1], lambda d: d ^ 1)]
    for k in range(1, lines):
        blocks.append(hop(parts[2 * k], lambda d: (d // 2 + k) % lines * 2 + d % 2))
        blocks.append(hop(parts[2 * k + 1], lambda d: (d // 2 + k) % lines * 2 + 1 - d % 2))
    return blocks


def sum_cores(mine, theirs):
    total = mine.astype(F32) + hop(theirs, lambda d: d ^ 1).astype(F32)
    return total[0], total[1:].astype(BF)


def sum_lines(kept, others):
    lines = others.shape[0] + 1
    for k in range(1, lines):
        part = hop(others[k - 1], lambda d: (d // 2 + k) % lines * 2 + d % 2)
        kept = kept + part.astype(F32)
    return jnp.transpose(kept, (1, 0, 2))


def whole_features(parts, depth):
    lines = lax.axis_size("dp") // 2
    me = lax.axis_index("dp")
    rows = jnp.zeros((parts[0].shape[0] * parts[0].shape[1], depth), parts[0].dtype)
    for k, part in enumerate(parts):
        owner = (me // 2 + k // 2) % lines * 2 + (me % 2 + k % 2) % 2
        part = part.reshape(-1, part.shape[2])
        rows = lax.dynamic_update_slice_in_dim(rows, part, owner * part.shape[1], 1)
    return rows


def halves_back(xs, z, wide):
    half = wide // 2
    low = lax.axis_index("wide") < half
    even = [(2 * v, v) if v < half else (2 * (v - half) + 1, v) for v in range(wide)]
    odd = [(2 * v + 1, v) if v < half else (2 * (v - half), v) for v in range(wide)]
    is_even = lax.axis_index("wide") % 2 == 0
    got_a = lax.ppermute(jnp.where(is_even, xs, z), "wide", even)
    got_b = lax.ppermute(jnp.where(is_even, z, xs), "wide", odd)
    return jnp.concatenate([jnp.where(low, got_a, got_b), jnp.where(low, got_b, got_a)], axis=1)


def body(
    x_in,
    lengths,
    modality,
    norm_gain,
    conv_weight,
    conv_bias,
    a_log,
    d_skip,
    in_master,
    xproj_master,
    dtproj_master,
    dt_bias,
    out_master,
    cotangent,
):
    wide, dp = lax.axis_size("wide"), lax.axis_size("dp")
    place = lax.axis_index("wide")
    count = x_in.shape[0]
    span = count * wide
    channels = INNER // wide
    width = conv_weight.shape[0]
    own = lambda table: lax.dynamic_slice_in_dim(table, place * channels, channels, table.ndim - 1)

    pieces = lengths.reshape(-1)
    ends = [pieces[0]]
    for at in range(1, pieces.shape[0]):
        ends.append(ends[-1] + pieces[at])
    bounds = jnp.stack(ends)
    places = jnp.arange(span, dtype=jnp.int32)
    living = places < bounds[-1]
    masks = conv_masks(places, bounds, width)
    alive_here = (place * count + jnp.arange(count, dtype=jnp.int32)) < bounds[-1]

    scale = lax.rsqrt(jnp.mean(x_in * x_in, axis=1, keepdims=True) + EPSILON)
    rank_rows, step_rows = xproj_master.shape[0], dtproj_master.shape[0]
    small = jnp.concatenate([xproj_master, dtproj_master], axis=0)
    small = jnp.pad(small, ((0, -small.shape[0] % 16), (0, 0), (0, 0)))
    tag = jnp.where(alive_here, modality, 3).astype(BF)
    mask_table = jnp.stack(masks, axis=1)
    *normed_parts, w_in, w_out, d_branch_all, tags_all, w_x_kinds, w_dt_kinds, xs, z, inner, d_gated, proj = front(
        jnp.transpose(in_master, (1, 0, 2)),
        jnp.transpose(out_master, (1, 0, 2)),
        jnp.transpose(small, (1, 0, 2)),
        x_in,
        cotangent,
        norm_gain[None, :],
        jnp.broadcast_to(tag[:, None], (count, 128)),
        mask_table,
        conv_weight,
        conv_bias[None, :],
        rank_rows,
        step_rows,
        0,
    )
    w_in = w_in.reshape(-1, in_master.shape[2])
    kinds_all = tags_all[:, :, 0].reshape(span)
    kinds = kinds_all[:, None] == jnp.arange(3, dtype=BF)[None, :]

    kinds_parts = from_partners(kinds_all[:, None])
    features = swap_features(normed_parts)

    rank = w_x_kinds.shape[1]
    tags_flat = tags_all.reshape(span, -1)
    skip_row = d_skip[None, :]
    dtp, gated, y_value, heads = scan_forward(
        proj, w_dt_kinds, dt_bias, tags_flat, inner, mask_table, a_log, skip_row, z
    )
    branch = branch_of(gated, tags_flat, w_out, x_in.shape[1])
    branch = lax.psum_scatter(branch, "wide", scatter_dimension=0, tiled=True)
    result = x_in + branch.astype(F32)
    mine, theirs = gate(d_branch_all.reshape(span, -1), gated, tags_flat, dp)
    mine, theirs, y_value = lax.optimization_barrier((mine, theirs, y_value))
    d_dtp, d_scan, d_z, d_columns, extra = scan_backward(
        dtp, inner, proj, mask_table, a_log, skip_row, z, y_value, d_gated, heads
    )
    sums = sum_cores(mine, theirs)
    d_dtp, features, kinds_parts, sums = lax.optimization_barrier((d_dtp, features, kinds_parts, sums))
    out_grad = sum_lines(*sums)
    d_maps = d_columns.reshape(-1, 2, d_columns.shape[2] // STATE, STATE)
    d_maps = d_maps.transpose(1, 3, 0, 2).reshape(2 * STATE, span)
    if span * x_in.shape[1] * 4 <= 12 << 20 and dp == 4 and w_in.shape[0] % (3 * dp * channels) == 0:
        in_grad, d_normed, tables, small = back(
            w_in.reshape(dp, 3, -1, w_in.shape[1]),
            features,
            normed_parts,
            kinds_parts,
            count,
            (
                d_dtp,
                d_scan,
                d_z,
                xs,
                inner,
                d_maps,
                proj,
                w_x_kinds,
                w_dt_kinds,
                tags_all,
                jnp.broadcast_to(kinds_all.astype(F32)[None], (8, span)),
                mask_table,
                conv_weight,
                conv_bias[None, :],
                extra,
            ),
            rank_rows,
            step_rows,
            2,
        )
        d_normed, tables, small, out_grad = lax.optimization_barrier((d_normed, tables, small, out_grad))
        in_grad = jnp.transpose(in_grad, (1, 0, 2))
    else:
        taps = own(conv_weight)
        across = kinds.T[:, None, :]
        rates_kinds = split_kinds(proj[:DT_RANK].T, kinds, 1)
        d_dtp = jnp.where(living[:, None], d_dtp, jnp.zeros((), BF))
        xs_value = xs.astype(F32)
        extended = jnp.concatenate([jnp.zeros((width - 1, channels), F32), xs_value], axis=0)
        pre = own(conv_bias)[None, :]
        for offset in range(width):
            begin = width - 1 - offset
            pre = (
                pre + taps[begin][None, :] * extended[begin : begin + span] * masks[offset][:, None]
            )

        feature_kinds = [
            split_kinds(rows, tags == jnp.arange(3, dtype=BF)[None, :], 1)
            for rows, tags in zip(features, kinds_parts)
        ]
        by_kind = contract(w_dt_kinds.reshape(3 * DT_RANK, channels), d_dtp, 1, 1)
        d_rates = jnp.sum(jnp.where(across, by_kind.reshape(3, DT_RANK, span), 0.0), axis=0)
        d_proj = sum_wide(jnp.concatenate([d_rates, d_maps], axis=0).astype(BF), 3)
        d_proj = jnp.where(living[None], d_proj, jnp.zeros((), BF)).T
        grad_dt = contract(rates_kinds, d_dtp, 0, 0).reshape(3, dp, step_rows, channels)
        bias_part = jnp.stack(
            [jnp.sum(jnp.where(kinds[:, k : k + 1], d_dtp.astype(F32), 0.0), axis=0) for k in range(3)]
        )
        d_proj_kinds = split_kinds(d_proj, kinds, 1)
        d_inner = contract(d_proj_kinds, w_x_kinds.reshape(3 * rank, channels), 1, 0).astype(BF)
        grad_x = contract(d_proj_kinds, inner, 0, 0)
        grad_x = grad_x.reshape(3, dp, rank_rows, channels)

        d_pre = (d_inner.astype(F32) + d_scan) * silu_slope(pre)
        later = conv_masks(jnp.arange(span + width - 1, dtype=jnp.int32), bounds, width)
        further = jnp.concatenate([d_pre, jnp.zeros((width - 1, channels), F32)], axis=0)
        conv_rows = []
        d_xs = jnp.zeros_like(xs_value)
        for offset in range(width):
            begin = width - 1 - offset
            conv_rows.append(
                jnp.sum(d_pre * masks[offset][:, None] * extended[begin : begin + span], axis=0)
            )
            masked = further * later[offset][:, None]
            d_xs = d_xs + taps[begin][None, :] * masked[offset : offset + span]
        conv_part = jnp.stack(conv_rows[::-1], axis=0)
        conv_bias_part = jnp.sum(d_pre, axis=0)
        d_xs = jnp.where(living[:, None], d_xs, 0.0).astype(BF)
        d_z = jnp.where(living[:, None], d_z, jnp.zeros((), BF))
        d_mixed = halves_back(d_xs, d_z, wide)
        mixed_parts = from_partners(d_mixed)
        grad_in = 0.0
        for pair in range(0, dp, 2):
            left = jnp.concatenate(feature_kinds[pair : pair + 2], axis=0)
            grad_in = grad_in + contract(left, jnp.concatenate(mixed_parts[pair : pair + 2], axis=0), 0, 0)
        in_grad = jnp.transpose(grad_in.reshape(3, -1, d_mixed.shape[1]), (1, 0, 2))

        d_normed = jnp.zeros((span, x_in.shape[1]), F32)
        w_in_kinds = w_in.reshape(dp, 3, -1, w_in.shape[1])
        for kind in range(3):
            picked = jnp.where(kinds[:, kind : kind + 1], d_mixed, jnp.zeros((), BF))
            d_normed = d_normed + contract(
                picked, w_in_kinds[:, kind].reshape(-1, w_in.shape[1]), 1, 1
            )
        d_normed = d_normed.astype(BF)
        normed_all = whole_features(normed_parts, x_in.shape[1])
        gain_part = jnp.sum(d_normed.astype(F32) * normed_all.astype(F32), axis=0)
        table = [conv_part, conv_bias_part[None], extra, bias_part]
        table.append(gain_part.reshape(-1, channels))
        table = jnp.concatenate(table, axis=0)
        table = jnp.pad(table, ((0, -table.shape[0] % 8), (0, 0)))
        small = jnp.concatenate([grad_x, grad_dt], axis=2).transpose(1, 0, 2, 3)
        small = jnp.pad(small, ((0, 0), (0, 0), (0, -small.shape[2] % 16), (0, 0))).astype(BF)
        d_normed, tables, small = finish(d_normed.reshape(wide, count, -1), table, small, 4)
    xproj_grad = jnp.transpose(small[:, :rank_rows], (1, 0, 2))
    dtproj_grad = jnp.transpose(small[:, rank_rows : rank_rows + step_rows], (1, 0, 2))
    d_normed = d_normed.astype(BF).astype(F32)
    scaled_back = d_normed * norm_gain[None, :]
    x_grad = cotangent + scale * (
        scaled_back - x_in * scale * scale * jnp.mean(scaled_back * x_in, axis=1, keepdims=True)
    )

    edge = width + 1 + STATE + 1
    shared = tables[:, :edge].transpose(1, 0, 2).reshape(edge, INNER)
    bias_grad = lax.dynamic_index_in_dim(tables, place, 0, False)[edge : edge + 3]
    kept = edge + 3 + x_in.shape[1] // channels
    gain_grad = jnp.sum(tables[:, edge + 3 : kept], axis=0).reshape(-1) / norm_gain
    return (
        result,
        x_grad,
        gain_grad,
        shared[:width],
        shared[width],
        shared[width + 1 : width + 1 + STATE],
        shared[width + 1 + STATE],
        in_grad,
        xproj_grad,
        dtproj_grad,
        bias_grad,
        out_grad,
    )


def solution(mesh):
    in_specs = (
        P(("dp", "wide"), None),
        P("dp", None),
        P(("dp", "wide")),
        P(),
        P(),
        P(),
        P(),
        P(),
        P("dp", None, "wide"),
        P("dp", None, "wide"),
        P("dp", None, "wide"),
        P(None, "wide"),
        P("dp", None, "wide"),
        P(("dp", "wide"), None),
    )
    out_specs = (
        P(("dp", "wide"), None),
        P(("dp", "wide"), None),
        P(),
        P(),
        P(),
        P(),
        P(),
        P("dp", None, "wide"),
        P("dp", None, "wide"),
        P("dp", None, "wide"),
        P(None, "wide"),
        P("dp", None, "wide"),
    )
    return jax.shard_map(body, mesh=mesh, in_specs=in_specs, out_specs=out_specs, check_vma=False)
```
